128 devices in a mesh: dp: 64 (over z, x, y), fsdp: 2 (over core).
Axes of the slice: x: 4, y: 4, z: 4, core: 2. Of those that a mesh axis runs over, the one named last changes fastest.
Arguments:
- hidden: bfloat16 [128, 256, 768], P('dp', 'fsdp'), may hold values from -6 to 6
- cotangent: bfloat16 [128, 256, 768], P('dp', 'fsdp'), may hold values from -16 to 16
- remaining: int32 [128], P('dp'), may hold values from 1 to 256, 16384 in all
- order: int32 [128, 256], P('dp'), may hold values from 0 to 255, each once within a row
- norm1_gain: bfloat16 [2, 768], P(None, ('dp', 'fsdp')), may hold values from 0.5 to 1.5
- norm1_bias: bfloat16 [2, 768], P(None, ('dp', 'fsdp')), may hold values from -1 to 1
- w_qkv: bfloat16 [2, 768, 2304], P(None, ('dp', 'fsdp')), may hold values from -0.21875 to 0.21875
- bias_qv: bfloat16 [2, 1536], P(None, ('dp', 'fsdp')), may hold values from -1.5 to 1.5
- w_out: bfloat16 [2, 768, 768], P(None, ('dp', 'fsdp')), may hold values from -1.75 to 1.75
- bias_out: bfloat16 [2, 768], P(None, ('dp', 'fsdp')), may hold values from -1.5 to 1.5
- norm2_gain: bfloat16 [2, 768], P(None, ('dp', 'fsdp')), may hold values from 0.5 to 1.5
- norm2_bias: bfloat16 [2, 768], P(None, ('dp', 'fsdp')), may hold values from -1 to 1
- w_up: bfloat16 [2, 768, 3072], P(None, ('dp', 'fsdp')), may hold values from -0.21875 to 0.21875
- bias_up: bfloat16 [2, 3072], P(None, ('dp', 'fsdp')), may hold values from -1.5 to 1.5
- w_down: bfloat16 [2, 3072, 768], P(None, ('dp', 'fsdp')), may hold values from -0.21875 to 0.21875
- bias_down: bfloat16 [2, 768], P(None, ('dp', 'fsdp')), may hold values from -1.5 to 1.5
Outputs:
- output: bfloat16 [128, 256, 768], P('dp', 'fsdp')
- grad_hidden: float32 [128, 256, 768], P('dp', 'fsdp')
- grad_norm1_gain: float32 [2, 768], P(None, ('dp', 'fsdp'))
- grad_norm1_bias: float32 [2, 768], P(None, ('dp', 'fsdp'))
- grad_w_qkv: float32 [2, 768, 2304], P(None, ('dp', 'fsdp'))
- grad_bias_qv: float32 [2, 1536], P(None, ('dp', 'fsdp'))
- grad_w_out: float32 [2, 768, 768], P(None, ('dp', 'fsdp'))
- grad_bias_out: float32 [2, 768], P(None, ('dp', 'fsdp'))
- grad_norm2_gain: float32 [2, 768], P(None, ('dp', 'fsdp'))
- grad_norm2_bias: float32 [2, 768], P(None, ('dp', 'fsdp'))
- grad_w_up: float32 [2, 768, 3072], P(None, ('dp', 'fsdp'))
- grad_bias_up: float32 [2, 3072], P(None, ('dp', 'fsdp'))
- grad_w_down: float32 [2, 3072, 768], P(None, ('dp', 'fsdp'))
- grad_bias_down: float32 [2, 768], P(None, ('dp', 'fsdp'))
The draws below stay inside these ranges and needn't reach their ends.
Inputs may be any that keep to these rules, and one draw needn't show every extreme that they name: `remaining`: the counts sum to 16384 and one of them is 256. `order`: each row is a permutation of the positions 0 .. 255.
All inputs are finite; a program needn't handle non-finite values. No bound on the sum of `remaining` on one device may be relied on, other than what follows from the above.
Results may differ from the reference program's by a relative error of at most 0.014.
Values may be sent and summed in bfloat16 or wider, within the bound.
A program may use at most 256 MiB of HBM per device.

```python
import math
import jax
import jax.numpy as jnp
import numpy as np
from jax import lax

D = 768
FF = 3072
HEADS = 12
HEAD = 64
LAYERS = 2
LENGTH = 256
SEQUENCES = 128


def raised(values, own_key, source, target, shards_of, factor):
    def block_of(position):
        return (jnp.arange(values.shape[position]) // (values.shape[position] // shards_of)).reshape((-1,) + (1,) * (values.ndim - 1 - position))

    first = jax.random.permutation(own_key, shards_of)[block_of(target)]
    second = (block_of(target) + shards_of // 2) % shards_of
    return jnp.where((block_of(source) == first) | (block_of(source) == second), factor * values, values)


def levels(stream_key, dims, cuts, least, high):
    level = 1.0
    for position, shards_of in cuts:
        steps = jax.random.uniform(jax.random.fold_in(jax.random.fold_in(stream_key, 6), position), (shards_of,), jnp.float32, least / len(cuts), high / len(cuts))
        level = level * jnp.repeat(jnp.exp(steps), dims[position] // shards_of).reshape((-1,) + (1,) * (len(dims) - 1 - position))
    return level


def profile(count, total, most, skew):
    weights = [(1 << 20) // math.isqrt(grade ** skew) + 1 for grade in range(2, count + 1)]
    spare, counts = total - most - (count - 1), [1] * (count - 1)
    while spare > 0:
        free = [i for i in range(count - 1) if counts[i] < most]
        pool, left = sum([weights[i] for i in free]), spare
        for i in free:
            addition = min(most - counts[i], max(1, left * weights[i] // pool), spare)
            counts[i] = counts[i] + addition
            spare = spare - addition
    return np.array([most] + counts)


def uneven_parts(own_key, count, total, reach, slope):
    if count == 2:
        one = jax.random.randint(own_key, (), max(1, total - reach), min(reach, total - 1) + 1)
        return jnp.stack([one, total - one])
    lengths = jnp.asarray(profile(count, total, reach, slope), jnp.int32)
    twos = (count - 1) // 2
    giver, receiver = lengths[1:1 + 2 * twos:2], lengths[2:2 + 2 * twos:2]
    room = jnp.minimum(giver - 1, reach - receiver)
    moved = jax.random.randint(jax.random.fold_in(own_key, 1), (twos,), 0, 1 << 20) % (room + 1)
    lengths = lengths.at[1:1 + 2 * twos:2].set(giver - moved).at[2:2 + 2 * twos:2].set(receiver + moved)
    return lengths[jax.random.permutation(jax.random.fold_in(own_key, 2), count)]


def normal_values(stream_key, extent, scale, bound, cuts=(), kind=jnp.bfloat16):
    level = levels(stream_key, extent, cuts, -0.22, 0.18) if cuts else 1.0
    entries = jax.random.normal(stream_key, extent, jnp.float32) * scale * level
    return jnp.minimum(jnp.maximum(entries, -bound), bound).astype(kind)


def bell_draw_with(own_key, shape, scale, reach, shards, heavy, kind=jnp.bfloat16):
    drawn = scale * jax.random.normal(own_key, shape, jnp.float32)
    if shards:
        drawn = drawn * levels(own_key, shape, shards, -0.22, 0.18)
    return jnp.clip(raised(drawn, jax.random.fold_in(own_key, 3), *heavy), -reach, reach).astype(kind)


def setup_inputs(seed: int = 0) -> dict:
    streams_of = jax.random.split(jax.random.key(seed), 17)
    hidden = normal_values(streams_of[0], (SEQUENCES, LENGTH, D), 1.0, 6.0, ((0, 64), (1, 2)))
    cotangent = bell_draw_with(streams_of[1], (SEQUENCES, LENGTH, D), 1.0, 16.0, ((0, 64), (1, 2)), (0, 2, 64, 4.0))
    remaining = uneven_parts(streams_of[2], SEQUENCES, SEQUENCES * LENGTH // 2, LENGTH, 2).astype(jnp.int32)
    order = jax.vmap(lambda own: jax.random.permutation(own, LENGTH))(jax.random.split(streams_of[3], SEQUENCES)).reshape((SEQUENCES, LENGTH)).astype(jnp.int32)
    norm1_gain = jnp.clip(1.0 + 0.1 * jax.random.normal(streams_of[4], (LAYERS, D), jnp.float32), 0.5, 1.5).astype(jnp.bfloat16)
    norm1_bias = normal_values(streams_of[5], (LAYERS, D), 0.2, 1.0, ((1, 128),))
    w_qkv = normal_values(streams_of[6], (LAYERS, D, 3 * D), D ** -0.5, 0.21875, ((1, 128),))
    bias_qv = normal_values(streams_of[7], (LAYERS, 2 * D), 0.3, 1.5, ((1, 128),))
    w_out = normal_values(streams_of[8], (LAYERS, D, D), (D // 64) ** -0.5, 1.75, ((1, 128),))
    bias_out = normal_values(streams_of[9], (LAYERS, D), 0.3, 1.5, ((1, 128),))
    norm2_gain = jnp.clip(1.0 + 0.1 * jax.random.normal(streams_of[10], (LAYERS, D), jnp.float32), 0.5, 1.5).astype(jnp.bfloat16)
    norm2_bias = normal_values(streams_of[11], (LAYERS, D), 0.2, 1.0, ((1, 128),))
    w_up = normal_values(streams_of[12], (LAYERS, D, FF), D ** -0.5, 0.21875, ((1, 128),))
    bias_up = normal_values(streams_of[13], (LAYERS, FF), 0.3, 1.5, ((1, 128),))
    w_down = normal_values(streams_of[14], (LAYERS, FF, D), (FF // 4) ** -0.5, 0.21875, ((1, 128),))
    bias_down = normal_values(streams_of[15], (LAYERS, D), 0.3, 1.5, ((1, 128),))
    return {"hidden": hidden, "cotangent": cotangent, "remaining": remaining, "order": order, "norm1_gain": norm1_gain, "norm1_bias": norm1_bias, "w_qkv": w_qkv, "bias_qv": bias_qv, "w_out": w_out, "bias_out": bias_out, "norm2_gain": norm2_gain, "norm2_bias": norm2_bias, "w_up": w_up, "bias_up": bias_up, "w_down": w_down, "bias_down": bias_down}


@jax.custom_vjp
def low(v):
    return lax.optimization_barrier(v.astype(jnp.bfloat16)).astype(jnp.float32)

@jax.custom_vjp
def low_back(v):
    return v

def low_keep(v):
    return (low(v), None)

def low_pass(kept, grad):
    return (grad,)

def back_keep(v):
    return (v, None)

def back_low(kept, grad):
    return (low(grad),)
low.defvjp(low_keep, low_pass)
low_back.defvjp(back_keep, back_low)

def matmul(left, right):
    return jnp.dot(left, right, precision=lax.Precision.HIGHEST, preferred_element_type=jnp.float32)

def norm_apply(stream, gain, offset):
    center = stream - lax.optimization_barrier(jnp.mean(stream, axis=-1, keepdims=True))
    spread = lax.optimization_barrier(jnp.mean(center * center, axis=-1, keepdims=True))
    return center * lax.rsqrt(spread + 1e-05) * gain + offset

def layer_apply(stream, params):
    gain_one, offset_one, w_qkv, bias_qv, w_out, bias_out, gain_two, offset_two, w_up, bias_up, w_down, bias_down = params
    normed = low(norm_apply(stream, gain_one, offset_one))
    qkv_bias = jnp.concatenate([bias_qv[:D], jnp.zeros((D,), jnp.float32), bias_qv[D:]])
    qkv = low(low_back(matmul(normed, w_qkv) + qkv_bias))
    qkv = qkv.reshape(-1, LENGTH, 3, HEADS, HEAD)
    query, keys, values = (qkv[:, :, 0], qkv[:, :, 1], qkv[:, :, 2])
    scores = low_back(jnp.einsum('sqhe,skhe->shqk', query, keys, precision=lax.Precision.HIGHEST) * 0.125)
    probs = jax.nn.softmax(scores, axis=-1)
    attended = jnp.einsum('shqk,skhe->sqhe', low(probs), values, precision=lax.Precision.HIGHEST)
    attended = low(low_back(attended)).reshape(-1, D)
    middle = stream + low_back(matmul(attended, w_out) + bias_out)
    normed_two = low(norm_apply(middle, gain_two, offset_two))
    hidden_pre = low_back(matmul(normed_two, w_up) + bias_up)
    active = low(jax.nn.gelu(hidden_pre, approximate=True))
    return middle + low_back(matmul(active, w_down) + bias_down)

def model(params, stream):
    for layer_index in range(LAYERS):
        stream = layer_apply(stream, tuple((weight[layer_index] for weight in params)))
    return stream

def reference(hidden, cotangent, remaining, order, norm1_gain, norm1_bias, w_qkv, bias_qv, w_out, bias_out, norm2_gain, norm2_bias, w_up, bias_up, w_down, bias_down):
    params = tuple((weight.astype(jnp.float32) for weight in (norm1_gain, norm1_bias, w_qkv, bias_qv, w_out, bias_out, norm2_gain, norm2_bias, w_up, bias_up, w_down, bias_down)))
    positions = jnp.arange(LENGTH, dtype=jnp.int32)
    live = positions[None, :] >= (LENGTH - remaining)[:, None]
    matched = (order[:, :, None] == positions[None, None, :]) & live[:, :, None]
    mask = jnp.any(matched, axis=1).astype(jnp.float32)
    upstream = cotangent.astype(jnp.float32) * mask[:, :, None]
    group = math.gcd(SEQUENCES, 16)
    blocks = SEQUENCES // group
    streams = hidden.astype(jnp.float32).reshape(blocks, group * LENGTH, D)
    backs = upstream.reshape(blocks, group * LENGTH, D)
    zeros = jax.tree.map(jnp.zeros_like, params)

    def block_step(totals, inputs):
        stream, back_grad = inputs
        result, pull = jax.vjp(model, params, stream)
        grad_params, grad_stream = pull(back_grad)
        return (jax.tree.map(jnp.add, totals, grad_params), (result, grad_stream))
    totals, (results, grad_streams) = lax.scan(block_step, zeros, (streams, backs))
    output = results.reshape(SEQUENCES, LENGTH, D).astype(jnp.bfloat16)
    grad_hidden = grad_streams.reshape(SEQUENCES, LENGTH, D)
    return (output, grad_hidden, totals[0], totals[1], totals[2], totals[3], totals[4], totals[5], totals[6], totals[7], totals[8], totals[9], totals[10], totals[11])
```

```python
import functools

import jax
import jax.numpy as jnp
from jax import lax
from jax.experimental import pallas as pl
from jax.experimental.pallas import tpu as pltpu
from jax.sharding import PartitionSpec as P

HEAD = 64
HEADS = 12
LAYERS = 2
D = 768
FF = 3072
VECTOR_WIDTHS = (6, 6, 12, 6, 6, 6, 24, 6)
VECTOR_ROWS = 2 * 72
MESH = pl.DeviceIdType.MESH
BF16, F32 = jnp.bfloat16, jnp.float32


def place():
    dp, core = lax.axis_index("dp"), lax.axis_index("fsdp")
    return {"z": dp // 16, "x": (dp // 4) % 4, "y": dp % 4, "c": core}


def device(at):
    return ((at["z"] * 4 + at["x"]) * 4 + at["y"], at["c"])


def moved(at, axis, step):
    size = 2 if axis == "c" else 4
    return {**at, axis: (at[axis] + step) % size}


class Links:
    def __init__(self, send_sems, recv_sems):
        self.send_sems, self.recv_sems, self.used, self.open = send_sems, recv_sems, 0, []

    def send(self, src, dst, target):
        copy = pltpu.make_async_remote_copy(
            src_ref=src,
            dst_ref=dst,
            send_sem=self.send_sems.at[self.used],
            recv_sem=self.recv_sems.at[self.used],
            device_id=device(target),
            device_id_type=MESH,
        )
        self.used += 1
        copy.start()
        self.open.append(copy)
        return copy

    def drain(self):
        for copy in self.open:
            copy.wait_send()
        self.open = []


def greet(me):
    partners = [moved(moved(me, "y", dy), "c", dc) for dy in range(4) for dc in range(2)][1:]
    partners += [moved(me, axis, step) for axis in "xz" for step in (1, 2, 3)]
    barrier = pltpu.get_barrier_semaphore()
    for partner in partners:
        pl.semaphore_signal(barrier, inc=1, device_id=device(partner), device_id_type=MESH)
    pl.semaphore_wait(barrier, len(partners))


def block_of(wide, deep, stream, layer, at):
    kind, part, _ = stream
    if kind == "wide":
        return wide.at[layer, at["y"], at["c"], at["z"], at["x"], :, part]
    return deep.at[layer, at["c"], at["z"], at["x"], at["y"], part, :]


ALL = slice(None)
STREAMS = (
    ("wide", slice(0, 384), "xyz"),
    ("wide", slice(384, 768), "xzy"),
    ("deep", slice(0, 16), "xyz"),
    ("deep", slice(16, 32), "xzy"),
    ("deep", slice(32, 48), "yzx"),
)


def gather_kernel(
    hidden, cot, w_qkv, w_out, w_up, w_down, vecs,
    seq_out, cot_out, wide, deep, vec_out,
    send_a, recv_a, send_d, recv_d, asm, piece_c, piece_d, vec_state, vec_recv,
    send_sems, recv_sems, local_sems,
):
    me = place()
    links = Links(send_sems, recv_sems)
    sibling = moved(me, "c", 1)
    mine = 2 * me["y"] + me["c"]
    for layer in range(LAYERS):
        rows = slice(8 * layer, 8 * layer + 6)
        for slab in range(8):
            if slab < 3:
                part = w_qkv[layer, :, slab * D : (slab + 1) * D]
            elif slab == 3:
                part = w_out[layer]
            else:
                part = w_up[layer, :, (slab - 4) * D : (slab - 3) * D]
            asm[slab, rows, :] = part.astype(F32)
    for slab in range(8):
        send_a[slab] = asm[slab, 0:16, :].astype(BF16)
    for half in range(2):
        for layer in range(LAYERS):
            asm[half, 16 + 24 * layer : 40 + 24 * layer, 0:384] = w_down[
                layer, :, half * 384 : (half + 1) * 384
            ].astype(F32)
        send_d[half] = asm[half, 16:64, 0:384].astype(BF16)

    greet(me)

    arrivals = []
    for dy in range(4):
        for dc in range(2):
            if dy == 0 and dc == 0:
                continue
            target = moved(moved(me, "y", dy), "c", dc)
            arrivals.append(
                links.send(send_a.at[2 * target["y"] + target["c"]], recv_a.at[mine], target)
            )
    arrivals.append(links.send(send_d.at[1 - me["c"]], recv_d.at[me["c"]], sibling))
    recv_a[mine] = send_a[mine]
    recv_d[me["c"]] = send_d[me["c"]]
    vec_state[0] = vecs[...]
    seq_links, locals_ = [], []
    for index, (src, dst) in enumerate(((hidden, seq_out), (cot, cot_out))):
        seq_links.append(links.send(src.at[1 - me["c"]], dst.at[me["c"]], sibling))
        copy = pltpu.make_async_copy(src.at[me["c"]], dst.at[me["c"]], local_sems.at[index])
        copy.start()
        locals_.append(copy)

    def vec_phase(number):
        axis = "xyzc"[number]
        return [
            links.send(vec_state.at[number], vec_recv.at[3 * number + step - 1], moved(me, axis, step))
            for step in range(1, 2 if axis == "c" else 4)
        ]

    def vec_sum(number, copies):
        total = vec_state[number].astype(F32)
        for copy in copies:
            copy.wait_recv()
        for step in range(len(copies)):
            total += vec_recv[3 * number + step].astype(F32)
        if number < 3:
            vec_state[number + 1] = total.astype(BF16)
        else:
            vec_out[...] = total.astype(BF16)

    vec_copies = vec_phase(0)
    for copy in arrivals:
        copy.wait_recv()
    own = []
    for layer in range(LAYERS):
        for source in range(8):
            asm[layer, 6 * source : 6 * source + 6, :] = recv_a[source].astype(F32)[
                8 * layer : 8 * layer + 6
            ]
        piece_c[layer] = asm[layer, 0:48, :].astype(BF16)
        for half in range(2):
            asm[2 + layer, 24 * half : 24 * half + 24, 0:384] = recv_d[half].astype(F32)[
                24 * layer : 24 * layer + 24
            ]
        piece_d[layer] = asm[2 + layer, 0:48, 0:384].astype(BF16)
        own.append(
            pltpu.make_async_copy(
                piece_c.at[layer],
                wide.at[layer, me["y"], me["c"], me["z"], me["x"]],
                local_sems.at[2 + 2 * layer],
            )
        )
        own.append(
            pltpu.make_async_copy(
                piece_d.at[layer],
                deep.at[layer, me["c"], me["z"], me["x"], me["y"]],
                local_sems.at[3 + 2 * layer],
            )
        )
        own[-2].start()
        own[-1].start()

    flows = [
        {"stream": stream, "layer": layer, "at": dict(me)}
        for layer in range(LAYERS)
        for stream in STREAMS
    ]

    def block(flow, at):
        return block_of(wide, deep, flow["stream"], flow["layer"], at)

    def begin(flow, phase):
        axis = flow["stream"][2][phase]
        src = block(flow, flow["at"])
        steps = (1, 3) if phase == 2 else (1, 3, 2)
        flow["copies"] = {step: links.send(src, src, moved(me, axis, step)) for step in steps}

    to_sibling = []

    def hand_over(flow, at):
        part = block(flow, at)
        to_sibling.append(links.send(part, part, sibling))

    def end(flow, phase):
        axis = flow["stream"][2][phase]
        if phase < 2:
            for step in (1, 3, 2):
                flow["copies"][step].wait_recv()
                if phase > 0:
                    hand_over(flow, moved(flow["at"], axis, -step))
            flow["at"] = {**flow["at"], axis: ALL}
            if phase == 0:
                hand_over(flow, flow["at"])
        else:
            split = flow["stream"][2][0]
            flow["halves"] = []
            for step, start in ((1, 0), (3, 2)):
                flow["copies"][step].wait_recv()
                came = moved(flow["at"], axis, -step)
                part = block(flow, {**came, split: pl.ds(start, 2)})
                flow["halves"].append(links.send(part, part, moved(me, axis, step)))
                hand_over(flow, came)

    def finish(flow):
        axis, split = flow["stream"][2][2], flow["stream"][2][0]
        for copy in flow["halves"]:
            copy.wait_recv()
        hand_over(flow, moved(flow["at"], axis, 2))

    for copy in own:
        copy.wait()
    for flow in flows:
        begin(flow, 0)
    vec_sum(0, vec_copies)
    vec_copies = vec_phase(1)
    for flow in flows:
        end(flow, 0)
        begin(flow, 1)
    vec_sum(1, vec_copies)
    vec_copies = vec_phase(2)
    for flow in flows:
        end(flow, 1)
        begin(flow, 2)
    vec_sum(2, vec_copies)
    vec_copies = vec_phase(3)
    for flow in flows:
        end(flow, 2)
    vec_sum(3, vec_copies)
    for flow in flows:
        finish(flow)
    for copy in to_sibling:
        copy.wait_recv()
    for copy in seq_links:
        copy.wait_recv()
    for copy in locals_:
        copy.wait()
    links.drain()


def gather(hidden, cot, w_qkv, w_out, w_up, w_down, vecs):
    vmem, hbm = pl.BlockSpec(memory_space=pltpu.VMEM), pl.BlockSpec(memory_space=pl.ANY)
    half = hidden.shape[1]
    return pl.pallas_call(
        gather_kernel,
        out_shape=(
            jax.ShapeDtypeStruct((2, half, D), BF16),
            jax.ShapeDtypeStruct((2, half, D), BF16),
            jax.ShapeDtypeStruct((LAYERS, 4, 2, 4, 4, 48, D), BF16),
            jax.ShapeDtypeStruct((LAYERS, 2, 4, 4, 4, 48, 384), BF16),
            jax.ShapeDtypeStruct((VECTOR_ROWS, 128), BF16),
        ),
        in_specs=[hbm, hbm, vmem, vmem, vmem, vmem, vmem],
        out_specs=(hbm, hbm, hbm, hbm, vmem),
        scratch_shapes=[
            pltpu.VMEM((8, 16, D), BF16),
            pltpu.VMEM((8, 16, D), BF16),
            pltpu.VMEM((2, 48, 384), BF16),
            pltpu.VMEM((2, 48, 384), BF16),
            pltpu.VMEM((8, 64, D), F32),
            pltpu.VMEM((LAYERS, 48, D), BF16),
            pltpu.VMEM((LAYERS, 48, 384), BF16),
            pltpu.VMEM((4, VECTOR_ROWS, 128), BF16),
            pltpu.VMEM((10, VECTOR_ROWS, 128), BF16),
            pltpu.SemaphoreType.DMA((240,)),
            pltpu.SemaphoreType.DMA((240,)),
            pltpu.SemaphoreType.DMA((8,)),
        ],
        compiler_params=pltpu.CompilerParams(
            collective_id=0, has_side_effects=True, vmem_limit_bytes=32 << 20
        ),
        name="gather",
    )(hidden, cot, w_qkv, w_out, w_up, w_down, vecs)


def spread(vectors, index):
    slot = (jnp.arange(128, dtype=jnp.int32) == index)[None, :, None]
    parts = [
        jnp.where(slot, vector[:, None, :], jnp.zeros((), BF16)).reshape(LAYERS, -1)
        for vector in vectors
    ]
    return jnp.concatenate(parts, axis=1).reshape(VECTOR_ROWS, 128)


WIDE_AXES, DEEP_AXES = "yzx", "zxy"
SUMS = (
    ("wide", slice(0, 48), slice(0, 384), "zyx"),
    ("wide", slice(0, 48), slice(384, 768), "yzx"),
    ("deep", slice(0, 16), slice(0, 384), "zyx"),
    ("deep", slice(16, 32), slice(0, 384), "yzx"),
    ("deep", slice(32, 48), slice(0, 384), "xzy"),
)


def extent(part):
    return part.stop - part.start


def scatter_kernel(layers, *refs):
    (wide_in, deep_in, vec_in, half_out, half_grad), refs = refs[:5], refs[5:]
    (g_qkv, g_out, g_up, g_down, vec_out, out, grad), refs = refs[:7], refs[7:]
    (own_wide, own_deep, got_wide, got_deep, vec_state, vec_recv), refs = refs[:6], refs[6:]
    first, second, third = refs[0:5], refs[5:10], refs[10:15]
    sum_wide, sum_deep, send_a, recv_a, send_d, recv_d, send_sems, recv_sems, local_sems = refs[15:]
    me = place()
    links = Links(send_sems, recv_sems)
    sibling = moved(me, "c", 1)
    mine = 2 * me["y"] + me["c"]

    def cut(wide, deep, flow, at):
        kind, rows, cols, _ = SUMS[flow["sum"]]
        axes = WIDE_AXES if kind == "wide" else DEEP_AXES
        index = tuple(at.get(axis, ALL) for axis in axes)
        return (wide if kind == "wide" else deep).at[(flow["layer"], *index, rows, cols)]

    def cut_in(flow, core, at):
        kind, rows, cols, _ = SUMS[flow["sum"]]
        if kind == "wide":
            index = (at.get("y", ALL), core, at.get("z", ALL), at.get("x", ALL))
            return wide_in.at[(flow["layer"], *index, rows, cols)]
        index = (core, at.get("z", ALL), at.get("x", ALL), at.get("y", ALL))
        return deep_in.at[(flow["layer"], *index, rows, cols)]

    greet(me)

    moves = []
    for index, (src, dst) in enumerate(((half_out, out), (half_grad, grad))):
        moves.append(links.send(src.at[1 - me["c"]], dst.at[me["c"]], sibling))
        copy = pltpu.make_async_copy(src.at[me["c"]], dst.at[me["c"]], local_sems.at[index])
        copy.start()
        moves.append(copy)
    used = 2

    vec_state[0] = vec_in[...]

    def vec_phase(number):
        axis = "xyzc"[number]
        return [
            links.send(vec_state.at[number], vec_recv.at[3 * number + step - 1], moved(me, axis, step))
            for step in range(1, 2 if axis == "c" else 4)
        ]

    def vec_sum(number, copies):
        total = vec_state[number]
        for copy in copies:
            copy.wait_recv()
        for step in range(len(copies)):
            total += vec_recv[3 * number + step]
        if number < 3:
            vec_state[number + 1] = total
        else:
            vec_out[...] = total

    vec_copies = vec_phase(0)
    flows = [{"sum": index, "layer": layer} for layer in layers for index in range(len(SUMS))]
    order = (1, 3, 2, 0)
    for step in order:
        for flow in flows:
            axis = SUMS[flow["sum"]][3][0]
            at = {axis: moved(me, axis, step)[axis]}
            core = me["c"]
            remote = links.send(
                cut_in(flow, 1 - core, at), cut(got_wide, got_deep, flow, at), sibling
            )
            copy = pltpu.make_async_copy(
                cut_in(flow, core, at), cut(own_wide, own_deep, flow, at), local_sems.at[used]
            )
            used += 1
            copy.start()
            flow.setdefault("pair", {})[step] = (remote, copy)
            flow.setdefault("at", {})[step] = at

    def rest(flow, at):
        kind = SUMS[flow["sum"]][0]
        return [axis for axis in (WIDE_AXES if kind == "wide" else DEEP_AXES) if axis not in at]

    def each(flow, at, body):
        axes = rest(flow, at)
        if len(axes) == 2:

            @pl.loop(0, 16)
            def _(index):
                body({**at, axes[0]: index // 4, axes[1]: index % 4}, (index // 4, index % 4))

        else:

            @pl.loop(0, 4)
            def _(index):
                body({**at, axes[0]: index}, (index,))

    for step in order:
        for flow in flows:
            at = flow["at"][step]
            for copy in flow["pair"][step]:
                copy.wait_recv() if copy is flow["pair"][step][0] else copy.wait()

            def add(spot, index):
                target = cut(own_wide, own_deep, flow, spot)
                target[...] += cut(got_wide, got_deep, flow, spot)[...]

            each(flow, at, add)
            if step:
                axis = SUMS[flow["sum"]][3][0]
                flow.setdefault("first", []).append(
                    links.send(
                        cut(own_wide, own_deep, flow, at),
                        first[flow["sum"]].at[flow["layer"], step - 1],
                        moved(me, axis, step),
                    )
                )

    vec_sum(0, vec_copies)
    vec_copies = vec_phase(1)

    def total_of(target, slots):
        total = target[...].astype(F32)
        for slot in slots:
            total += slot[...].astype(F32)
        return total

    for number, slots in ((0, first), (1, second)):
        for flow in flows:
            axes = SUMS[flow["sum"]][3]
            for copy in flow[("first", "second")[number]]:
                copy.wait_recv()
            at = {axis: me[axis] for axis in axes[: number + 1]}
            slot = slots[flow["sum"]]

            def add(spot, index):
                target = cut(own_wide, own_deep, flow, spot)
                target[...] = total_of(
                    target, [slot.at[(flow["layer"], s, *index)] for s in range(3)]
                ).astype(BF16)

            each(flow, at, add)
            axis = axes[number + 1]
            after = (second, third)[number][flow["sum"]]
            flow[("second", "third")[number]] = [
                links.send(
                    cut(own_wide, own_deep, flow, {**at, axis: moved(me, axis, step)[axis]}),
                    after.at[flow["layer"], step - 1],
                    moved(me, axis, step),
                )
                for step in (1, 3, 2)
            ]
        vec_sum(number + 1, vec_copies)
        vec_copies = vec_phase(number + 2)
    for flow in flows:
        kind, rows, cols, axes = SUMS[flow["sum"]]
        for copy in flow["third"]:
            copy.wait_recv()
        target = cut(own_wide, own_deep, flow, {axis: me[axis] for axis in axes})
        slot = third[flow["sum"]]
        total = total_of(target, [slot.at[flow["layer"], s] for s in range(3)])
        (sum_wide if kind == "wide" else sum_deep)[flow["layer"], rows, cols] = total
    vec_sum(3, vec_copies)

    for layer in layers:
        for owner in range(8):
            send_a[owner, 8 * layer : 8 * layer + 6, :] = sum_wide[
                layer, 6 * owner : 6 * owner + 6, :
            ]
        for owner in range(2):
            send_d[owner, 24 * layer : 24 * layer + 24, :] = sum_deep[
                layer, 24 * owner : 24 * owner + 24, :
            ]
    last = []
    for dy in range(4):
        for dc in range(2):
            if dy == 0 and dc == 0:
                continue
            target = moved(moved(me, "y", dy), "c", dc)
            last.append(
                links.send(send_a.at[2 * target["y"] + target["c"]], recv_a.at[mine], target)
            )
    last.append(links.send(send_d.at[1 - me["c"]], recv_d.at[me["c"]], sibling))
    recv_a[mine] = send_a[mine]
    recv_d[me["c"]] = send_d[me["c"]]
    for copy in last:
        copy.wait_recv()
    for layer in layers:
        rows = slice(8 * layer, 8 * layer + 6)
        for slab in range(8):
            value = recv_a[slab, rows, :]
            if slab < 3:
                g_qkv[layer, :, slab * D : (slab + 1) * D] = value
            elif slab == 3:
                g_out[layer] = value
            else:
                g_up[layer, :, (slab - 4) * D : (slab - 3) * D] = value
        for half in range(2):
            g_down[layer, :, half * 384 : (half + 1) * 384] = recv_d[
                half, 24 * layer : 24 * layer + 24, :
            ]
    moves[0].wait_recv()
    moves[1].wait()
    moves[2].wait_recv()
    moves[3].wait()
    links.drain()


def scatter(wide, deep, vecs, half_out, half_grad):
    vmem, hbm = pl.BlockSpec(memory_space=pltpu.VMEM), pl.BlockSpec(memory_space=pl.ANY)
    half = half_out.shape[1]
    sizes = [(extent(rows), extent(cols)) for _, rows, cols, _ in SUMS]
    return pl.pallas_call(
        functools.partial(scatter_kernel, (1, 0)),
        out_shape=(
            jax.ShapeDtypeStruct((LAYERS, 6, 3 * D), F32),
            jax.ShapeDtypeStruct((LAYERS, 6, D), F32),
            jax.ShapeDtypeStruct((LAYERS, 6, FF), F32),
            jax.ShapeDtypeStruct((LAYERS, 24, D), F32),
            jax.ShapeDtypeStruct((VECTOR_ROWS, 128), F32),
            jax.ShapeDtypeStruct((2, half, D), BF16),
            jax.ShapeDtypeStruct((2, half, D), F32),
        ),
        in_specs=[hbm, hbm, vmem, hbm, hbm],
        out_specs=(vmem, vmem, vmem, vmem, vmem, hbm, hbm),
        scratch_shapes=[
            pltpu.VMEM((LAYERS, 4, 4, 4, 48, D), BF16),
            pltpu.VMEM((LAYERS, 4, 4, 4, 48, 384), BF16),
            pltpu.VMEM((LAYERS, 4, 4, 4, 48, D), BF16),
            pltpu.VMEM((LAYERS, 4, 4, 4, 48, 384), BF16),
            pltpu.VMEM((4, VECTOR_ROWS, 128), F32),
            pltpu.VMEM((10, VECTOR_ROWS, 128), F32),
            *[pltpu.VMEM((LAYERS, 3, 4, 4, *size), BF16) for size in sizes],
            *[pltpu.VMEM((LAYERS, 3, 4, *size), BF16) for size in sizes],
            *[pltpu.VMEM((LAYERS, 3, *size), BF16) for size in sizes],
            pltpu.VMEM((LAYERS, 48, D), F32),
            pltpu.VMEM((LAYERS, 48, 384), F32),
            pltpu.VMEM((8, 16, D), F32),
            pltpu.VMEM((8, 16, D), F32),
            pltpu.VMEM((2, 48, 384), F32),
            pltpu.VMEM((2, 48, 384), F32),
            pltpu.SemaphoreType.DMA((200,)),
            pltpu.SemaphoreType.DMA((200,)),
            pltpu.SemaphoreType.DMA((64,)),
        ],
        compiler_params=pltpu.CompilerParams(
            collective_id=1, has_side_effects=True, vmem_limit_bytes=56 << 20
        ),
        name="scatter",
    )(wide, deep, vecs, half_out, half_grad)


def norm_apply(stream, gain, offset):
    center = stream - jnp.mean(stream, axis=-1, keepdims=True)
    spread = jnp.mean(center * center, axis=-1, keepdims=True)
    return center * lax.rsqrt(spread + 1e-05) * gain + offset


def col_sums(values):
    return jnp.sum(values.astype(F32), axis=0)


def dot(a, b):
    return jnp.dot(a, b, preferred_element_type=F32)


def dot_nt(a, b):
    return lax.dot_general(a, b, (((1,), (1,)), ((), ())), preferred_element_type=F32)


def dot_tn(a, b):
    return lax.dot_general(a, b, (((0,), (0,)), ((), ())), preferred_element_type=F32)


def split_vectors(row):
    parts, start = [], 0
    for width in VECTOR_WIDTHS:
        parts.append(row[start : start + 128 * width].astype(F32))
        start += 128 * width
    return parts


def layer_forward(stream, wide, deep, vectors):
    gain_one, offset_one, bias_qv, bias_out, gain_two, offset_two, bias_up, bias_down = vectors
    normed = norm_apply(stream, gain_one, offset_one).astype(BF16)
    length = stream.shape[0]
    query, keys, values = (
        (dot(normed, wide[slab]) + bias).astype(BF16).reshape(length, HEADS, HEAD)
        for slab, bias in ((0, bias_qv[:D]), (1, 0.0), (2, bias_qv[D:]))
    )
    scores = jnp.einsum("qhe,khe->hqk", query, keys, preferred_element_type=F32) * 0.125
    probs = jax.nn.softmax(scores, axis=-1)
    attended = jnp.einsum("hqk,khe->qhe", probs.astype(BF16), values, preferred_element_type=F32)
    attended = attended.astype(BF16).reshape(length, D)
    middle = stream + dot(attended, wide[3]) + bias_out
    normed_two = norm_apply(middle, gain_two, offset_two).astype(BF16)
    pre = [dot(normed_two, wide[4 + i]) + bias_up[i * D : (i + 1) * D] for i in range(4)]
    active = [jax.nn.gelu(part, approximate=True).astype(BF16) for part in pre]
    active = jnp.concatenate(active, axis=1)
    result = middle + jnp.concatenate([dot(active, deep[i]) for i in range(2)], axis=1) + bias_down
    return result, (normed, query, keys, values, probs, attended, middle, normed_two, pre, active)


def layer_backward(stream, wide, deep, vectors, saved, grad_top):
    gain_one, offset_one, bias_qv, bias_out, gain_two, offset_two, bias_up, bias_down = vectors
    normed, query, keys, values, probs, attended, middle, normed_two, pre, active = saved
    length = stream.shape[0]
    grad_z = grad_top.astype(BF16)
    grad_deep = jnp.stack([dot_tn(active, grad_z[:, i * 384 : (i + 1) * 384]) for i in range(2)])
    grad_bias_down = col_sums(grad_z)
    grad_active = dot_nt(grad_z[:, :384], deep[0]) + dot_nt(grad_z[:, 384:], deep[1])
    pre = jnp.concatenate(pre, axis=1)
    pull = jax.vjp(lambda inner: jax.nn.gelu(inner, approximate=True), pre)[1]
    grad_pre = pull(grad_active)[0].astype(BF16)
    grad_bias_up = col_sums(grad_pre)
    grad_up = [dot_tn(normed_two, grad_pre[:, i * D : (i + 1) * D]) for i in range(4)]
    grad_normed_two = sum(dot_nt(grad_pre[:, i * D : (i + 1) * D], wide[4 + i]) for i in range(4))
    pull = jax.vjp(norm_apply, middle, gain_two, offset_two)[1]
    grad_norm, grad_gain_two, grad_offset_two = pull(grad_normed_two)
    grad_middle = grad_top + grad_norm
    grad_branch = grad_middle.astype(BF16)
    grad_out = dot_tn(attended, grad_branch)
    grad_bias_out = col_sums(grad_branch)
    grad_attended = dot_nt(grad_branch, wide[3]).astype(BF16).reshape(length, HEADS, HEAD)
    grad_probs = jnp.einsum("qhe,khe->hqk", grad_attended, values, preferred_element_type=F32)
    grad_values = jnp.einsum(
        "hqk,qhe->khe", probs.astype(BF16), grad_attended, preferred_element_type=F32
    )
    row_dot = jnp.sum(grad_probs * probs, axis=-1, keepdims=True)
    grad_scores = (probs * (grad_probs - row_dot)).astype(BF16)
    grad_query = jnp.einsum("hqk,khe->qhe", grad_scores, keys, preferred_element_type=F32) * 0.125
    grad_keys = jnp.einsum("hqk,qhe->khe", grad_scores, query, preferred_element_type=F32) * 0.125
    grad_qkv = [part.astype(BF16).reshape(length, D) for part in (grad_query, grad_keys, grad_values)]
    grad_w_qkv = [dot_tn(normed, part) for part in grad_qkv]
    grad_bias_qv = jnp.concatenate([col_sums(grad_qkv[0]), col_sums(grad_qkv[2])])
    grad_normed = sum(dot_nt(part, wide[slab]) for slab, part in enumerate(grad_qkv))
    pull = jax.vjp(norm_apply, stream, gain_one, offset_one)[1]
    grad_norm, grad_gain_one, grad_offset_one = pull(grad_normed)
    grad_wide = jnp.stack(
        [part.astype(BF16) for part in (*grad_w_qkv, grad_out, *grad_up)]
    )
    vecs = jnp.concatenate(
        [
            grad_gain_one, grad_offset_one, grad_bias_qv, grad_bias_out,
            grad_gain_two, grad_offset_two, grad_bias_up, grad_bias_down,
        ]
    )
    return grad_middle + grad_norm, grad_wide, grad_deep.astype(BF16), vecs


def shards(
    hidden, cotangent, remaining, order,
    norm1_gain, norm1_bias, w_qkv, bias_qv, w_out, bias_out,
    norm2_gain, norm2_bias, w_up, bias_up, w_down, bias_down,
):
    half_rows = hidden.shape[1]
    length = 2 * half_rows
    core = lax.axis_index("fsdp")
    index = lax.axis_index("dp") * 2 + core
    vectors = (
        norm1_gain, norm1_bias, bias_qv, bias_out, norm2_gain, norm2_bias, bias_up, bias_down
    )
    own_hidden, own_cot, wide, deep, vecs = gather(
        hidden, cotangent, w_qkv, w_out, w_up, w_down, spread(vectors, index)
    )
    wide = wide.reshape(LAYERS, 8, D, D)
    deep = deep.reshape(LAYERS, 2, FF, 384)
    vecs = vecs.reshape(LAYERS, -1)
    own_order, own_remaining = order[core], remaining[core]
    positions = jnp.arange(length, dtype=jnp.int32)
    live = positions >= length - own_remaining
    mask = jnp.any((own_order[:, None] == positions[None, :]) & live[:, None], axis=0)
    grad = own_cot.reshape(length, D).astype(F32) * mask.astype(F32)[:, None]
    stream = own_hidden.reshape(length, D).astype(F32)
    inputs, saved = [], []
    for layer in range(LAYERS):
        inputs.append(stream)
        stream, kept = layer_forward(stream, wide[layer], deep[layer], split_vectors(vecs[layer]))
        saved.append(kept)
    grads = [None] * LAYERS
    for layer in reversed(range(LAYERS)):
        grad, *grads[layer] = layer_backward(
            inputs[layer], wide[layer], deep[layer], split_vectors(vecs[layer]), saved[layer], grad
        )
    grad_wide, grad_deep, grad_vecs = (jnp.stack(parts) for parts in zip(*grads))
    g_qkv, g_out, g_up, g_down, vec_sums, out, grad_hidden = scatter(
        grad_wide.reshape(LAYERS, 4, 2, 4, 4, 48, D),
        grad_deep.reshape(LAYERS, 2, 4, 4, 4, 48, 384),
        grad_vecs.reshape(VECTOR_ROWS, 128),
        stream.astype(BF16).reshape(2, half_rows, D),
        grad.reshape(2, half_rows, D),
    )
    vec_sums, parts, start = vec_sums.reshape(LAYERS, -1), [], 0
    for width in VECTOR_WIDTHS:
        parts.append(lax.dynamic_slice_in_dim(vec_sums, start + width * index, width, 1))
        start += 128 * width
    gain_one, offset_one, qv, out_bias, gain_two, offset_two, up, down = parts
    return (
        out, grad_hidden, gain_one, offset_one, g_qkv, qv, g_out, out_bias,
        gain_two, offset_two, g_up, up, g_down, down,
    )


def solution(mesh):
    tokens, rows = P("dp", "fsdp", None), P(None, ("dp", "fsdp"), None)
    vector = P(None, ("dp", "fsdp"))
    weights = (
        vector, vector, rows, vector, rows, vector, vector, vector, rows, vector, rows, vector
    )
    return jax.shard_map(
        shards,
        mesh=mesh,
        in_specs=(tokens, tokens, P("dp"), P("dp", None), *weights),
        out_specs=(tokens, tokens, *weights),
        check_vma=False,
    )
```

```python
import types

import jax
import jax.numpy as jnp
from jax import lax
from jax.experimental import pallas as pl
from jax.experimental.pallas import tpu as pltpu
from jax.sharding import PartitionSpec as P

HEAD = 64
HEADS = 12
LAYERS = 2
D = 768
FF = 3072
MESH = pl.DeviceIdType.MESH
BF16, F32 = jnp.bfloat16, jnp.float32

AXES = {"q": "yczx", "u": "yczx", "d": "czxy"}
STREAMS = {
    "q": ((slice(0, 32), "xyz"), (slice(32, 48), "xzy")),
    "u": ((slice(0, 32), "xyz"), (slice(32, 48), "xzy")),
    "d": ((slice(0, 32), "xzy"), (slice(32, 48), "yzx")),
}
FIRST = {
    "q": ((slice(0, 48), "x"),),
    "u": ((slice(0, 48), "x"),),
    "d": ((slice(0, 32), "x"), (slice(32, 48), "y")),
}
KINDS = "qud"
ALL = slice(None)
STEPS = (1, 3, 2)


def place():
    dp, core = lax.axis_index("dp"), lax.axis_index("fsdp")
    return {"z": dp // 16, "x": (dp // 4) % 4, "y": dp % 4, "c": core}


def device(at):
    return ((at["z"] * 4 + at["x"]) * 4 + at["y"], at["c"])


def moved(at, axis, step):
    size = 2 if axis == "c" else 4
    return {**at, axis: (at[axis] + step) % size}


class Links:
    def __init__(self, send_sems, recv_sems):
        self.send_sems, self.recv_sems, self.used, self.open = send_sems, recv_sems, 0, []

    def copy(self, src, dst, target, number):
        return pltpu.make_async_remote_copy(
            src_ref=src,
            dst_ref=dst,
            send_sem=self.send_sems.at[number],
            recv_sem=self.recv_sems.at[number],
            device_id=device(target),
            device_id_type=MESH,
        )

    def take(self, count):
        self.used += count
        return self.used - count

    def send(self, src, dst, target):
        copy = self.copy(src, dst, target, self.take(1))
        copy.start()
        self.open.append(copy)
        return copy

    def drain(self):
        for copy in self.open:
            copy.wait_send()
        self.open = []


def greet(me):
    partners = [moved(moved(me, "y", dy), "c", dc) for dy in range(4) for dc in range(2)][1:]
    partners += [moved(me, axis, step) for axis in "xz" for step in (1, 2, 3)]
    barrier = pltpu.get_barrier_semaphore()
    for partner in partners:
        pl.semaphore_signal(barrier, inc=1, device_id=device(partner), device_id_type=MESH)
    pl.semaphore_wait(barrier, len(partners))


T = 256
ROWS = 128
GAIN1, OFF1, BIAS_Q, BIAS_OUT, GAIN2, OFF2, BIAS_UP, BIAS_DOWN = 0, 1, 2, 5, 6, 7, 8, 12


def dot(a, b):
    return jnp.dot(a, b, preferred_element_type=F32)


def dot_nt(a, b):
    return lax.dot_general(a, b, (((1,), (1,)), ((), ())), preferred_element_type=F32)


def dot_tn(a, b):
    return lax.dot_general(a, b, (((0,), (0,)), ((), ())), preferred_element_type=F32)


def slab(ref, layer, index):
    return jnp.concatenate([ref[layer, index, core].reshape(D, 384) for core in range(2)], axis=1)


def chunk(ref, layer, index):
    return jnp.concatenate([ref[layer, core, index].reshape(D, 384) for core in range(2)], axis=1)


def put_slab(ref, layer, index, value):
    for core in range(2):
        ref[layer, index, core] = value[:, core * 384 : (core + 1) * 384].reshape(4, 4, 48, 384)


def put_chunk(ref, layer, index, value):
    for core in range(2):
        ref[layer, core, index] = value[:, core * 384 : (core + 1) * 384].reshape(4, 4, 48, 384)


def rows_of(index):
    return pl.ds(pl.multiple_of(index * ROWS, ROWS), ROWS)


def normal(x):
    center = x - jnp.mean(x, axis=-1, keepdims=True)
    scale = lax.rsqrt(jnp.mean(center * center, axis=-1, keepdims=True) + 1e-05)
    return center * scale, scale


def norm_into(x_ref, vec, gain, offset, out_ref):
    @pl.loop(0, T // ROWS)
    def _(index):
        rows = rows_of(index)
        hat, _ = normal(x_ref[rows, :].astype(F32))
        out_ref[rows, :] = (hat * vec[gain : gain + 1, :] + vec[offset : offset + 1, :]).astype(BF16)


def fold(value):
    return jnp.sum(value.reshape(ROWS // 8, 8, value.shape[1]), axis=0)


def total(value):
    return jnp.sum(value, axis=0, keepdims=True)


def norm_back(x_ref, grad_ref, vec, sums, gain, offset, top_ref, out_ref, bias=None, low_ref=None):
    zero = jnp.zeros((8, D), F32)

    def body(index, carry):
        sum_gain, sum_offset, sum_bias = carry
        rows = rows_of(index)
        hat, scale = normal(x_ref[rows, :].astype(F32))
        grad = grad_ref[rows, :]
        scaled = grad * vec[gain : gain + 1, :]
        inner = scaled - jnp.mean(scaled, axis=-1, keepdims=True)
        inner -= hat * jnp.mean(scaled * hat, axis=-1, keepdims=True)
        result = top_ref[rows, :] + scale * inner
        out_ref[rows, :] = result
        low = result.astype(BF16)
        if low_ref is not None:
            low_ref[rows, :] = low
        return sum_gain + fold(grad * hat), sum_offset + fold(grad), sum_bias + fold(low.astype(F32))

    sum_gain, sum_offset, sum_bias = lax.fori_loop(0, T // ROWS, body, (zero, zero, zero))
    sums[gain : gain + 1, :] = total(sum_gain)
    sums[offset : offset + 1, :] = total(sum_offset)
    if bias is not None:
        sums[bias : bias + 1, :] = total(sum_bias)


def gelu_parts(u):
    inner = 0.7978845608028654 * (u + 0.044715 * u * u * u)
    t = jnp.tanh(inner)
    slope = 0.7978845608028654 * (1.0 + 0.134145 * u * u)
    half = 0.5 * (1.0 + t)
    return u * half, half + 0.5 * u * (1.0 - t * t) * slope


def gelu(u):
    return 0.5 * u * (1.0 + jnp.tanh(0.7978845608028654 * (u + 0.044715 * u * u * u)))


def head_mask(which, scale=1.0):
    lane = lax.broadcasted_iota(jnp.int32, (1, 128), 1)
    return jnp.where(lane // HEAD == which, scale, 0.0).astype(BF16)


def lanes_of(pair):
    return pl.ds(pl.multiple_of(pair * 128, 128), 128)


def forward_qkv(layer, m):
    norm_into(m.x[layer], m.vec.at[layer], GAIN1, OFF1, m.h.at[layer])

    @pl.loop(0, 3)
    def _(part):
        bias = m.vec[layer, pl.ds(BIAS_Q + part, 1), :]
        m.qkv[layer, part] = (dot(m.h[layer], slab(m.wq, layer, part)) + bias).astype(BF16)


def forward_attention(layer, m):
    @pl.loop(0, HEADS // 2)
    def _(pair):
        lanes = lanes_of(pair)
        query, keys, values = (m.qkv[layer, part, :, lanes] for part in range(3))
        attended = jnp.zeros((T, 128), F32)
        for which in range(2):
            scores = dot_nt(query * head_mask(which, 0.125), keys)
            grown = jnp.exp(scores - jnp.max(scores, axis=-1, keepdims=True))
            probs = grown * (1.0 / jnp.sum(grown, axis=-1, keepdims=True))
            probs = probs.astype(BF16)
            m.probs[layer, 2 * pair + which] = probs
            attended += dot(probs, values * head_mask(which))
        m.o[layer, :, lanes] = attended.astype(BF16)


def forward_out(layer, m):
    m.mid[layer] = (
        m.x[layer][...].astype(F32)
        + dot(m.o[layer], slab(m.wq, layer, 3))
        + m.vec[layer, BIAS_OUT : BIAS_OUT + 1, :]
    )
    norm_into(m.mid.at[layer], m.vec.at[layer], GAIN2, OFF2, m.h2.at[layer])


def forward_up(layer, m):
    @pl.loop(0, 4)
    def _(index):
        bias = m.vec[layer, pl.ds(BIAS_UP + index, 1), :]
        u = dot(m.h2[layer], slab(m.wu, layer, index)) + bias
        m.u[layer, index] = u.astype(BF16)
        m.a[index] = gelu(u).astype(BF16)


def forward_down(layer, m):
    out = m.x[layer + 1]
    out[...] = m.mid[layer] + m.vec[layer, BIAS_DOWN : BIAS_DOWN + 1, :]

    @pl.loop(0, 4)
    def _(index):
        out[...] += dot(m.a[index], chunk(m.wd, layer, index))


def backward_ffn(layer, m, index):
    grad_active = dot_nt(m.gz[...], chunk(m.wd, layer, index))
    active, slope = gelu_parts(m.u[layer, index].astype(F32))
    pre = (grad_active * slope).astype(BF16)
    m.gu[...] = pre
    m.a[0] = active.astype(BF16)
    m.sums[layer, pl.ds(BIAS_UP + index, 1), :] = total(pre.astype(F32))
    m.gh[...] += dot_nt(m.gu[...], slab(m.wu, layer, index))
    put_chunk(m.wd, layer, index, dot_tn(m.a[0], m.gz[...]).astype(BF16))
    put_slab(m.wu, layer, index, dot_tn(m.h2[layer], m.gu[...]).astype(BF16))


def backward_mid(layer, m):
    norm_back(
        m.mid.at[layer], m.gh, m.vec.at[layer], m.sums.at[layer], GAIN2, OFF2, m.g, m.g, BIAS_OUT, m.gz
    )
    m.go[...] = dot_nt(m.gz[...], slab(m.wq, layer, 3)).astype(BF16)
    put_slab(m.wq, layer, 3, dot_tn(m.o[layer], m.gz[...]).astype(BF16))


def backward_attention(layer, m):
    @pl.loop(0, HEADS // 2)
    def _(pair):
        lanes = lanes_of(pair)
        query, keys, values = (m.qkv[layer, part, :, lanes] for part in range(3))
        grad = m.go[:, lanes]
        zero = jnp.zeros((T, 128), F32)
        grad_query, grad_keys, grad_values = zero, zero, zero
        for which in range(2):
            low = m.probs[layer, 2 * pair + which]
            probs = low.astype(F32)
            part = grad * head_mask(which)
            grad_probs = dot_nt(part, values)
            grad_values += dot_tn(low, part)
            row_dot = jnp.sum(grad_probs * probs, axis=-1, keepdims=True)
            grad_scores = (probs * (grad_probs - row_dot)).astype(BF16)
            grad_query += dot(grad_scores, keys * head_mask(which, 0.125))
            grad_keys += dot_tn(grad_scores, query * head_mask(which, 0.125))
        for part, value in enumerate((grad_query, grad_keys, grad_values)):
            m.gqkv[part, :, lanes] = value.astype(BF16)


def backward_qkv(layer, m, part):
    m.sums[layer, pl.ds(BIAS_Q + part, 1), :] = total(m.gqkv[part].astype(F32))
    m.gh[...] += dot_nt(m.gqkv[part], slab(m.wq, layer, part))
    put_slab(m.wq, layer, part, dot_tn(m.h[layer], m.gqkv[part]).astype(BF16))


def backward_in(layer, m, out_ref):
    norm_back(m.x[layer], m.gh, m.vec.at[layer], m.sums.at[layer], GAIN1, OFF1, m.g, out_ref)


def upstream(order_ref, remaining_ref, cot_ref, m):
    live = lax.broadcasted_iota(jnp.int32, (1, T), 1) >= T - remaining_ref

    def body(index, carry):
        rows = rows_of(index)
        spot = index * ROWS + lax.broadcasted_iota(jnp.int32, (ROWS, 1), 0)
        hit = jnp.where((order_ref == spot) & live, 1.0, 0.0)
        mask = jnp.max(hit, axis=-1, keepdims=True)
        grad = cot_ref[rows, :].astype(F32) * mask
        m.g[rows, :] = grad
        return carry

    lax.fori_loop(0, T // ROWS, body, 0)


def top(layer, m):
    def body(index, carry):
        rows = rows_of(index)
        low = m.g[rows, :].astype(BF16)
        m.gz[rows, :] = low
        return carry + fold(low.astype(F32))

    sums = lax.fori_loop(0, T // ROWS, body, jnp.zeros((8, D), F32))
    m.sums[layer, BIAS_DOWN : BIAS_DOWN + 1, :] = total(sums)
    m.gh[...] = jnp.zeros((T, D), F32)


class Gather:
    def __init__(self, kind, layer, m):
        self.kind, self.layer, self.m = kind, layer, m
        self.streams, self.handed = STREAMS[kind], []

    def part(self, rows, at):
        index = tuple(at[axis] for axis in AXES[self.kind])
        return self.m.weights[self.kind].at[(self.layer, *index, rows, ALL)]

    def hand_over(self, rows, at):
        part = self.part(rows, at)
        self.handed.append(self.m.links.send(part, part, moved(self.m.me, "c", 1)))

    def out(self, rows, at, axis, steps):
        part, me = self.part(rows, at), self.m.me
        return {step: self.m.links.send(part, part, moved(me, axis, step)) for step in steps}

    def first(self):
        me = self.m.me
        self.copies = [self.out(rows, me, axis, STEPS) for rows, axis in FIRST[self.kind]]

    def second(self):
        me = self.m.me
        for (rows, axis), copies in zip(FIRST[self.kind], self.copies):
            for step in STEPS:
                copies[step].wait_recv()
            self.hand_over(rows, {**me, axis: ALL})
        self.copies = [
            self.out(rows, {**me, axes[0]: ALL}, axes[1], STEPS) for rows, axes in self.streams
        ]

    def third(self):
        me = self.m.me
        for (rows, axes), copies in zip(self.streams, self.copies):
            for step in STEPS:
                copies[step].wait_recv()
                self.hand_over(rows, {**moved(me, axes[1], -step), axes[0]: ALL})
        self.copies = [
            self.out(rows, {**me, axes[0]: ALL, axes[1]: ALL}, axes[2], (1, 3))
            for rows, axes in self.streams
        ]

    def relay(self):
        me, self.halves = self.m.me, []
        for (rows, axes), copies in zip(self.streams, self.copies):
            for step, start in ((1, 0), (3, 2)):
                copies[step].wait_recv()
                came = {**moved(me, axes[2], -step), axes[1]: ALL}
                half = self.part(rows, {**came, axes[0]: pl.ds(start, 2)})
                self.halves.append(self.m.links.send(half, half, moved(me, axes[2], step)))
                self.hand_over(rows, {**came, axes[0]: ALL})

    def finish(self):
        for copy in self.halves:
            copy.wait_recv()
        for rows, axes in self.streams:
            self.hand_over(rows, {**moved(self.m.me, axes[2], 2), axes[0]: ALL, axes[1]: ALL})

    def arrive(self):
        for copy in self.handed:
            copy.wait_recv()


class Scatter:
    def __init__(self, kind, layer, m):
        self.kind, self.layer, self.m = kind, layer, m
        self.streams = [(rows, axes[::-1]) for rows, axes in STREAMS[kind]]
        self.base = m.links.take(4)
        self.slots = [m.first[kind, number] for number in range(2)]
        self.later = [m.second[kind, number].at[layer] for number in range(2)]
        self.last = [m.third[kind, number].at[layer] for number in range(2)]
        self.free = [m.free.at[2 * KINDS.index(kind) + number] for number in range(2)]
        self.room, self.got = (m.free.at[6], m.got_d) if kind == "d" else (m.free.at[7], m.got_qu)

    def part(self, rows, at):
        index = tuple(at.get(axis, ALL) for axis in AXES[self.kind])
        return self.m.weights[self.kind].at[(self.layer, *index, rows, ALL)]

    def between(self, index):
        axis, sibling = ("z" if self.kind == "d" else "y"), moved(self.m.me, "c", 1)
        src = self.part(ALL, {axis: index, "c": sibling["c"]})
        return self.m.links.copy(src, self.got.at[index], sibling, self.base + index)

    def wait_room(self):
        pl.semaphore_wait(self.room, 1)

    def join(self, more):
        m, me = self.m, self.m.me
        axis, others = ("z", "xy") if self.kind == "d" else ("y", "zx")
        for index in range(4):
            copy = self.between(index)
            copy.wait_recv()
            m.links.open.append(copy)

        @pl.loop(0, 16)
        def _(spot):
            for third in range(4):
                at = {axis: spot // 4, others[0]: spot % 4, others[1]: third, "c": me["c"]}
                own = self.part(ALL, at)
                own[...] += self.got[spot // 4, spot % 4, third]

        if more:
            pl.semaphore_signal(
                self.room, inc=1, device_id=device(moved(me, "c", 1)), device_id_type=MESH
            )
        self.copies = []
        for (rows, axes), slots, free in zip(self.streams, self.slots, self.free):
            if self.layer == 0:
                pl.semaphore_wait(free, 3)
            for step in STEPS:
                target = moved(me, axes[0], step)
                src = self.part(rows, {"c": me["c"], axes[0]: target[axes[0]]})
                self.copies.append(m.links.send(src, slots.at[step - 1], target))

    def rest(self, done):
        return [axis for axis in AXES[self.kind] if axis != "c" and axis not in done]

    def add(self, target, slots):
        value = target[...].astype(F32)
        for slot in slots:
            value += slot[...].astype(F32)
        return value

    def second(self):
        m, me = self.m, self.m.me
        for copy in self.copies:
            copy.wait_recv()
        self.copies = []
        for (rows, axes), slots, later, free in zip(
            self.streams, self.slots, self.later, self.free
        ):
            here = {"c": me["c"], axes[0]: me[axes[0]]}
            others = self.rest(here)

            @pl.loop(0, 4)
            def _(one):
                for two in range(4):
                    target = self.part(rows, {**here, others[0]: one, others[1]: two})
                    total = self.add(target, [slots.at[step, one, two] for step in range(3)])
                    target[...] = total.astype(BF16)

            if self.layer == 1:
                for step in STEPS:
                    peer = device(moved(me, axes[0], step))
                    pl.semaphore_signal(free, inc=1, device_id=peer, device_id_type=MESH)
            for step in STEPS:
                target = moved(me, axes[1], step)
                src = self.part(rows, {**here, axes[1]: target[axes[1]]})
                self.copies.append(m.links.send(src, later.at[step - 1], target))

    def third(self):
        m, me = self.m, self.m.me
        for copy in self.copies:
            copy.wait_recv()
        self.copies = []
        for (rows, axes), later, last in zip(self.streams, self.later, self.last):
            here = {"c": me["c"], axes[0]: me[axes[0]], axes[1]: me[axes[1]]}
            for one in range(4):
                target = self.part(rows, {**here, axes[2]: one})
                target[...] = self.add(target, [later.at[step, one] for step in range(3)]).astype(BF16)
            for step in STEPS:
                target = moved(me, axes[2], step)
                src = self.part(rows, {**here, axes[2]: target[axes[2]]})
                self.copies.append(m.links.send(src, last.at[step - 1], target))

    def finish(self):
        for copy in self.copies:
            copy.wait_recv()
        for (rows, _), last in zip(self.streams, self.last):
            total = self.add(self.part(rows, self.m.me), [last.at[step] for step in range(3)])
            self.m.totals[self.kind][self.layer, rows, :] = total


def spot_matrix(base, width):
    row = lax.broadcasted_iota(jnp.int32, (128, D), 0)
    lane = lax.broadcasted_iota(jnp.int32, (128, D), 1)
    return jnp.where((lane == base + row) & (row < width), 1.0, 0.0).astype(BF16)


def flag(condition):
    return jnp.where(condition, 1.0, 0.0).astype(F32)


NARROW_ROWS = (GAIN1, OFF1, BIAS_OUT, GAIN2, OFF2, BIAS_DOWN)


def spread_vectors(index, narrow, wide_qv, wide_up, stage, out):
    stage[...] = jnp.zeros(stage.shape, F32)
    for layer in range(LAYERS):
        rows = slice(layer, layer + 1)
        for row, vector in zip(NARROW_ROWS, narrow):
            stage[0, layer, row : row + 1, 0:6] = vector[rows, :].astype(F32)
        pair = wide_qv[rows, :].astype(F32)
        stage[1, layer, BIAS_Q : BIAS_Q + 1, 0:12] = pair * flag(index < 64)
        stage[1, layer, BIAS_Q + 2 : BIAS_Q + 3, 0:12] = pair * flag(index >= 64)
        for row in range(4):
            up = wide_up[rows, :].astype(F32) * flag(index // 32 == row)
            stage[2, layer, BIAS_UP + row : BIAS_UP + row + 1, 0:24] = up
    for layer in range(LAYERS):
        total = jnp.zeros((16, D), F32)
        for number, matrix in enumerate(spot_matrices(index)):
            total += dot(stage[number, layer].astype(BF16), matrix)
        out[layer] = total


def spot_matrices(index):
    return (
        spot_matrix(6 * index, 6), spot_matrix(12 * (index % 64), 12), spot_matrix(24 * (index % 32), 24)
    )


def own_entries(index, total, out):
    for layer in range(LAYERS):
        value = total[layer]
        high = value.astype(BF16)
        middle = (value - high.astype(F32)).astype(BF16)
        low = (value - high.astype(F32) - middle.astype(F32)).astype(BF16)
        found = []
        for matrix in spot_matrices(index):
            found.append(dot_nt(high, matrix) + (dot_nt(middle, matrix) + dot_nt(low, matrix)))
        for place_out, row in enumerate(NARROW_ROWS):
            out[layer, place_out : place_out + 1, :] = found[0][row : row + 1]
        out[layer, 6:7, :] = found[1][BIAS_Q : BIAS_Q + 1] * flag(index < 64) + found[1][
            BIAS_Q + 2 : BIAS_Q + 3
        ] * flag(index >= 64)
        up = jnp.zeros((1, 128), F32)
        for row in range(4):
            up += found[2][BIAS_UP + row : BIAS_UP + row + 1] * flag(index // 32 == row)
        out[layer, 7:8, :] = up


class VectorSum:
    ORDER = "xyzc"

    def __init__(self, m):
        self.m, self.number = m, 0

    def begin(self):
        m, axis = self.m, self.ORDER[self.number]
        self.copies = [
            m.links.send(
                m.vec_state.at[self.number],
                m.vec_recv.at[3 * self.number + step - 1],
                moved(m.me, axis, step),
            )
            for step in range(1, 2 if axis == "c" else 4)
        ]

    def end(self):
        m, total = self.m, self.m.vec_state[self.number]
        for copy in self.copies:
            copy.wait_recv()
        for step in range(len(self.copies)):
            total += m.vec_recv[3 * self.number + step]
        self.number += 1
        if self.number < 4:
            m.vec_state[self.number] = total
        return total

    def turn(self):
        self.end()
        self.begin()


def kernel(
    hidden, cot, order, remaining, w_qkv, w_out, w_up, w_down,
    gain1, off1, bias_qv, bias_out, gain2, off2, bias_up, bias_down,
    out, grad, g_qkv, g_out, g_up, g_down, vec_out,
    wq, wu, wd, got_qu, got_d, q_a, q_b, u_a, u_b, d_a, d_b, q_a2, q_b2, u_a2, u_b2, d_a2, d_b2,
    q_a3, q_b3, u_a3, u_b3, d_a3, d_b3, sum_q, sum_u, sum_d,
    x0, x1, h, qkv, probs, o, mid, h2, u, tmp, g, gh, gz, cots, outs, vec, sums,
    vec_state, vec_recv, stage, send_a, recv_a, send_d, recv_d, asm, send_f, recv_f, send_df, recv_df,
    send_sems, recv_sems, local_sems, free,
):
    me = place()
    sibling = moved(me, "c", 1)
    mine = 2 * me["y"] + me["c"]
    index = ((me["z"] * 4 + me["x"]) * 4 + me["y"]) * 2 + me["c"]
    links = Links(send_sems, recv_sems)
    m = types.SimpleNamespace(
        me=me, links=links, weights={"q": wq, "u": wu, "d": wd}, wq=wq, wu=wu, wd=wd,
        got_qu=got_qu, got_d=got_d, free=free, totals={"q": sum_q, "u": sum_u, "d": sum_d},
        first={("q", 0): q_a, ("q", 1): q_b, ("u", 0): u_a, ("u", 1): u_b, ("d", 0): d_a, ("d", 1): d_b},
        second={
            ("q", 0): q_a2, ("q", 1): q_b2, ("u", 0): u_a2, ("u", 1): u_b2, ("d", 0): d_a2, ("d", 1): d_b2
        },
        third={
            ("q", 0): q_a3, ("q", 1): q_b3, ("u", 0): u_a3, ("u", 1): u_b3, ("d", 0): d_a3, ("d", 1): d_b3
        },
        x=[x0, x1, g], h=h, qkv=qkv, probs=probs, o=o, mid=mid, h2=h2, u=u, a=tmp, g=g, gh=gh, gz=gz,
        gu=tmp.at[1], go=tmp.at[3], gqkv=tmp, vec=vec, sums=sums, vec_state=vec_state, vec_recv=vec_recv,
    )

    asm[...] = jnp.zeros(asm.shape, F32)
    send_f[...] = jnp.zeros(send_f.shape, F32)
    for owner in range(8):
        columns = slice(384 * (owner % 2), 384 * (owner % 2) + 384)
        for layer in range(LAYERS):
            for row in range(6):
                if owner < 6:
                    part = w_qkv[row, layer : layer + 1, 384 * owner : 384 * owner + 384]
                else:
                    part = w_out[row, layer : layer + 1, columns]
                asm[owner, 8 * layer + row : 8 * layer + row + 1, :] = part.astype(F32)
                part = w_up[row, layer : layer + 1, 384 * owner : 384 * owner + 384]
                asm[owner, 16 + 8 * layer + row : 17 + 8 * layer + row, :] = part.astype(F32)
    for owner in range(8):
        send_a[owner] = asm[owner, 0:32, :].astype(BF16)
    for half in range(2):
        for layer in range(LAYERS):
            part = w_down[layer, :, 384 * half : 384 * half + 384]
            send_df[half, 24 * layer : 24 * layer + 24, :] = part.astype(F32)
        send_d[half] = send_df[half].astype(BF16)
    narrow = (gain1, off1, bias_out, gain2, off2, bias_down)
    spread_vectors(index, narrow, bias_qv, bias_up, stage, vec_state.at[0])

    greet(me)

    def group_sends(src, dst):
        copies = []
        for dy in range(4):
            for dc in range(2):
                if dy or dc:
                    target = moved(moved(me, "y", dy), "c", dc)
                    spot = src.at[2 * target["y"] + target["c"]]
                    copies.append(links.send(spot, dst.at[mine], target))
        return copies

    arrivals = group_sends(send_a, recv_a)
    arrivals.append(links.send(send_d.at[1 - me["c"]], recv_d.at[me["c"]], sibling))
    recv_a[mine] = send_a[mine]
    recv_d[me["c"]] = send_d[me["c"]]
    here = pl.ds(pl.multiple_of(128 * me["c"], 128), 128)
    there = pl.ds(pl.multiple_of(128 * (1 - me["c"]), 128), 128)
    halves = []
    for number, (src, dst) in enumerate(((hidden, x0), (cot, cots))):
        halves.append(links.send(src.at[1 - me["c"]], dst.at[here, :], sibling))
        copy = pltpu.make_async_copy(src.at[me["c"]], dst.at[here, :], local_sems.at[number])
        copy.start()
        halves.append(copy)
    vectors = VectorSum(m)
    vectors.begin()
    for copy in arrivals:
        copy.wait_recv()
    gathers = [Gather(kind, layer, m) for layer in range(LAYERS) for kind in KINDS]
    own = (me["y"], me["c"], me["z"], me["x"])
    for layer in range(LAYERS):
        for group, target in enumerate((wq, wu)):
            for source in range(8):
                rows = slice(16 * group + 8 * layer, 16 * group + 8 * layer + 6)
                asm[group, 6 * source : 6 * source + 6, :] = recv_a[source].astype(F32)[rows]
            target[(layer, *own)] = asm[group].astype(BF16)
        for half in range(2):
            asm[2, 24 * half : 24 * half + 24, :] = recv_d[half].astype(F32)[
                24 * layer : 24 * layer + 24
            ]
        wd[layer, me["c"], me["z"], me["x"], me["y"]] = asm[2].astype(BF16)
        for gather in gathers[3 * layer : 3 * layer + 3]:
            gather.first()
    vectors.turn()
    gathers[0].second()
    vectors.turn()
    gathers[1].second()
    gathers[0].third()
    gathers[2].second()
    gathers[1].third()
    for gather in gathers[3:]:
        gather.second()
    vectors.turn()
    gathers[0].relay()
    gathers[2].third()
    gathers[0].finish()
    gathers[1].relay()
    gathers[3].third()
    vec[...] = vectors.end()
    halves[0].wait_recv()
    halves[1].wait()
    gathers[0].arrive()

    forward_qkv(0, m)
    gathers[1].finish()
    gathers[2].relay()
    gathers[4].third()
    forward_attention(0, m)
    forward_out(0, m)
    gathers[2].finish()
    gathers[3].relay()
    gathers[5].third()
    gathers[1].arrive()
    forward_up(0, m)
    gathers[3].finish()
    gathers[4].relay()
    gathers[2].arrive()
    forward_down(0, m)
    gathers[4].finish()
    gathers[5].relay()
    gathers[3].arrive()
    forward_qkv(1, m)
    gathers[5].finish()
    forward_attention(1, m)
    forward_out(1, m)
    gathers[4].arrive()
    forward_up(1, m)
    gathers[5].arrive()
    forward_down(1, m)
    outs[...] = g[...].astype(BF16)
    links.drain()
    halves[2].wait_recv()
    halves[3].wait()

    def swap(src, dst, number):
        remote = links.send(src.at[there, :], dst.at[me["c"]], sibling)
        copy = pltpu.make_async_copy(src.at[here, :], dst.at[me["c"]], local_sems.at[number])
        copy.start()
        return remote, copy

    results = [swap(outs, out, 2)]
    upstream(order[me["c"]], remaining[me["c"]], cots, m)
    sums[...] = jnp.zeros(sums.shape, F32)
    scatters = {(kind, layer): Scatter(kind, layer, m) for layer in (1, 0) for kind in KINDS}

    def ffn(layer):
        ups, downs = scatters["u", layer], scatters["d", layer]
        if layer == 0:
            ups.wait_room()
            downs.wait_room()

        @pl.loop(0, 4)
        def _(part):
            backward_ffn(layer, m, part)
            ups.between(part).start()
            downs.between(part).start()

    def attention_grads(layer):
        scatter = scatters["q", layer]
        scatter.wait_room()
        scatter.between(3).start()
        m.gh[...] = jnp.zeros((T, D), F32)

        @pl.loop(0, 3)
        def _(part):
            backward_qkv(layer, m, part)
            scatter.between(part).start()

    top(1, m)
    ffn(1)
    backward_mid(1, m)
    scatters["u", 1].join(True)
    scatters["d", 1].join(True)
    backward_attention(1, m)
    attention_grads(1)
    backward_in(1, m, g)
    top(0, m)
    scatters["q", 1].join(True)
    ffn(0)
    scatters["u", 1].second()
    scatters["d", 1].second()
    backward_mid(0, m)
    scatters["q", 1].second()
    scatters["u", 0].join(True)
    scatters["d", 0].join(False)
    backward_attention(0, m)
    scatters["u", 1].third()
    scatters["d", 1].third()
    attention_grads(0)
    scatters["q", 1].third()
    backward_in(0, m, g)
    results.append(swap(g, grad, 3))
    vec_state[0] = sums[...]
    scatters["q", 0].join(False)
    for kind in "udq":
        scatters[kind, 1].finish()
    vectors = VectorSum(m)
    vectors.begin()
    scatters["u", 0].second()
    scatters["d", 0].second()
    vectors.turn()
    scatters["q", 0].second()
    scatters["u", 0].third()
    scatters["d", 0].third()
    vectors.turn()
    scatters["q", 0].third()
    vectors.turn()
    for kind in "udq":
        scatters[kind, 0].finish()

    for layer in range(LAYERS):
        for owner in range(8):
            for group, total in enumerate((sum_q, sum_u)):
                start = 16 * group + 8 * layer
                send_f[owner, start : start + 6, :] = total[layer, 6 * owner : 6 * owner + 6, :]
        for owner in range(2):
            send_df[owner, 24 * layer : 24 * layer + 24, :] = sum_d[
                layer, 24 * owner : 24 * owner + 24, :
            ]
    last = group_sends(send_f, recv_f)
    last.append(links.send(send_df.at[1 - me["c"]], recv_df.at[me["c"]], sibling))
    recv_f[mine] = send_f[mine]
    recv_df[me["c"]] = send_df[me["c"]]
    sums[...] = vectors.end()
    own_entries(index, sums, vec_out)
    for copy in last:
        copy.wait_recv()
    for owner in range(8):
        columns = slice(384 * (owner % 2), 384 * (owner % 2) + 384)
        for layer in range(LAYERS):
            for row in range(6):
                spot = 8 * layer + row
                value = recv_f[owner, spot : spot + 1, :]
                if owner < 6:
                    g_qkv[row, layer : layer + 1, 384 * owner : 384 * owner + 384] = value
                else:
                    g_out[row, layer : layer + 1, columns] = value
                value = recv_f[owner, 16 + spot : 17 + spot, :]
                g_up[row, layer : layer + 1, 384 * owner : 384 * owner + 384] = value
    for layer in range(LAYERS):
        for half in range(2):
            g_down[layer, :, 384 * half : 384 * half + 384] = recv_df[
                half, 24 * layer : 24 * layer + 24, :
            ]
    for remote, copy in results:
        remote.wait_recv()
        copy.wait()
    links.drain()


def shards(
    hidden, cotangent, remaining, order,
    norm1_gain, norm1_bias, w_qkv, bias_qv, w_out, bias_out,
    norm2_gain, norm2_bias, w_up, bias_up, w_down, bias_down,
):
    vmem, hbm = pl.BlockSpec(memory_space=pltpu.VMEM), pl.BlockSpec(memory_space=pl.ANY)
    half = hidden.shape[1]
    swapped = [jnp.transpose(weight, (1, 0, 2)) for weight in (w_qkv, w_out, w_up)]
    wide, deep = (LAYERS, 4, 2, 4, 4, 48, 384), (LAYERS, 2, 4, 4, 4, 48, 384)
    sizes = [rows.stop - rows.start for kind in KINDS for rows, _ in STREAMS[kind]]
    out, grad, g_qkv, g_out, g_up, g_down, vecs = pl.pallas_call(
        kernel,
        out_shape=(
            jax.ShapeDtypeStruct((2, half, D), BF16),
            jax.ShapeDtypeStruct((2, half, D), F32),
            jax.ShapeDtypeStruct((6, LAYERS, 3 * D), F32),
            jax.ShapeDtypeStruct((6, LAYERS, D), F32),
            jax.ShapeDtypeStruct((6, LAYERS, FF), F32),
            jax.ShapeDtypeStruct((LAYERS, 24, D), F32),
            jax.ShapeDtypeStruct((LAYERS, 8, 128), F32),
        ),
        in_specs=[hbm, hbm] + [vmem] * 14,
        out_specs=(hbm, hbm) + (vmem,) * 5,
        scratch_shapes=[
            pltpu.VMEM(wide, BF16),
            pltpu.VMEM(wide, BF16),
            pltpu.VMEM(deep, BF16),
            pltpu.VMEM((4, 4, 4, 48, 384), BF16),
            pltpu.VMEM((4, 4, 4, 48, 384), BF16),
            *[pltpu.VMEM((3, 4, 4, size, 384), BF16) for size in sizes],
            *[pltpu.VMEM((LAYERS, 3, 4, size, 384), BF16) for size in sizes],
            *[pltpu.VMEM((LAYERS, 3, size, 384), BF16) for size in sizes],
            *[pltpu.VMEM((LAYERS, 48, 384), F32) for _ in range(3)],
            pltpu.VMEM((T, D), BF16),
            pltpu.VMEM((T, D), F32),
            pltpu.VMEM((LAYERS, T, D), BF16),
            pltpu.VMEM((LAYERS, 3, T, D), BF16),
            pltpu.VMEM((LAYERS, HEADS, T, T), BF16),
            pltpu.VMEM((LAYERS, T, D), BF16),
            pltpu.VMEM((LAYERS, T, D), F32),
            pltpu.VMEM((LAYERS, T, D), BF16),
            pltpu.VMEM((LAYERS, 4, T, D), BF16),
            pltpu.VMEM((4, T, D), BF16),
            pltpu.VMEM((T, D), F32),
            pltpu.VMEM((T, D), F32),
            pltpu.VMEM((T, D), BF16),
            pltpu.VMEM((T, D), BF16),
            pltpu.VMEM((T, D), BF16),
            pltpu.VMEM((LAYERS, 16, D), F32),
            pltpu.VMEM((LAYERS, 16, D), F32),
            pltpu.VMEM((4, LAYERS, 16, D), F32),
            pltpu.VMEM((10, LAYERS, 16, D), F32),
            pltpu.VMEM((3, LAYERS, 16, 128), F32),
            pltpu.VMEM((8, 32, 384), BF16),
            pltpu.VMEM((8, 32, 384), BF16),
            pltpu.VMEM((2, 48, 384), BF16),
            pltpu.VMEM((2, 48, 384), BF16),
            pltpu.VMEM((8, 48, 384), F32),
            pltpu.VMEM((8, 32, 384), F32),
            pltpu.VMEM((8, 32, 384), F32),
            pltpu.VMEM((2, 48, 384), F32),
            pltpu.VMEM((2, 48, 384), F32),
            pltpu.SemaphoreType.DMA((400,)),
            pltpu.SemaphoreType.DMA((400,)),
            pltpu.SemaphoreType.DMA((4,)),
            pltpu.SemaphoreType.REGULAR((8,)),
        ],
        compiler_params=pltpu.CompilerParams(
            collective_id=0, has_side_effects=True, vmem_limit_bytes=(63 << 20) + (1 << 19)
        ),
        name="layers",
    )(
        hidden, cotangent, order[:, None, :],
        jnp.broadcast_to(remaining[:, None, None], (2, 1, T)),
        *swapped, w_down,
        norm1_gain, norm1_bias, bias_qv, bias_out, norm2_gain, norm2_bias, bias_up, bias_down,
    )
    g_qkv, g_out, g_up = (jnp.transpose(part, (1, 0, 2)) for part in (g_qkv, g_out, g_up))
    gain1, off1, out_bias, gain2, off2, down = (vecs[:, row, 0:6] for row in range(6))
    return (
        out, grad, gain1, off1, g_qkv, vecs[:, 6, 0:12], g_out, out_bias,
        gain2, off2, g_up, vecs[:, 7, 0:24], g_down, down,
    )


def solution(mesh):
    tokens, rows = P("dp", "fsdp", None), P(None, ("dp", "fsdp"), None)
    vector = P(None, ("dp", "fsdp"))
    weights = (
        vector, vector, rows, vector, rows, vector, vector, vector, rows, vector, rows, vector
    )
    return jax.shard_map(
        shards,
        mesh=mesh,
        in_specs=(tokens, tokens, P("dp"), P("dp", None), *weights),
        out_specs=(tokens, tokens, *weights),
        check_vma=False,
    )
```

```python
import types

import jax
import jax.numpy as jnp
from jax import lax
from jax.experimental import pallas as pl
from jax.experimental.pallas import tpu as pltpu
from jax.sharding import PartitionSpec as P

HEAD = 64
HEADS = 12
LAYERS = 2
D = 768
FF = 3072
MESH = pl.DeviceIdType.MESH
BF16, F32 = jnp.bfloat16, jnp.float32

AXES = {"q": "yczx", "u": "yczx", "d": "czxy"}
STREAMS = ((slice(0, 16), "xyz"), (slice(16, 32), "yzx"), (slice(32, 48), "zxy"))
KINDS = "qud"
ALL = slice(None)
STEPS = (1, 3, 2)


def place():
    dp, core = lax.axis_index("dp"), lax.axis_index("fsdp")
    return {"z": dp // 16, "x": (dp // 4) % 4, "y": dp % 4, "c": core}


def device(at):
    return ((at["z"] * 4 + at["x"]) * 4 + at["y"], at["c"])


def moved(at, axis, step):
    size = 2 if axis == "c" else 4
    return {**at, axis: (at[axis] + step) % size}


class Links:
    def __init__(self, send_sems, recv_sems):
        self.send_sems, self.recv_sems, self.used, self.open = send_sems, recv_sems, 0, []

    def copy(self, src, dst, target, number):
        return pltpu.make_async_remote_copy(
            src_ref=src,
            dst_ref=dst,
            send_sem=self.send_sems.at[number],
            recv_sem=self.recv_sems.at[number],
            device_id=device(target),
            device_id_type=MESH,
        )

    def take(self, count):
        self.used += count
        return self.used - count

    def send(self, src, dst, target):
        copy = self.copy(src, dst, target, self.take(1))
        copy.start()
        self.open.append(copy)
        return copy

    def drain(self):
        for copy in self.open:
            copy.wait_send()
        self.open = []


def greet(me):
    partners = [moved(moved(me, "y", dy), "c", dc) for dy in range(4) for dc in range(2)][1:]
    partners += [moved(me, axis, step) for axis in "xz" for step in (1, 2, 3)]
    barrier = pltpu.get_barrier_semaphore()
    for partner in partners:
        pl.semaphore_signal(barrier, inc=1, device_id=device(partner), device_id_type=MESH)
    pl.semaphore_wait(barrier, len(partners))


T = 256
ROWS = 128
GAIN1, OFF1, BIAS_Q, BIAS_OUT, GAIN2, OFF2, BIAS_UP, BIAS_DOWN = 0, 1, 2, 5, 6, 7, 8, 12


def dot(a, b):
    return jnp.dot(a, b, preferred_element_type=F32)


def dot_nt(a, b):
    return lax.dot_general(a, b, (((1,), (1,)), ((), ())), preferred_element_type=F32)


def dot_tn(a, b):
    return lax.dot_general(a, b, (((0,), (0,)), ((), ())), preferred_element_type=F32)


def slab(ref, layer, index):
    return jnp.concatenate([ref[layer, index, core].reshape(D, 384) for core in range(2)], axis=1)


def chunk(ref, layer, index):
    return jnp.concatenate([ref[layer, core, index].reshape(D, 384) for core in range(2)], axis=1)


def put_slab(ref, layer, index, value):
    for core in range(2):
        ref[layer, index, core] = value[:, core * 384 : (core + 1) * 384].reshape(4, 4, 48, 384)


def put_chunk(ref, layer, index, value):
    for core in range(2):
        ref[layer, core, index] = value[:, core * 384 : (core + 1) * 384].reshape(4, 4, 48, 384)


def rows_of(index):
    return pl.ds(pl.multiple_of(index * ROWS, ROWS), ROWS)


def normal(x):
    center = x - jnp.mean(x, axis=-1, keepdims=True)
    scale = lax.rsqrt(jnp.mean(center * center, axis=-1, keepdims=True) + 1e-05)
    return center * scale, scale


def norm_into(x_ref, vec, gain, offset, out_ref):
    @pl.loop(0, T // ROWS)
    def _(index):
        rows = rows_of(index)
        hat, _ = normal(x_ref[rows, :].astype(F32))
        out_ref[rows, :] = (hat * vec[gain : gain + 1, :] + vec[offset : offset + 1, :]).astype(BF16)


def fold(value):
    return jnp.sum(value.reshape(ROWS // 8, 8, value.shape[1]), axis=0)


def total(value):
    return jnp.sum(value, axis=0, keepdims=True)


def norm_back(x_ref, grad_ref, vec, sums, gain, offset, top_ref, out_ref, bias=None, low_ref=None):
    zero = jnp.zeros((8, D), F32)

    def body(index, carry):
        sum_gain, sum_offset, sum_bias = carry
        rows = rows_of(index)
        hat, scale = normal(x_ref[rows, :].astype(F32))
        grad = grad_ref[rows, :]
        scaled = grad * vec[gain : gain + 1, :]
        inner = scaled - jnp.mean(scaled, axis=-1, keepdims=True)
        inner -= hat * jnp.mean(scaled * hat, axis=-1, keepdims=True)
        result = top_ref[rows, :] + scale * inner
        out_ref[rows, :] = result
        low = result.astype(BF16)
        if low_ref is not None:
            low_ref[rows, :] = low
        return sum_gain + fold(grad * hat), sum_offset + fold(grad), sum_bias + fold(low.astype(F32))

    sum_gain, sum_offset, sum_bias = lax.fori_loop(0, T // ROWS, body, (zero, zero, zero))
    sums[gain : gain + 1, :] = total(sum_gain)
    sums[offset : offset + 1, :] = total(sum_offset)
    if bias is not None:
        sums[bias : bias + 1, :] = total(sum_bias)


def gelu_parts(u):
    inner = 0.7978845608028654 * (u + 0.044715 * u * u * u)
    t = jnp.tanh(inner)
    slope = 0.7978845608028654 * (1.0 + 0.134145 * u * u)
    half = 0.5 * (1.0 + t)
    return u * half, half + 0.5 * u * (1.0 - t * t) * slope


def gelu(u):
    return 0.5 * u * (1.0 + jnp.tanh(0.7978845608028654 * (u + 0.044715 * u * u * u)))


def head_mask(which, scale=1.0):
    lane = lax.broadcasted_iota(jnp.int32, (1, 128), 1)
    return jnp.where(lane // HEAD == which, scale, 0.0).astype(BF16)


def lanes_of(pair):
    return pl.ds(pl.multiple_of(pair * 128, 128), 128)


def forward_qkv(layer, m):
    norm_into(m.x[layer], m.vec.at[layer], GAIN1, OFF1, m.h.at[layer])

    @pl.loop(0, 3)
    def _(part):
        bias = m.vec[layer, pl.ds(BIAS_Q + part, 1), :]
        m.qkv[layer, part] = (dot(m.h[layer], slab(m.wq, layer, part)) + bias).astype(BF16)


def forward_attention(layer, m):
    @pl.loop(0, HEADS // 2)
    def _(pair):
        lanes = lanes_of(pair)
        query, keys, values = (m.qkv[layer, part, :, lanes] for part in range(3))
        attended = jnp.zeros((T, 128), F32)
        for which in range(2):
            scores = dot_nt(query * head_mask(which, 0.125), keys)
            grown = jnp.exp(scores - jnp.max(scores, axis=-1, keepdims=True))
            probs = grown * (1.0 / jnp.sum(grown, axis=-1, keepdims=True))
            probs = probs.astype(BF16)
            m.probs[layer, 2 * pair + which] = probs
            attended += dot(probs, values * head_mask(which))
        m.o[layer, :, lanes] = attended.astype(BF16)


def forward_out(layer, m):
    m.mid[layer] = (
        m.x[layer][...].astype(F32)
        + dot(m.o[layer], slab(m.wq, layer, 3))
        + m.vec[layer, BIAS_OUT : BIAS_OUT + 1, :]
    )
    norm_into(m.mid.at[layer], m.vec.at[layer], GAIN2, OFF2, m.h2.at[layer])


def forward_up(layer, m):
    @pl.loop(0, 4)
    def _(index):
        bias = m.vec[layer, pl.ds(BIAS_UP + index, 1), :]
        u = dot(m.h2[layer], slab(m.wu, layer, index)) + bias
        m.u[layer, index] = u.astype(BF16)
        m.a[index] = gelu(u).astype(BF16)


def forward_down(layer, m):
    out = m.x[layer + 1]
    out[...] = m.mid[layer] + m.vec[layer, BIAS_DOWN : BIAS_DOWN + 1, :]

    @pl.loop(0, 4)
    def _(index):
        out[...] += dot(m.a[index], chunk(m.wd, layer, index))


def backward_ffn(layer, m, index):
    grad_active = dot_nt(m.gz[...], chunk(m.wd, layer, index))
    active, slope = gelu_parts(m.u[layer, index].astype(F32))
    pre = (grad_active * slope).astype(BF16)
    m.gu[...] = pre
    m.a[0] = active.astype(BF16)
    m.sums[layer, pl.ds(BIAS_UP + index, 1), :] = total(pre.astype(F32))
    m.gh[...] += dot_nt(m.gu[...], slab(m.wu, layer, index))
    put_chunk(m.wd, layer, index, dot_tn(m.a[0], m.gz[...]).astype(BF16))
    put_slab(m.wu, layer, index, dot_tn(m.h2[layer], m.gu[...]).astype(BF16))


def backward_mid(layer, m):
    norm_back(
        m.mid.at[layer], m.gh, m.vec.at[layer], m.sums.at[layer], GAIN2, OFF2, m.g, m.g, BIAS_OUT, m.gz
    )
    m.go[...] = dot_nt(m.gz[...], slab(m.wq, layer, 3)).astype(BF16)
    put_slab(m.wq, layer, 3, dot_tn(m.o[layer], m.gz[...]).astype(BF16))


def backward_attention(layer, m):
    @pl.loop(0, HEADS // 2)
    def _(pair):
        lanes = lanes_of(pair)
        query, keys, values = (m.qkv[layer, part, :, lanes] for part in range(3))
        grad = m.go[:, lanes]
        zero = jnp.zeros((T, 128), F32)
        grad_query, grad_keys, grad_values = zero, zero, zero
        for which in range(2):
            low = m.probs[layer, 2 * pair + which]
            probs = low.astype(F32)
            part = grad * head_mask(which)
            grad_probs = dot_nt(part, values)
            grad_values += dot_tn(low, part)
            row_dot = jnp.sum(grad_probs * probs, axis=-1, keepdims=True)
            grad_scores = (probs * (grad_probs - row_dot)).astype(BF16)
            grad_query += dot(grad_scores, keys * head_mask(which, 0.125))
            grad_keys += dot_tn(grad_scores, query * head_mask(which, 0.125))
        for part, value in enumerate((grad_query, grad_keys, grad_values)):
            m.gqkv[part, :, lanes] = value.astype(BF16)


def backward_qkv(layer, m, part):
    m.sums[layer, pl.ds(BIAS_Q + part, 1), :] = total(m.gqkv[part].astype(F32))
    m.gh[...] += dot_nt(m.gqkv[part], slab(m.wq, layer, part))
    put_slab(m.wq, layer, part, dot_tn(m.h[layer], m.gqkv[part]).astype(BF16))


def backward_in(layer, m, out_ref):
    norm_back(m.x[layer], m.gh, m.vec.at[layer], m.sums.at[layer], GAIN1, OFF1, m.g, out_ref)


def upstream(order_ref, remaining_ref, cot_ref, m):
    live = lax.broadcasted_iota(jnp.int32, (1, T), 1) >= T - remaining_ref

    def body(index, carry):
        rows = rows_of(index)
        spot = index * ROWS + lax.broadcasted_iota(jnp.int32, (ROWS, 1), 0)
        hit = jnp.where((order_ref == spot) & live, 1.0, 0.0)
        mask = jnp.max(hit, axis=-1, keepdims=True)
        grad = cot_ref[rows, :].astype(F32) * mask
        m.g[rows, :] = grad
        return carry

    lax.fori_loop(0, T // ROWS, body, 0)


def top(layer, m):
    def body(index, carry):
        rows = rows_of(index)
        low = m.g[rows, :].astype(BF16)
        m.gz[rows, :] = low
        return carry + fold(low.astype(F32))

    sums = lax.fori_loop(0, T // ROWS, body, jnp.zeros((8, D), F32))
    m.sums[layer, BIAS_DOWN : BIAS_DOWN + 1, :] = total(sums)
    m.gh[...] = jnp.zeros((T, D), F32)


class Gather:
    def __init__(self, kind, layer, m):
        self.kind, self.layer, self.m, self.handed = kind, layer, m, []

    def part(self, rows, at):
        index = tuple(at[axis] for axis in AXES[self.kind])
        return self.m.weights[self.kind].at[(self.layer, *index, rows, ALL)]

    def hand_over(self, rows, at):
        part = self.part(rows, at)
        self.handed.append(self.m.links.send(part, part, moved(self.m.me, "c", 1)))

    def out(self, rows, at, axis, steps):
        part, me = self.part(rows, at), self.m.me
        return {step: self.m.links.send(part, part, moved(me, axis, step)) for step in steps}

    def first(self):
        me = self.m.me
        self.copies = [self.out(rows, me, axes[0], STEPS) for rows, axes in STREAMS]

    def second(self):
        me, before = self.m.me, self.copies
        self.copies = []
        for (rows, axes), copies in zip(STREAMS, before):
            for step in STEPS:
                copies[step].wait_recv()
            self.copies.append(self.out(rows, {**me, axes[0]: ALL}, axes[1], STEPS))

    def third(self):
        me, before = self.m.me, self.copies
        self.copies = []
        for (rows, axes), copies in zip(STREAMS, before):
            for step in STEPS:
                copies[step].wait_recv()
            plane = {**me, axes[0]: ALL, axes[1]: ALL}
            self.copies.append(self.out(rows, plane, axes[2], (1, 3)))
            self.hand_over(rows, plane)

    def relay(self):
        me, self.halves = self.m.me, []
        for (rows, axes), copies in zip(STREAMS, self.copies):
            for step, start in ((1, 0), (3, 2)):
                copies[step].wait_recv()
                came = {**moved(me, axes[2], -step), axes[1]: ALL}
                half = self.part(rows, {**came, axes[0]: pl.ds(start, 2)})
                self.halves.append(self.m.links.send(half, half, moved(me, axes[2], step)))
                self.hand_over(rows, {**came, axes[0]: ALL})

    def finish(self):
        for copy in self.halves:
            copy.wait_recv()
        for rows, axes in STREAMS:
            self.hand_over(rows, {**moved(self.m.me, axes[2], 2), axes[0]: ALL, axes[1]: ALL})

    def arrive(self):
        for copy in self.handed:
            copy.wait_recv()


class Scatter:
    def __init__(self, kind, layer, m):
        self.kind, self.layer, self.m = kind, layer, m
        number = KINDS.index(kind)
        self.streams = [
            (
                rows,
                axes[::-1],
                m.first.at[number, stream],
                m.second.at[layer, number, stream],
                m.third.at[layer, number, stream],
                m.free.at[3 * number + stream],
            )
            for stream, (rows, axes) in enumerate(STREAMS)
        ]
        self.base = m.links.take(4)
        self.room, self.got = (m.free.at[9], m.got_d) if kind == "d" else (m.free.at[10], m.got_qu)

    def part(self, rows, at):
        index = tuple(at.get(axis, ALL) for axis in AXES[self.kind])
        return self.m.weights[self.kind].at[(self.layer, *index, rows, ALL)]

    def between(self, index):
        axis, sibling = ("z" if self.kind == "d" else "y"), moved(self.m.me, "c", 1)
        src = self.part(ALL, {axis: index, "c": sibling["c"]})
        return self.m.links.copy(src, self.got.at[index], sibling, self.base + index)

    def wait_room(self):
        pl.semaphore_wait(self.room, 1)

    def join(self, more):
        m, me = self.m, self.m.me
        axis, other = ("z", "x") if self.kind == "d" else ("y", "z")
        for index in range(4):
            copy = self.between(index)
            copy.wait_recv()
            m.links.open.append(copy)

        @pl.loop(0, 16)
        def _(spot):
            own = self.part(ALL, {axis: spot // 4, other: spot % 4, "c": me["c"]})
            own[...] += self.got[spot // 4, spot % 4]

        if more:
            pl.semaphore_signal(
                self.room, inc=1, device_id=device(moved(me, "c", 1)), device_id_type=MESH
            )
        self.copies = []
        for rows, axes, slots, _, _, free in self.streams:
            if self.layer == 0:
                pl.semaphore_wait(free, 3)
            for step in STEPS:
                target = moved(me, axes[0], step)
                src = self.part(rows, {"c": me["c"], axes[0]: target[axes[0]]})
                self.copies.append(m.links.send(src, slots.at[step - 1], target))

    def add(self, target, slots):
        value = target[...].astype(F32)
        for slot in slots:
            value += slot[...].astype(F32)
        return value

    def second(self):
        m, me, before = self.m, self.m.me, self.copies
        self.copies = []
        for number, (rows, axes, slots, later, _, free) in enumerate(self.streams):
            for copy in before[3 * number : 3 * number + 3]:
                copy.wait_recv()
            here = {"c": me["c"], axes[0]: me[axes[0]]}
            other = [axis for axis in AXES[self.kind] if axis not in here][0]

            @pl.loop(0, 4)
            def _(index):
                target = self.part(rows, {**here, other: index})
                total = self.add(target, [slots.at[step, index] for step in range(3)])
                target[...] = total.astype(BF16)

            if self.layer == 1:
                for step in STEPS:
                    peer = device(moved(me, axes[0], step))
                    pl.semaphore_signal(free, inc=1, device_id=peer, device_id_type=MESH)
            for step in STEPS:
                target = moved(me, axes[1], step)
                src = self.part(rows, {**here, axes[1]: target[axes[1]]})
                self.copies.append(m.links.send(src, later.at[step - 1], target))

    def third(self):
        m, me, before = self.m, self.m.me, self.copies
        self.copies = []
        for number, (rows, axes, _, later, last, _) in enumerate(self.streams):
            for copy in before[3 * number : 3 * number + 3]:
                copy.wait_recv()
            here = {"c": me["c"], axes[0]: me[axes[0]], axes[1]: me[axes[1]]}
            target = self.part(rows, here)
            target[...] = self.add(target, [later.at[step] for step in range(3)]).astype(BF16)
            for step in STEPS:
                target = moved(me, axes[2], step)
                src = self.part(rows, {**here, axes[2]: target[axes[2]]})
                self.copies.append(m.links.send(src, last.at[step - 1], target))

    def finish(self):
        for copy in self.copies:
            copy.wait_recv()
        for rows, _, _, _, last, _ in self.streams:
            total = self.add(self.part(rows, self.m.me), [last.at[step] for step in range(3)])
            self.m.totals[self.kind][self.layer, rows, :] = total


def spot_matrix(base, width):
    row = lax.broadcasted_iota(jnp.int32, (128, D), 0)
    lane = lax.broadcasted_iota(jnp.int32, (128, D), 1)
    return jnp.where((lane == base + row) & (row < width), 1.0, 0.0).astype(BF16)


def flag(condition):
    return jnp.where(condition, 1.0, 0.0).astype(F32)


NARROW_ROWS = (GAIN1, OFF1, BIAS_OUT, GAIN2, OFF2, BIAS_DOWN)


def spread_vectors(index, narrow, wide_qv, wide_up, stage, out):
    stage[...] = jnp.zeros(stage.shape, F32)
    for layer in range(LAYERS):
        rows = slice(layer, layer + 1)
        for row, vector in zip(NARROW_ROWS, narrow):
            stage[0, layer, row : row + 1, 0:6] = vector[rows, :].astype(F32)
        pair = wide_qv[rows, :].astype(F32)
        stage[1, layer, BIAS_Q : BIAS_Q + 1, 0:12] = pair * flag(index < 64)
        stage[1, layer, BIAS_Q + 2 : BIAS_Q + 3, 0:12] = pair * flag(index >= 64)
        for row in range(4):
            up = wide_up[rows, :].astype(F32) * flag(index // 32 == row)
            stage[2, layer, BIAS_UP + row : BIAS_UP + row + 1, 0:24] = up
    for layer in range(LAYERS):
        total = jnp.zeros((16, D), F32)
        for number, matrix in enumerate(spot_matrices(index)):
            total += dot(stage[number, layer].astype(BF16), matrix)
        out[layer] = total.astype(BF16)


def spot_matrices(index):
    return (
        spot_matrix(6 * index, 6), spot_matrix(12 * (index % 64), 12), spot_matrix(24 * (index % 32), 24)
    )


def own_entries(index, total, out):
    for layer in range(LAYERS):
        value = total[layer]
        high = value.astype(BF16)
        middle = (value - high.astype(F32)).astype(BF16)
        low = (value - high.astype(F32) - middle.astype(F32)).astype(BF16)
        found = []
        for matrix in spot_matrices(index):
            found.append(dot_nt(high, matrix) + (dot_nt(middle, matrix) + dot_nt(low, matrix)))
        for place_out, row in enumerate(NARROW_ROWS):
            out[place_out][layer : layer + 1, :] = found[0][row : row + 1, 0:6]
        pair = found[1][BIAS_Q : BIAS_Q + 1] * flag(index < 64)
        pair += found[1][BIAS_Q + 2 : BIAS_Q + 3] * flag(index >= 64)
        out[6][layer : layer + 1, :] = pair[:, 0:12]
        up = jnp.zeros((1, 128), F32)
        for row in range(4):
            up += found[2][BIAS_UP + row : BIAS_UP + row + 1] * flag(index // 32 == row)
        out[7][layer : layer + 1, :] = up[:, 0:24]


class VectorSum:
    ORDER = "xyzc"

    def __init__(self, m, state, recv):
        self.m, self.state, self.recv, self.number = m, state, recv, 0

    def begin(self):
        m, axis = self.m, self.ORDER[self.number]
        self.copies = [
            m.links.send(
                self.state.at[self.number],
                self.recv.at[3 * self.number + step - 1],
                moved(m.me, axis, step),
            )
            for step in range(1, 2 if axis == "c" else 4)
        ]

    def end(self):
        total = self.state[self.number].astype(F32)
        for copy in self.copies:
            copy.wait_recv()
        for step in range(len(self.copies)):
            total += self.recv[3 * self.number + step].astype(F32)
        self.number += 1
        if self.number < 4:
            self.state[self.number] = total.astype(self.state.dtype)
        return total

    def turn(self):
        self.end()
        self.begin()


def kernel(*refs):
    inputs, refs = refs[:16], refs[16:]
    outputs, refs = refs[:14], refs[14:]
    staged, refs = refs[:14], refs[14:]
    ready, refs = refs[:12], refs[12:]
    (
        wq, wu, wd, got_qu, got_d, first, second, third, sum_q, sum_u, sum_d,
        x0, x1, h, qkv, probs, o, mid, h2, u, tmp, g, gh, gz, cots, outs, vec, sums,
        low_state, low_recv, vec_state, vec_recv, stage,
        send_a, recv_a, send_d, recv_d, asm, send_f, recv_f, send_df, recv_df,
        send_sems, recv_sems, local_sems, free,
    ) = refs
    hidden, cot = inputs[:2]
    out, grad = outputs[:2]
    order, remaining, w_qkv, w_out, w_up, w_down, *vectors_in = staged
    gain1, off1, bias_qv, bias_out, gain2, off2, bias_up, bias_down = vectors_in
    g_qkv, g_out, g_up, g_down, *vectors_out = ready
    loads = []
    for number, (src, dst) in enumerate(zip(inputs[2:], staged)):
        loads.append(pltpu.make_async_copy(src, dst, local_sems.at[4 + number]))
        loads[-1].start()
    me = place()
    sibling = moved(me, "c", 1)
    mine = 2 * me["y"] + me["c"]
    index = ((me["z"] * 4 + me["x"]) * 4 + me["y"]) * 2 + me["c"]
    links = Links(send_sems, recv_sems)
    m = types.SimpleNamespace(
        me=me, links=links, weights={"q": wq, "u": wu, "d": wd}, wq=wq, wu=wu, wd=wd,
        got_qu=got_qu, got_d=got_d, free=free, totals={"q": sum_q, "u": sum_u, "d": sum_d},
        first=first, second=second, third=third,
        x=[x0, x1, g], h=h, qkv=qkv, probs=probs, o=o, mid=mid, h2=h2, u=u, a=tmp, g=g, gh=gh, gz=gz,
        gu=tmp.at[1], go=tmp.at[3], gqkv=tmp, vec=vec, sums=sums,
    )
    send_f[...] = jnp.zeros(send_f.shape, F32)
    for copy in loads:
        copy.wait()

    for owner in range(8):
        columns = slice(384 * (owner % 2), 384 * (owner % 2) + 384)
        for layer in range(LAYERS):
            for row in range(6):
                if owner < 6:
                    part = w_qkv[row, layer : layer + 1, 384 * owner : 384 * owner + 384]
                else:
                    part = w_out[row, layer : layer + 1, columns]
                send_f[owner, 8 * layer + row : 8 * layer + row + 1, :] = part.astype(F32)
                part = w_up[row, layer : layer + 1, 384 * owner : 384 * owner + 384]
                send_f[owner, 16 + 8 * layer + row : 17 + 8 * layer + row, :] = part.astype(F32)
    for owner in range(8):
        send_a[owner] = send_f[owner].astype(BF16)
    for half in range(2):
        for layer in range(LAYERS):
            part = w_down[layer, :, 384 * half : 384 * half + 384]
            send_df[half, 24 * layer : 24 * layer + 24, :] = part.astype(F32)
        send_d[half] = send_df[half].astype(BF16)
    narrow = (gain1, off1, bias_out, gain2, off2, bias_down)
    spread_vectors(index, narrow, bias_qv, bias_up, stage, low_state.at[0])

    greet(me)

    def group_sends(src, dst):
        copies = []
        for dy in range(4):
            for dc in range(2):
                if dy or dc:
                    target = moved(moved(me, "y", dy), "c", dc)
                    spot = src.at[2 * target["y"] + target["c"]]
                    copies.append(links.send(spot, dst.at[mine], target))
        return copies

    arrivals = group_sends(send_a, recv_a)
    arrivals.append(links.send(send_d.at[1 - me["c"]], recv_d.at[me["c"]], sibling))
    recv_a[mine] = send_a[mine]
    recv_d[me["c"]] = send_d[me["c"]]
    here = pl.ds(pl.multiple_of(128 * me["c"], 128), 128)
    there = pl.ds(pl.multiple_of(128 * (1 - me["c"]), 128), 128)
    halves = []
    for number, (src, dst) in enumerate(((hidden, x0), (cot, cots))):
        halves.append(links.send(src.at[1 - me["c"]], dst.at[here, :], sibling))
        copy = pltpu.make_async_copy(src.at[me["c"]], dst.at[here, :], local_sems.at[number])
        copy.start()
        halves.append(copy)
    for copy in arrivals:
        copy.wait_recv()
    gathers = [Gather(kind, layer, m) for layer in range(LAYERS) for kind in KINDS]
    own = (me["y"], me["c"], me["z"], me["x"])
    vectors = VectorSum(m, low_state, low_recv)
    for layer in range(LAYERS):
        for group, target in enumerate((wq, wu)):
            for source in range(8):
                rows = slice(16 * group + 8 * layer, 16 * group + 8 * layer + 6)
                asm[group, 6 * source : 6 * source + 6, :] = recv_a[source].astype(F32)[rows]
            target[(layer, *own)] = asm[group].astype(BF16)
            if layer == 0:
                gathers[group].first()
        for half in range(2):
            asm[2, 24 * half : 24 * half + 24, :] = recv_d[half].astype(F32)[
                24 * layer : 24 * layer + 24
            ]
        wd[layer, me["c"], me["z"], me["x"], me["y"]] = asm[2].astype(BF16)
        if layer == 0:
            vectors.begin()
            gathers[2].first()
    gathers[0].second()
    gathers[1].second()
    vectors.turn()
    gathers[0].third()
    gathers[2].second()
    gathers[3].first()
    gathers[1].third()
    vectors.turn()
    gathers[4].first()
    gathers[5].first()
    gathers[0].relay()
    vectors.turn()
    gathers[2].third()
    gathers[3].second()
    gathers[0].finish()
    gathers[4].second()
    vec[...] = vectors.end()
    gathers[1].relay()
    gathers[3].third()
    gathers[5].second()
    halves[0].wait_recv()
    halves[1].wait()
    gathers[0].arrive()

    forward_qkv(0, m)
    gathers[1].finish()
    gathers[2].relay()
    gathers[4].third()
    forward_attention(0, m)
    forward_out(0, m)
    gathers[2].finish()
    gathers[3].relay()
    gathers[5].third()
    gathers[1].arrive()
    forward_up(0, m)
    gathers[3].finish()
    gathers[4].relay()
    gathers[2].arrive()
    forward_down(0, m)
    gathers[4].finish()
    gathers[5].relay()
    gathers[3].arrive()
    forward_qkv(1, m)
    gathers[5].finish()
    forward_attention(1, m)
    forward_out(1, m)
    gathers[4].arrive()
    forward_up(1, m)
    gathers[5].arrive()
    forward_down(1, m)
    outs[...] = g[...].astype(BF16)
    links.drain()
    halves[2].wait_recv()
    halves[3].wait()

    def swap(src, dst, number):
        remote = links.send(src.at[there, :], dst.at[me["c"]], sibling)
        copy = pltpu.make_async_copy(src.at[here, :], dst.at[me["c"]], local_sems.at[number])
        copy.start()
        return remote, copy

    results = [swap(outs, out, 2)]
    upstream(order[pl.ds(me["c"], 1), :], remaining[me["c"]], cots, m)
    sums[...] = jnp.zeros(sums.shape, F32)
    scatters = {(kind, layer): Scatter(kind, layer, m) for layer in (1, 0) for kind in KINDS}

    def ffn(layer):
        ups, downs = scatters["u", layer], scatters["d", layer]
        if layer == 0:
            ups.wait_room()
            downs.wait_room()

        @pl.loop(0, 4)
        def _(part):
            backward_ffn(layer, m, part)
            ups.between(part).start()
            downs.between(part).start()

    def attention_grads(layer):
        scatter = scatters["q", layer]
        scatter.wait_room()
        scatter.between(3).start()
        m.gh[...] = jnp.zeros((T, D), F32)

        @pl.loop(0, 3)
        def _(part):
            backward_qkv(layer, m, part)
            scatter.between(part).start()

    top(1, m)
    ffn(1)
    backward_mid(1, m)
    scatters["u", 1].join(True)
    scatters["d", 1].join(True)
    backward_attention(1, m)
    attention_grads(1)
    backward_in(1, m, g)
    top(0, m)
    scatters["q", 1].join(True)
    ffn(0)
    scatters["u", 1].second()
    scatters["d", 1].second()
    backward_mid(0, m)
    scatters["q", 1].second()
    scatters["u", 0].join(True)
    scatters["d", 0].join(False)
    backward_attention(0, m)
    scatters["u", 1].third()
    scatters["d", 1].third()
    attention_grads(0)
    scatters["q", 1].third()
    backward_in(0, m, g)
    results.append(swap(g, grad, 3))
    vec_state[0] = sums[...]
    scatters["q", 0].join(False)
    for kind in "udq":
        scatters[kind, 1].finish()
    vectors = VectorSum(m, vec_state, vec_recv)
    vectors.begin()
    scatters["u", 0].second()
    scatters["d", 0].second()
    vectors.turn()
    scatters["q", 0].second()
    scatters["u", 0].third()
    scatters["d", 0].third()
    vectors.turn()
    scatters["q", 0].third()
    vectors.turn()
    for kind in "udq":
        scatters[kind, 0].finish()

    for layer in range(LAYERS):
        for owner in range(8):
            for group, total in enumerate((sum_q, sum_u)):
                start = 16 * group + 8 * layer
                send_f[owner, start : start + 6, :] = total[layer, 6 * owner : 6 * owner + 6, :]
        for owner in range(2):
            send_df[owner, 24 * layer : 24 * layer + 24, :] = sum_d[
                layer, 24 * owner : 24 * owner + 24, :
            ]
    last = group_sends(send_f, recv_f)
    last.append(links.send(send_df.at[1 - me["c"]], recv_df.at[me["c"]], sibling))
    recv_f[mine] = send_f[mine]
    recv_df[me["c"]] = send_df[me["c"]]
    sums[...] = vectors.end()
    own_entries(index, sums, vectors_out)
    for copy in last:
        copy.wait_recv()
    for owner in range(8):
        columns = slice(384 * (owner % 2), 384 * (owner % 2) + 384)
        for layer in range(LAYERS):
            for row in range(6):
                spot = 8 * layer + row
                value = recv_f[owner, spot : spot + 1, :]
                if owner < 6:
                    g_qkv[row, layer : layer + 1, 384 * owner : 384 * owner + 384] = value
                else:
                    g_out[row, layer : layer + 1, columns] = value
                value = recv_f[owner, 16 + spot : 17 + spot, :]
                g_up[row, layer : layer + 1, 384 * owner : 384 * owner + 384] = value
    for layer in range(LAYERS):
        for half in range(2):
            g_down[layer, :, 384 * half : 384 * half + 384] = recv_df[
                half, 24 * layer : 24 * layer + 24, :
            ]
    stores = []
    for number, (src, dst) in enumerate(zip(ready, outputs[2:])):
        stores.append(pltpu.make_async_copy(src, dst, local_sems.at[4 + number]))
        stores[-1].start()
    for remote, copy in results:
        remote.wait_recv()
        copy.wait()
    links.drain()
    for copy in stores:
        copy.wait()


def deliver_kernel(*refs):
    count = len(refs) // 3
    sources, results, held, sems = refs[:count], refs[count : 2 * count], refs[2 * count : -1], refs[-1]
    loads = [
        pltpu.make_async_copy(src, dst, sems.at[0, number])
        for number, (src, dst) in enumerate(zip(sources, held))
    ]
    stores = [
        pltpu.make_async_copy(src, dst, sems.at[1, number])
        for number, (src, dst) in enumerate(zip(held, results))
    ]
    for copy in loads:
        copy.start()
    for load, store in zip(loads, stores):
        load.wait()
        store.start()
    for copy in stores:
        copy.wait()


def deliver(values):
    hbm = pl.BlockSpec(memory_space=pl.ANY)
    return pl.pallas_call(
        deliver_kernel,
        out_shape=[jax.ShapeDtypeStruct(value.shape, value.dtype) for value in values],
        in_specs=[hbm] * len(values),
        out_specs=[hbm] * len(values),
        scratch_shapes=[
            *[pltpu.VMEM(value.shape, value.dtype) for value in values],
            pltpu.SemaphoreType.DMA((2, len(values))),
        ],
        name="deliver",
    )(*values)


def shards(
    hidden, cotangent, remaining, order,
    norm1_gain, norm1_bias, w_qkv, bias_qv, w_out, bias_out,
    norm2_gain, norm2_bias, w_up, bias_up, w_down, bias_down,
):
    half = hidden.shape[1]
    hbm = pl.BlockSpec(memory_space=pl.ANY)
    swapped = [jnp.transpose(weight, (1, 0, 2)) for weight in (w_qkv, w_out, w_up)]
    wide, deep = (LAYERS, 4, 2, 4, 4, 48, 384), (LAYERS, 2, 4, 4, 4, 48, 384)
    inputs = (
        hidden, cotangent, order, remaining, *swapped, w_down,
        norm1_gain, norm1_bias, bias_qv, bias_out, norm2_gain, norm2_bias, bias_up, bias_down,
    )
    results = [((2, half, D), BF16)] + [
        (shape, F32)
        for shape in (
            (2, half, D), (6, LAYERS, 3 * D), (6, LAYERS, D), (6, LAYERS, FF), (LAYERS, 24, D),
            *[(LAYERS, 6)] * 6, (LAYERS, 12), (LAYERS, 24),
        )
    ]
    staged = [pltpu.VMEM(value.shape, value.dtype) for value in inputs[2:]]
    staged[1] = pltpu.SMEM(remaining.shape, remaining.dtype)
    values = pl.pallas_call(
        kernel,
        out_shape=[jax.ShapeDtypeStruct(*result) for result in results],
        in_specs=[hbm] * len(inputs),
        out_specs=[hbm] * len(results),
        scratch_shapes=[
            *staged,
            *[pltpu.VMEM(*result) for result in results[2:]],
            pltpu.VMEM(wide, BF16),
            pltpu.VMEM(wide, BF16),
            pltpu.VMEM(deep, BF16),
            pltpu.VMEM((4, 4, 4, 48, 384), BF16),
            pltpu.VMEM((4, 4, 4, 48, 384), BF16),
            pltpu.VMEM((3, 3, 3, 4, 4, 16, 384), BF16),
            pltpu.VMEM((LAYERS, 3, 3, 3, 4, 16, 384), BF16),
            pltpu.VMEM((LAYERS, 3, 3, 3, 16, 384), BF16),
            *[pltpu.VMEM((LAYERS, 48, 384), F32) for _ in range(3)],
            pltpu.VMEM((T, D), BF16),
            pltpu.VMEM((T, D), F32),
            pltpu.VMEM((LAYERS, T, D), BF16),
            pltpu.VMEM((LAYERS, 3, T, D), BF16),
            pltpu.VMEM((LAYERS, HEADS, T, T), BF16),
            pltpu.VMEM((LAYERS, T, D), BF16),
            pltpu.VMEM((LAYERS, T, D), F32),
            pltpu.VMEM((LAYERS, T, D), BF16),
            pltpu.VMEM((LAYERS, 4, T, D), BF16),
            pltpu.VMEM((4, T, D), BF16),
            pltpu.VMEM((T, D), F32),
            pltpu.VMEM((T, D), F32),
            pltpu.VMEM((T, D), BF16),
            pltpu.VMEM((T, D), BF16),
            pltpu.VMEM((T, D), BF16),
            pltpu.VMEM((LAYERS, 16, D), F32),
            pltpu.VMEM((LAYERS, 16, D), F32),
            pltpu.VMEM((4, LAYERS, 16, D), BF16),
            pltpu.VMEM((10, LAYERS, 16, D), BF16),
            pltpu.VMEM((4, LAYERS, 16, D), F32),
            pltpu.VMEM((10, LAYERS, 16, D), F32),
            pltpu.VMEM((3, LAYERS, 16, 128), F32),
            pltpu.VMEM((8, 32, 384), BF16),
            pltpu.VMEM((8, 32, 384), BF16),
            pltpu.VMEM((2, 48, 384), BF16),
            pltpu.VMEM((2, 48, 384), BF16),
            pltpu.VMEM((3, 48, 384), F32),
            pltpu.VMEM((8, 32, 384), F32),
            pltpu.VMEM((8, 32, 384), F32),
            pltpu.VMEM((2, 48, 384), F32),
            pltpu.VMEM((2, 48, 384), F32),
            pltpu.SemaphoreType.DMA((600,)),
            pltpu.SemaphoreType.DMA((600,)),
            pltpu.SemaphoreType.DMA((18,)),
            pltpu.SemaphoreType.REGULAR((11,)),
        ],
        compiler_params=pltpu.CompilerParams(
            collective_id=0, has_side_effects=True, vmem_limit_bytes=(63 << 20) + (1 << 19)
        ),
        name="layers",
    )(*inputs)
    values = deliver(values)
    out, grad, g_qkv, g_out, g_up, g_down, gain1, off1, b_out, gain2, off2, b_down, b_qv, b_up = values
    g_qkv, g_out, g_up = (jnp.transpose(part, (1, 0, 2)) for part in (g_qkv, g_out, g_up))
    return out, grad, gain1, off1, g_qkv, b_qv, g_out, b_out, gain2, off2, g_up, b_up, g_down, b_down


def solution(mesh):
    tokens, rows = P("dp", "fsdp", None), P(None, ("dp", "fsdp"), None)
    vector = P(None, ("dp", "fsdp"))
    weights = (
        vector, vector, rows, vector, rows, vector, vector, vector, rows, vector, rows, vector
    )
    return jax.shard_map(
        shards,
        mesh=mesh,
        in_specs=(tokens, tokens, P("dp"), P("dp", None), *weights),
        out_specs=(tokens, tokens, *weights),
        check_vma=False,
    )
```

```python
import types

import jax
import jax.numpy as jnp
from jax import lax
from jax.experimental import pallas as pl
from jax.experimental.pallas import tpu as pltpu
from jax.sharding import PartitionSpec as P

HEAD = 64
HEADS = 12
LAYERS = 2
D = 768
FF = 3072
MESH = pl.DeviceIdType.MESH
BF16, F32 = jnp.bfloat16, jnp.float32

AXES = {"q": "yczx", "u": "yczx", "d": "czxy"}
STREAMS = ((slice(0, 16), "xyz"), (slice(16, 32), "yzx"), (slice(32, 48), "zxy"))
KINDS = "qud"
ALL = slice(None)
STEPS = (1, 3, 2)


def place():
    dp, core = lax.axis_index("dp"), lax.axis_index("fsdp")
    return {"z": dp // 16, "x": (dp // 4) % 4, "y": dp % 4, "c": core}


def device(at):
    return ((at["z"] * 4 + at["x"]) * 4 + at["y"], at["c"])


def moved(at, axis, step):
    size = 2 if axis == "c" else 4
    return {**at, axis: (at[axis] + step) % size}


class Batch:
    def __init__(self, links, whole):
        self.links, self.whole = links, whole
        self.number = links.batches
        links.batches += 1
        links.open.append(self)

    def copy(self, src, dst, target):
        return pltpu.make_async_remote_copy(
            src_ref=src,
            dst_ref=dst,
            send_sem=self.links.send_sems.at[self.number],
            recv_sem=self.links.recv_sems.at[self.number],
            device_id=device(target),
            device_id_type=MESH,
        )

    def send(self, src, dst, target):
        self.copy(src, dst, target).start()

    def all(self):
        return self.copy(self.whole, self.whole, self.links.sibling)

    def wait(self):
        self.all().wait_recv()


class Links:
    def __init__(self, me, send_sems, recv_sems):
        self.sibling = moved(me, "c", 1)
        self.send_sems, self.recv_sems, self.open, self.batches = send_sems, recv_sems, [], 0

    def send(self, src, dst, target):
        batch = Batch(self, src)
        batch.send(src, dst, target)
        return batch

    def drain(self):
        for batch in self.open:
            batch.all().wait_send()
        self.open = []


def greet(me):
    partners = [moved(moved(me, "y", dy), "c", dc) for dy in range(4) for dc in range(2)][1:]
    partners += [moved(me, axis, step) for axis in "xz" for step in (1, 2, 3)]
    barrier = pltpu.get_barrier_semaphore()
    for partner in partners:
        pl.semaphore_signal(barrier, inc=1, device_id=device(partner), device_id_type=MESH)
    pl.semaphore_wait(barrier, len(partners))


T = 256
ROWS = 128
GAIN1, OFF1, BIAS_Q, BIAS_OUT, GAIN2, OFF2, BIAS_UP, BIAS_DOWN = 0, 1, 2, 5, 6, 7, 8, 12


def dot(a, b):
    return jnp.dot(a, b, preferred_element_type=F32)


def dot_nt(a, b):
    return lax.dot_general(a, b, (((1,), (1,)), ((), ())), preferred_element_type=F32)


def dot_tn(a, b):
    return lax.dot_general(a, b, (((0,), (0,)), ((), ())), preferred_element_type=F32)


def slab(ref, layer, index):
    return jnp.concatenate([ref[layer, index, core].reshape(D, 384) for core in range(2)], axis=1)


def chunk(ref, layer, index):
    return jnp.concatenate([ref[layer, core, index].reshape(D, 384) for core in range(2)], axis=1)


def put_slab(ref, layer, index, value):
    for core in range(2):
        ref[layer, index, core] = value[:, core * 384 : (core + 1) * 384].reshape(4, 4, 48, 384)


def put_chunk(ref, layer, index, value):
    for core in range(2):
        ref[layer, core, index] = value[:, core * 384 : (core + 1) * 384].reshape(4, 4, 48, 384)


def rows_of(index):
    return pl.ds(pl.multiple_of(index * ROWS, ROWS), ROWS)


def normal(x):
    center = x - jnp.mean(x, axis=-1, keepdims=True)
    scale = lax.rsqrt(jnp.mean(center * center, axis=-1, keepdims=True) + 1e-05)
    return center * scale, scale


def norm_into(x_ref, vec, gain, offset, out_ref):
    @pl.loop(0, T // ROWS)
    def _(index):
        rows = rows_of(index)
        hat, _ = normal(x_ref[rows, :].astype(F32))
        out_ref[rows, :] = (hat * vec[gain : gain + 1, :] + vec[offset : offset + 1, :]).astype(BF16)


def fold(value):
    return jnp.sum(value.reshape(ROWS // 8, 8, value.shape[1]), axis=0)


def total(value):
    return jnp.sum(value, axis=0, keepdims=True)


def norm_back(x_ref, grad_ref, vec, sums, gain, offset, top_ref, out_ref, bias=None, low_ref=None):
    zero = jnp.zeros((8, D), F32)

    def body(index, carry):
        sum_gain, sum_offset, sum_bias = carry
        rows = rows_of(index)
        hat, scale = normal(x_ref[rows, :].astype(F32))
        grad = grad_ref[rows, :]
        scaled = grad * vec[gain : gain + 1, :]
        inner = scaled - jnp.mean(scaled, axis=-1, keepdims=True)
        inner -= hat * jnp.mean(scaled * hat, axis=-1, keepdims=True)
        result = top_ref[rows, :] + scale * inner
        out_ref[rows, :] = result
        low = result.astype(BF16)
        if low_ref is not None:
            low_ref[rows, :] = low
        return sum_gain + fold(grad * hat), sum_offset + fold(grad), sum_bias + fold(low.astype(F32))

    sum_gain, sum_offset, sum_bias = lax.fori_loop(0, T // ROWS, body, (zero, zero, zero))
    sums[gain : gain + 1, :] = total(sum_gain)
    sums[offset : offset + 1, :] = total(sum_offset)
    if bias is not None:
        sums[bias : bias + 1, :] = total(sum_bias)


def gelu_parts(u):
    inner = 0.7978845608028654 * (u + 0.044715 * u * u * u)
    t = jnp.tanh(inner)
    slope = 0.7978845608028654 * (1.0 + 0.134145 * u * u)
    half = 0.5 * (1.0 + t)
    return u * half, half + 0.5 * u * (1.0 - t * t) * slope


def gelu(u):
    return 0.5 * u * (1.0 + jnp.tanh(0.7978845608028654 * (u + 0.044715 * u * u * u)))


def head_mask(which, scale=1.0):
    lane = lax.broadcasted_iota(jnp.int32, (1, 128), 1)
    return jnp.where(lane // HEAD == which, scale, 0.0).astype(BF16)


def lanes_of(pair):
    return pl.ds(pl.multiple_of(pair * 128, 128), 128)


def forward_qkv(layer, m):
    norm_into(m.x[layer], m.vec.at[layer], GAIN1, OFF1, m.h.at[layer])

    @pl.loop(0, 3)
    def _(part):
        bias = m.vec[layer, pl.ds(BIAS_Q + part, 1), :]
        m.qkv[layer, part] = (dot(m.h[layer], slab(m.wq, layer, part)) + bias).astype(BF16)


def forward_attention(layer, m):
    @pl.loop(0, HEADS // 2)
    def _(pair):
        lanes = lanes_of(pair)
        query, keys, values = (m.qkv[layer, part, :, lanes] for part in range(3))
        attended = jnp.zeros((T, 128), F32)
        for which in range(2):
            scores = dot_nt(query * head_mask(which, 0.125), keys)
            grown = jnp.exp(scores - jnp.max(scores, axis=-1, keepdims=True))
            probs = grown * (1.0 / jnp.sum(grown, axis=-1, keepdims=True))
            probs = probs.astype(BF16)
            m.probs[layer, 2 * pair + which] = probs
            attended += dot(probs, values * head_mask(which))
        m.o[layer, :, lanes] = attended.astype(BF16)


def forward_out(layer, m):
    m.mid[layer] = (
        m.x[layer][...].astype(F32)
        + dot(m.o[layer], slab(m.wq, layer, 3))
        + m.vec[layer, BIAS_OUT : BIAS_OUT + 1, :]
    )
    norm_into(m.mid.at[layer], m.vec.at[layer], GAIN2, OFF2, m.h2.at[layer])


def forward_up(layer, m):
    @pl.loop(0, 4)
    def _(index):
        bias = m.vec[layer, pl.ds(BIAS_UP + index, 1), :]
        u = dot(m.h2[layer], slab(m.wu, layer, index)) + bias
        m.u[layer, index] = u.astype(BF16)
        m.a[index] = gelu(u).astype(BF16)


def forward_down(layer, m):
    out = m.x[layer + 1]
    out[...] = m.mid[layer] + m.vec[layer, BIAS_DOWN : BIAS_DOWN + 1, :]

    @pl.loop(0, 4)
    def _(index):
        out[...] += dot(m.a[index], chunk(m.wd, layer, index))


def backward_ffn(layer, m, index):
    grad_active = dot_nt(m.gz[...], chunk(m.wd, layer, index))
    active, slope = gelu_parts(m.u[layer, index].astype(F32))
    pre = (grad_active * slope).astype(BF16)
    m.gu[...] = pre
    m.a[0] = active.astype(BF16)
    m.sums[layer, pl.ds(BIAS_UP + index, 1), :] = total(pre.astype(F32))
    m.gh[...] += dot_nt(m.gu[...], slab(m.wu, layer, index))
    put_chunk(m.wd, layer, index, dot_tn(m.a[0], m.gz[...]).astype(BF16))
    put_slab(m.wu, layer, index, dot_tn(m.h2[layer], m.gu[...]).astype(BF16))


def backward_mid(layer, m):
    norm_back(
        m.mid.at[layer], m.gh, m.vec.at[layer], m.sums.at[layer], GAIN2, OFF2, m.g, m.g, BIAS_OUT, m.gz
    )
    m.go[...] = dot_nt(m.gz[...], slab(m.wq, layer, 3)).astype(BF16)
    put_slab(m.wq, layer, 3, dot_tn(m.o[layer], m.gz[...]).astype(BF16))


def backward_attention(layer, m):
    @pl.loop(0, HEADS // 2)
    def _(pair):
        lanes = lanes_of(pair)
        query, keys, values = (m.qkv[layer, part, :, lanes] for part in range(3))
        grad = m.go[:, lanes]
        zero = jnp.zeros((T, 128), F32)
        grad_query, grad_keys, grad_values = zero, zero, zero
        for which in range(2):
            low = m.probs[layer, 2 * pair + which]
            probs = low.astype(F32)
            part = grad * head_mask(which)
            grad_probs = dot_nt(part, values)
            grad_values += dot_tn(low, part)
            row_dot = jnp.sum(grad_probs * probs, axis=-1, keepdims=True)
            grad_scores = (probs * (grad_probs - row_dot)).astype(BF16)
            grad_query += dot(grad_scores, keys * head_mask(which, 0.125))
            grad_keys += dot_tn(grad_scores, query * head_mask(which, 0.125))
        for part, value in enumerate((grad_query, grad_keys, grad_values)):
            m.gqkv[part, :, lanes] = value.astype(BF16)


def backward_qkv(layer, m, part):
    m.sums[layer, pl.ds(BIAS_Q + part, 1), :] = total(m.gqkv[part].astype(F32))
    m.gh[...] += dot_nt(m.gqkv[part], slab(m.wq, layer, part))
    put_slab(m.wq, layer, part, dot_tn(m.h[layer], m.gqkv[part]).astype(BF16))


def backward_in(layer, m, out_ref):
    norm_back(m.x[layer], m.gh, m.vec.at[layer], m.sums.at[layer], GAIN1, OFF1, m.g, out_ref)


def upstream(order_ref, remaining_ref, cot_ref, m):
    live = lax.broadcasted_iota(jnp.int32, (1, T), 1) >= T - remaining_ref

    def body(index, carry):
        rows = rows_of(index)
        spot = index * ROWS + lax.broadcasted_iota(jnp.int32, (ROWS, 1), 0)
        hit = jnp.where((order_ref == spot) & live, 1.0, 0.0)
        mask = jnp.max(hit, axis=-1, keepdims=True)
        grad = cot_ref[rows, :].astype(F32) * mask
        m.g[rows, :] = grad
        return carry

    lax.fori_loop(0, T // ROWS, body, 0)


def top(layer, m):
    def body(index, carry):
        rows = rows_of(index)
        low = m.g[rows, :].astype(BF16)
        m.gz[rows, :] = low
        return carry + fold(low.astype(F32))

    sums = lax.fori_loop(0, T // ROWS, body, jnp.zeros((8, D), F32))
    m.sums[layer, BIAS_DOWN : BIAS_DOWN + 1, :] = total(sums)
    m.gh[...] = jnp.zeros((T, D), F32)


class Gather:
    def __init__(self, kind, layer, m):
        self.kind, self.layer, self.m = kind, layer, m
        sizes = m.wq.at[0]
        self.handed = Batch(m.links, sizes.at[:, 0])
        self.one = Batch(m.links, sizes.at[0, 0, 0, pl.ds(0, 3)])
        self.two = Batch(m.links, sizes.at[0, 0, pl.ds(0, 3)])
        self.three = Batch(m.links, sizes.at[pl.ds(0, 2), 0])
        self.halves = Batch(m.links, sizes.at[0, 0])

    def part(self, rows, at):
        index = tuple(at[axis] for axis in AXES[self.kind])
        return self.m.weights[self.kind].at[(self.layer, *index, rows, ALL)]

    def hand_over(self, rows, at):
        part = self.part(rows, at)
        self.handed.send(part, part, self.m.links.sibling)

    def out(self, batch, rows, at, axis, steps):
        part = self.part(rows, at)
        for step in steps:
            batch.send(part, part, moved(self.m.me, axis, step))

    def first(self):
        for rows, axes in STREAMS:
            self.out(self.one, rows, self.m.me, axes[0], STEPS)

    def second(self):
        self.one.wait()
        for rows, axes in STREAMS:
            self.out(self.two, rows, {**self.m.me, axes[0]: ALL}, axes[1], STEPS)

    def third(self):
        self.two.wait()
        planes = [
            (rows, axes, {**self.m.me, axes[0]: ALL, axes[1]: ALL}) for rows, axes in STREAMS
        ]
        for rows, axes, plane in planes:
            self.out(self.three, rows, plane, axes[2], (1, 3))
        for rows, axes, plane in planes:
            self.hand_over(rows, plane)

    def relay(self):
        self.three.wait()
        came = [
            (rows, axes, step, {**moved(self.m.me, axes[2], -step), axes[0]: ALL, axes[1]: ALL})
            for rows, axes in STREAMS
            for step in (1, 3)
        ]
        for rows, axes, step, at in came:
            self.out(self.halves, rows, {**at, axes[0]: pl.ds(step - 1, 2)}, axes[2], (step,))
        for rows, axes, step, at in came:
            self.hand_over(rows, at)

    def finish(self):
        self.halves.wait()
        for rows, axes in STREAMS:
            self.hand_over(rows, {**moved(self.m.me, axes[2], 2), axes[0]: ALL, axes[1]: ALL})

    def arrive(self):
        self.handed.wait()


class Scatter:
    def __init__(self, kind, layer, m):
        self.kind, self.layer, self.m = kind, layer, m
        self.slow = "z" if kind == "d" else "y"
        number = KINDS.index(kind)
        self.streams = []
        for stream, (rows, axes) in enumerate(STREAMS):
            others = [axis for axis in AXES[kind] if axis not in ("c", axes[2])]
            slots = m.first.at[number, stream]
            later = (m.second.at[layer, number, stream], m.third.at[layer, number, stream])
            free = m.free.at[3 * number + stream]
            self.streams.append((rows, axes[::-1], others, slots, *later, free))
        sizes = m.wq.at[0]
        self.shared = [Batch(m.links, sizes.at[pl.ds(0, 2), 0]) for _ in range(2)]
        self.passing, self.direct, self.passed = (Batch(m.links, sizes.at[0, 0]) for _ in range(3))
        self.two = Batch(m.links, sizes.at[0, 0, pl.ds(0, 3)])
        self.one = Batch(m.links, sizes.at[0, 0, 0, pl.ds(0, 3)])
        self.room, self.got = (m.free.at[9], m.got_d) if kind == "d" else (m.free.at[10], m.got_qu)

    def part(self, rows, at):
        index = tuple(at.get(axis, ALL) for axis in AXES[self.kind])
        return self.m.weights[self.kind].at[(self.layer, *index, rows, ALL)]

    def share(self, index, half):
        sibling = self.m.links.sibling
        src = self.part(ALL, {self.slow: index, "c": sibling["c"]})
        self.shared[half].send(src, self.got.at[index], sibling)

    def wait_room(self):
        pl.semaphore_wait(self.room, 1)

    def give_room(self):
        sibling = device(self.m.links.sibling)
        pl.semaphore_signal(self.room, inc=1, device_id=sibling, device_id_type=MESH)

    def join(self, half):
        m, me = self.m, self.m.me
        other = "x" if self.kind == "d" else "z"
        self.shared[half].wait()

        @pl.loop(8 * half, 8 * half + 8)
        def _(spot):
            own = self.part(ALL, {self.slow: spot // 4, other: spot % 4, "c": me["c"]})
            own[...] += self.got[spot // 4, spot % 4]

        for rows, axes, others, slots, _, _, free in self.streams:
            split = others[0] == self.slow
            if self.layer == 0 and half == (0 if split else 1):
                pl.semaphore_wait(free, 2)
            for now in (half,) if split else (0, 1) if half else ():
                self.leave(rows, axes[0], others[0], slots, now)

    def leave(self, rows, axis, split, slots, half):
        me, step, back = self.m.me, 1 + 2 * half, 3 - 2 * half
        halves = pl.ds(2 * half, 2)
        spot = {"c": me["c"], split: halves}
        src = self.part(rows, {**spot, axis: moved(me, axis, 2)[axis]})
        self.passing.send(src, slots.at[2, halves], moved(me, axis, step))
        target = moved(me, axis, back)
        src = self.part(rows, {**spot, axis: target[axis]})
        self.direct.send(src, slots.at[1 - half, halves], target)

    def relay(self):
        me = self.m.me
        self.passing.wait()
        for rows, axes, others, slots, _, _, _ in self.streams:
            for half in range(2):
                target = moved(me, axes[0], 1 + 2 * half)
                spot = {"c": me["c"], axes[0]: target[axes[0]]}
                for index in (2 * half, 2 * half + 1):
                    own = self.part(rows, {**spot, others[0]: index})
                    own[...] += slots[2, index]
                halves = pl.ds(2 * half, 2)
                src = self.part(rows, {**spot, others[0]: halves})
                self.passed.send(src, slots.at[half, halves], target)

    def add(self, target, slots):
        value = target[...].astype(F32)
        for slot in slots:
            value += slot[...].astype(F32)
        return value

    def second(self):
        m, me = self.m, self.m.me
        self.direct.wait()
        self.passed.wait()
        for rows, axes, others, slots, later, _, free in self.streams:
            here = {"c": me["c"], axes[0]: me[axes[0]]}

            @pl.loop(0, 4)
            def _(index):
                target = self.part(rows, {**here, others[0]: index})
                total = self.add(target, [slots.at[side, index] for side in range(2)])
                target[...] = total.astype(BF16)

            if self.layer == 1:
                for step in (1, 3):
                    peer = device(moved(me, axes[0], step))
                    pl.semaphore_signal(free, inc=1, device_id=peer, device_id_type=MESH)
            for step in STEPS:
                target = moved(me, axes[1], step)
                src = self.part(rows, {**here, axes[1]: target[axes[1]]})
                self.two.send(src, later.at[step - 1], target)

    def third(self):
        m, me = self.m, self.m.me
        self.two.wait()
        for rows, axes, _, _, later, last, _ in self.streams:
            here = {"c": me["c"], axes[0]: me[axes[0]], axes[1]: me[axes[1]]}
            target = self.part(rows, here)
            target[...] = self.add(target, [later.at[step] for step in range(3)]).astype(BF16)
            for step in STEPS:
                target = moved(me, axes[2], step)
                src = self.part(rows, {**here, axes[2]: target[axes[2]]})
                self.one.send(src, last.at[step - 1], target)

    def finish(self):
        self.one.wait()
        for rows, _, _, _, _, last, _ in self.streams:
            total = self.add(self.part(rows, self.m.me), [last.at[step] for step in range(3)])
            self.m.totals[self.kind][self.layer, rows, :] = total


def spot_matrix(base, width):
    row = lax.broadcasted_iota(jnp.int32, (128, D), 0)
    lane = lax.broadcasted_iota(jnp.int32, (128, D), 1)
    return jnp.where((lane == base + row) & (row < width), 1.0, 0.0).astype(BF16)


def flag(condition):
    return jnp.where(condition, 1.0, 0.0).astype(F32)


NARROW_ROWS = (GAIN1, OFF1, BIAS_OUT, GAIN2, OFF2, BIAS_DOWN)


def spread_vectors(index, narrow, wide_qv, wide_up, stage, out):
    stage[...] = jnp.zeros(stage.shape, F32)
    for layer in range(LAYERS):
        rows = slice(layer, layer + 1)
        for row, vector in zip(NARROW_ROWS, narrow):
            stage[0, layer, row : row + 1, 0:6] = vector[rows, :].astype(F32)
        pair = wide_qv[rows, :].astype(F32)
        stage[1, layer, BIAS_Q : BIAS_Q + 1, 0:12] = pair * flag(index < 64)
        stage[1, layer, BIAS_Q + 2 : BIAS_Q + 3, 0:12] = pair * flag(index >= 64)
        for row in range(4):
            up = wide_up[rows, :].astype(F32) * flag(index // 32 == row)
            stage[2, layer, BIAS_UP + row : BIAS_UP + row + 1, 0:24] = up
    for layer in range(LAYERS):
        total = jnp.zeros((16, D), F32)
        for number, matrix in enumerate(spot_matrices(index)):
            total += dot(stage[number, layer].astype(BF16), matrix)
        out[layer] = total.astype(BF16)


def spot_matrices(index):
    return (
        spot_matrix(6 * index, 6), spot_matrix(12 * (index % 64), 12), spot_matrix(24 * (index % 32), 24)
    )


def own_entries(index, total, out):
    for layer in range(LAYERS):
        value = total[layer]
        high = value.astype(BF16)
        middle = (value - high.astype(F32)).astype(BF16)
        low = (value - high.astype(F32) - middle.astype(F32)).astype(BF16)
        found = []
        for matrix in spot_matrices(index):
            found.append(dot_nt(high, matrix) + (dot_nt(middle, matrix) + dot_nt(low, matrix)))
        for place_out, row in enumerate(NARROW_ROWS):
            out[place_out][layer : layer + 1, :] = found[0][row : row + 1, 0:6]
        pair = found[1][BIAS_Q : BIAS_Q + 1] * flag(index < 64)
        pair += found[1][BIAS_Q + 2 : BIAS_Q + 3] * flag(index >= 64)
        out[6][layer : layer + 1, :] = pair[:, 0:12]
        up = jnp.zeros((1, 128), F32)
        for row in range(4):
            up += found[2][BIAS_UP + row : BIAS_UP + row + 1] * flag(index // 32 == row)
        out[7][layer : layer + 1, :] = up[:, 0:24]


class VectorSum:
    ORDER = "xyzc"

    def __init__(self, m, state, recv):
        self.m, self.state, self.recv, self.number = m, state, recv, 0

    def begin(self):
        m, axis = self.m, self.ORDER[self.number]
        self.steps = range(1, 2 if axis == "c" else 4)
        self.batch = Batch(m.links, self.recv.at[pl.ds(0, len(self.steps))])
        for step in self.steps:
            slot = self.recv.at[3 * self.number + step - 1]
            self.batch.send(self.state.at[self.number], slot, moved(m.me, axis, step))

    def end(self, total):
        self.batch.wait()
        for step in self.steps:
            total += self.recv[3 * self.number + step - 1].astype(F32)
        self.number += 1
        if self.number < 4:
            self.state[self.number] = total.astype(self.state.dtype)
        return total

    def turn(self):
        self.end(self.state[self.number].astype(F32))
        self.begin()


def kernel(*refs):
    inputs, refs = refs[:16], refs[16:]
    outputs, refs = refs[:14], refs[14:]
    staged, refs = refs[:14], refs[14:]
    ready, refs = refs[:12], refs[12:]
    (
        wq, wu, wd, got_qu, got_d, first, second, third, sum_q, sum_u, sum_d,
        x0, x1, h, qkv, probs, o, mid, h2, u, tmp, g, gh, gz, cots, outs, vec, sums,
        low_state, low_recv, stage,
        send_a, recv_a, send_d, recv_d, asm, send_f, recv_f, send_df, recv_df,
        send_sems, recv_sems, local_sems, free,
    ) = refs
    hidden, cot = inputs[:2]
    out, grad = outputs[:2]
    order, remaining, w_qkv, w_out, w_up, w_down, *vectors_in = staged
    gain1, off1, bias_qv, bias_out, gain2, off2, bias_up, bias_down = vectors_in
    g_qkv, g_out, g_up, g_down, *vectors_out = ready
    loads = []
    for number, (src, dst) in enumerate(zip(inputs[2:], staged)):
        loads.append(pltpu.make_async_copy(src, dst, local_sems.at[4 + number]))
        loads[-1].start()
    me = place()
    sibling = moved(me, "c", 1)
    mine = 2 * me["y"] + me["c"]
    index = ((me["z"] * 4 + me["x"]) * 4 + me["y"]) * 2 + me["c"]
    links = Links(me, send_sems, recv_sems)
    m = types.SimpleNamespace(
        me=me, links=links, weights={"q": wq, "u": wu, "d": wd}, wq=wq, wu=wu, wd=wd,
        got_qu=got_qu, got_d=got_d, free=free, totals={"q": sum_q, "u": sum_u, "d": sum_d},
        first=first, second=second, third=third,
        x=[x0, x1, g], h=h, qkv=qkv, probs=probs, o=o, mid=mid, h2=h2, u=u, a=tmp, g=g, gh=gh, gz=gz,
        gu=tmp.at[1], go=tmp.at[3], gqkv=tmp, vec=vec, sums=sums,
    )
    send_f[...] = jnp.zeros(send_f.shape, F32)
    for copy in loads:
        copy.wait()

    for owner in range(8):
        columns = slice(384 * (owner % 2), 384 * (owner % 2) + 384)
        for layer in range(LAYERS):
            for row in range(6):
                if owner < 6:
                    part = w_qkv[row, layer : layer + 1, 384 * owner : 384 * owner + 384]
                else:
                    part = w_out[row, layer : layer + 1, columns]
                send_f[owner, 8 * layer + row : 8 * layer + row + 1, :] = part.astype(F32)
                part = w_up[row, layer : layer + 1, 384 * owner : 384 * owner + 384]
                send_f[owner, 16 + 8 * layer + row : 17 + 8 * layer + row, :] = part.astype(F32)
    for owner in range(8):
        send_a[owner] = send_f[owner].astype(BF16)
    for half in range(2):
        for layer in range(LAYERS):
            part = w_down[layer, :, 384 * half : 384 * half + 384]
            send_df[half, 24 * layer : 24 * layer + 24, :] = part.astype(F32)
        send_d[half] = send_df[half].astype(BF16)
    narrow = (gain1, off1, bias_out, gain2, off2, bias_down)
    spread_vectors(index, narrow, bias_qv, bias_up, stage, low_state.at[0])

    greet(me)

    def group_sends(src, dst, rows=ALL):
        batch = Batch(links, dst.at[pl.ds(0, 7), rows])
        for dy in range(4):
            for dc in range(2):
                if dy or dc:
                    target = moved(moved(me, "y", dy), "c", dc)
                    spot = src.at[2 * target["y"] + target["c"], rows]
                    batch.send(spot, dst.at[mine, rows], target)
        return batch

    arrivals = [group_sends(send_a, recv_a)]
    arrivals.append(links.send(send_d.at[1 - me["c"]], recv_d.at[me["c"]], sibling))
    recv_a[mine] = send_a[mine]
    recv_d[me["c"]] = send_d[me["c"]]
    here = pl.ds(pl.multiple_of(128 * me["c"], 128), 128)
    there = pl.ds(pl.multiple_of(128 * (1 - me["c"]), 128), 128)
    halves = []
    for number, (src, dst) in enumerate(((hidden, x0), (cot, cots))):
        halves.append(links.send(src.at[1 - me["c"]], dst.at[here, :], sibling))
        copy = pltpu.make_async_copy(src.at[me["c"]], dst.at[here, :], local_sems.at[number])
        copy.start()
        halves.append(copy)
    for batch in arrivals:
        batch.wait()
    gathers = [Gather(kind, layer, m) for layer in range(LAYERS) for kind in KINDS]
    own = (me["y"], me["c"], me["z"], me["x"])
    vectors = VectorSum(m, low_state, low_recv)
    for layer in range(LAYERS):
        for group, target in enumerate((wq, wu)):
            for source in range(8):
                rows = slice(16 * group + 8 * layer, 16 * group + 8 * layer + 6)
                asm[group, 6 * source : 6 * source + 6, :] = recv_a[source].astype(F32)[rows]
            target[(layer, *own)] = asm[group].astype(BF16)
            if layer == 0:
                gathers[group].first()
        for half in range(2):
            asm[2, 24 * half : 24 * half + 24, :] = recv_d[half].astype(F32)[
                24 * layer : 24 * layer + 24
            ]
        wd[layer, me["c"], me["z"], me["x"], me["y"]] = asm[2].astype(BF16)
        if layer == 0:
            vectors.begin()
            gathers[2].first()
    gathers[0].second()
    gathers[1].second()
    vectors.turn()
    gathers[0].third()
    gathers[2].second()
    gathers[3].first()
    gathers[1].third()
    vectors.turn()
    gathers[4].first()
    gathers[5].first()
    gathers[0].relay()
    vectors.turn()
    gathers[2].third()
    gathers[3].second()
    gathers[0].finish()
    gathers[4].second()
    vec[...] = vectors.end(low_state[3].astype(F32))
    gathers[1].relay()
    gathers[3].third()
    gathers[5].second()
    halves[0].wait()
    halves[1].wait()
    gathers[0].arrive()

    forward_qkv(0, m)
    gathers[1].finish()
    gathers[2].relay()
    gathers[4].third()
    forward_attention(0, m)
    forward_out(0, m)
    gathers[2].finish()
    gathers[3].relay()
    gathers[5].third()
    gathers[1].arrive()
    forward_up(0, m)
    gathers[3].finish()
    gathers[4].relay()
    gathers[2].arrive()
    forward_down(0, m)
    gathers[4].finish()
    gathers[5].relay()
    gathers[3].arrive()
    forward_qkv(1, m)
    gathers[5].finish()
    forward_attention(1, m)
    forward_out(1, m)
    gathers[4].arrive()
    forward_up(1, m)
    gathers[5].arrive()
    forward_down(1, m)
    outs[...] = g[...].astype(BF16)
    links.drain()
    halves[2].wait()
    halves[3].wait()

    def swap(src, dst, number):
        remote = links.send(src.at[there, :], dst.at[me["c"]], sibling)
        copy = pltpu.make_async_copy(src.at[here, :], dst.at[me["c"]], local_sems.at[number])
        copy.start()
        return remote, copy

    results = [swap(outs, out, 2)]
    upstream(order[pl.ds(me["c"], 1), :], remaining[me["c"]], cots, m)
    sums[...] = jnp.zeros(sums.shape, F32)
    scatters = {(kind, layer): Scatter(kind, layer, m) for layer in (1, 0) for kind in KINDS}

    def ffn(layer):
        groups = [scatters[kind, layer] for kind in "ud"]
        if layer == 0:
            for group in groups:
                group.wait_room()

        @pl.loop(0, 2)
        def _(half):
            @pl.loop(0, 2)
            def _(part):
                backward_ffn(layer, m, 2 * half + part)

                @pl.when(half == 0)
                def _():
                    for group in groups:
                        group.share(part, 0)

                @pl.when(half == 1)
                def _():
                    for group in groups:
                        group.share(2 + part, 1)

                    if layer == 1:

                        @pl.when(part == 0)
                        def _():
                            for group in groups:
                                group.join(0)

    def attention_grads(layer):
        scatter = scatters["q", layer]
        scatter.wait_room()
        scatter.share(3, 1)
        m.gh[...] = jnp.zeros((T, D), F32)

        @pl.loop(0, 3)
        def _(part):
            backward_qkv(layer, m, part)

            @pl.when(part < 2)
            def _():
                scatter.share(part, 0)

            @pl.when(part == 2)
            def _():
                scatter.share(2, 1)

    def steps(step, kinds, layer, *given):
        for kind in kinds:
            getattr(scatters[kind, layer], step)(*given)

    top(1, m)
    ffn(1)
    backward_mid(1, m)
    steps("join", "ud", 1, 1)
    steps("give_room", "ud", 1)
    backward_attention(1, m)
    steps("relay", "ud", 1)
    attention_grads(1)
    backward_in(1, m, g)
    top(0, m)
    steps("join", "q", 1, 0)
    steps("join", "q", 1, 1)
    steps("give_room", "q", 1)
    ffn(0)
    steps("second", "ud", 1)
    steps("relay", "q", 1)
    for half in range(2):
        steps("join", "ud", 0, half)
    steps("give_room", "u", 0)
    backward_mid(0, m)
    steps("third", "ud", 1)
    steps("second", "q", 1)
    backward_attention(0, m)
    steps("relay", "ud", 0)
    attention_grads(0)
    steps("third", "q", 1)
    backward_in(0, m, g)
    results.append(swap(g, grad, 3))
    low_state[0] = sums[...].astype(BF16)
    for half in range(2):
        steps("join", "q", 0, half)
    vectors = VectorSum(m, low_state, low_recv)
    vectors.begin()
    steps("second", "ud", 0)
    steps("finish", "udq", 1)
    steps("relay", "q", 0)
    vectors.turn()
    steps("third", "ud", 0)
    steps("second", "q", 0)
    vectors.turn()
    steps("finish", "ud", 0)

    def owned(total, layer, start):
        for owner in range(8):
            send_f[owner, start : start + 6, :] = total[layer, 6 * owner : 6 * owner + 6, :]

    owned(sum_q, 1, 8)
    owned(sum_u, 0, 16)
    owned(sum_u, 1, 24)
    for layer in range(LAYERS):
        for owner in range(2):
            send_df[owner, 24 * layer : 24 * layer + 24, :] = sum_d[
                layer, 24 * owner : 24 * owner + 24, :
            ]
    last = [group_sends(send_f, recv_f, slice(8, 32))]
    last.append(links.send(send_df.at[1 - me["c"]], recv_df.at[me["c"]], sibling))
    recv_df[me["c"]] = send_df[me["c"]]
    steps("third", "q", 0)
    vectors.turn()
    steps("finish", "q", 0)
    owned(sum_q, 0, 0)
    last.append(group_sends(send_f, recv_f, slice(0, 8)))
    recv_f[mine] = send_f[mine]
    sums[...] = vectors.end(low_state[3].astype(F32))
    own_entries(index, sums, vectors_out)
    for batch in last:
        batch.wait()
    for owner in range(8):
        columns = slice(384 * (owner % 2), 384 * (owner % 2) + 384)
        for layer in range(LAYERS):
            for row in range(6):
                spot = 8 * layer + row
                value = recv_f[owner, spot : spot + 1, :]
                if owner < 6:
                    g_qkv[row, layer : layer + 1, 384 * owner : 384 * owner + 384] = value
                else:
                    g_out[row, layer : layer + 1, columns] = value
                value = recv_f[owner, 16 + spot : 17 + spot, :]
                g_up[row, layer : layer + 1, 384 * owner : 384 * owner + 384] = value
    for layer in range(LAYERS):
        for half in range(2):
            g_down[layer, :, 384 * half : 384 * half + 384] = recv_df[
                half, 24 * layer : 24 * layer + 24, :
            ]
    stores = []
    for number, (src, dst) in enumerate(zip(ready, outputs[2:])):
        stores.append(pltpu.make_async_copy(src, dst, local_sems.at[4 + number]))
        stores[-1].start()
    for remote, copy in results:
        remote.wait()
        copy.wait()
    links.drain()
    for copy in stores:
        copy.wait()


def deliver_kernel(*refs):
    count = len(refs) // 3
    sources, results, held, sems = refs[:count], refs[count : 2 * count], refs[2 * count : -1], refs[-1]
    loads = [
        pltpu.make_async_copy(src, dst, sems.at[0, number])
        for number, (src, dst) in enumerate(zip(sources, held))
    ]
    stores = [
        pltpu.make_async_copy(src, dst, sems.at[1, number])
        for number, (src, dst) in enumerate(zip(held, results))
    ]
    for copy in loads:
        copy.start()
    for load, store in zip(loads, stores):
        load.wait()
        store.start()
    for copy in stores:
        copy.wait()


def deliver(values):
    hbm = pl.BlockSpec(memory_space=pl.ANY)
    return pl.pallas_call(
        deliver_kernel,
        out_shape=[jax.ShapeDtypeStruct(value.shape, value.dtype) for value in values],
        in_specs=[hbm] * len(values),
        out_specs=[hbm] * len(values),
        scratch_shapes=[
            *[pltpu.VMEM(value.shape, value.dtype) for value in values],
            pltpu.SemaphoreType.DMA((2, len(values))),
        ],
        name="deliver",
    )(*values)


def shards(
    hidden, cotangent, remaining, order,
    norm1_gain, norm1_bias, w_qkv, bias_qv, w_out, bias_out,
    norm2_gain, norm2_bias, w_up, bias_up, w_down, bias_down,
):
    half = hidden.shape[1]
    hbm = pl.BlockSpec(memory_space=pl.ANY)
    swapped = [jnp.transpose(weight, (1, 0, 2)) for weight in (w_qkv, w_out, w_up)]
    wide, deep = (LAYERS, 4, 2, 4, 4, 48, 384), (LAYERS, 2, 4, 4, 4, 48, 384)
    inputs = (
        hidden, cotangent, order, remaining, *swapped, w_down,
        norm1_gain, norm1_bias, bias_qv, bias_out, norm2_gain, norm2_bias, bias_up, bias_down,
    )
    results = [((2, half, D), BF16)] + [
        (shape, F32)
        for shape in (
            (2, half, D), (6, LAYERS, 3 * D), (6, LAYERS, D), (6, LAYERS, FF), (LAYERS, 24, D),
            *[(LAYERS, 6)] * 6, (LAYERS, 12), (LAYERS, 24),
        )
    ]
    staged = [pltpu.VMEM(value.shape, value.dtype) for value in inputs[2:]]
    staged[1] = pltpu.SMEM(remaining.shape, remaining.dtype)
    values = pl.pallas_call(
        kernel,
        out_shape=[jax.ShapeDtypeStruct(*result) for result in results],
        in_specs=[hbm] * len(inputs),
        out_specs=[hbm] * len(results),
        scratch_shapes=[
            *staged,
            *[pltpu.VMEM(*result) for result in results[2:]],
            pltpu.VMEM(wide, BF16),
            pltpu.VMEM(wide, BF16),
            pltpu.VMEM(deep, BF16),
            pltpu.VMEM((4, 4, 4, 48, 384), BF16),
            pltpu.VMEM((4, 4, 4, 48, 384), BF16),
            pltpu.VMEM((3, 3, 3, 4, 4, 16, 384), BF16),
            pltpu.VMEM((LAYERS, 3, 3, 3, 4, 16, 384), BF16),
            pltpu.VMEM((LAYERS, 3, 3, 3, 16, 384), BF16),
            *[pltpu.VMEM((LAYERS, 48, 384), F32) for _ in range(3)],
            pltpu.VMEM((T, D), BF16),
            pltpu.VMEM((T, D), F32),
            pltpu.VMEM((LAYERS, T, D), BF16),
            pltpu.VMEM((LAYERS, 3, T, D), BF16),
            pltpu.VMEM((LAYERS, HEADS, T, T), BF16),
            pltpu.VMEM((LAYERS, T, D), BF16),
            pltpu.VMEM((LAYERS, T, D), F32),
            pltpu.VMEM((LAYERS, T, D), BF16),
            pltpu.VMEM((LAYERS, 4, T, D), BF16),
            pltpu.VMEM((4, T, D), BF16),
            pltpu.VMEM((T, D), F32),
            pltpu.VMEM((T, D), F32),
            pltpu.VMEM((T, D), BF16),
            pltpu.VMEM((T, D), BF16),
            pltpu.VMEM((T, D), BF16),
            pltpu.VMEM((LAYERS, 16, D), F32),
            pltpu.VMEM((LAYERS, 16, D), F32),
            pltpu.VMEM((4, LAYERS, 16, D), BF16),
            pltpu.VMEM((10, LAYERS, 16, D), BF16),
            pltpu.VMEM((3, LAYERS, 16, 128), F32),
            pltpu.VMEM((8, 32, 384), BF16),
            pltpu.VMEM((8, 32, 384), BF16),
            pltpu.VMEM((2, 48, 384), BF16),
            pltpu.VMEM((2, 48, 384), BF16),
            pltpu.VMEM((3, 48, 384), F32),
            pltpu.VMEM((8, 32, 384), F32),
            pltpu.VMEM((8, 32, 384), F32),
            pltpu.VMEM((2, 48, 384), F32),
            pltpu.VMEM((2, 48, 384), F32),
            pltpu.SemaphoreType.DMA((89,)),
            pltpu.SemaphoreType.DMA((89,)),
            pltpu.SemaphoreType.DMA((18,)),
            pltpu.SemaphoreType.REGULAR((11,)),
        ],
        compiler_params=pltpu.CompilerParams(
            collective_id=0, has_side_effects=True, vmem_limit_bytes=(63 << 20) + (1 << 19)
        ),
        name="layers",
    )(*inputs)
    values = deliver(values)
    out, grad, g_qkv, g_out, g_up, g_down, gain1, off1, b_out, gain2, off2, b_down, b_qv, b_up = values
    g_qkv, g_out, g_up = (jnp.transpose(part, (1, 0, 2)) for part in (g_qkv, g_out, g_up))
    return out, grad, gain1, off1, g_qkv, b_qv, g_out, b_out, gain2, off2, g_up, b_up, g_down, b_down


def solution(mesh):
    tokens, rows = P("dp", "fsdp", None), P(None, ("dp", "fsdp"), None)
    vector = P(None, ("dp", "fsdp"))
    weights = (
        vector, vector, rows, vector, rows, vector, vector, vector, rows, vector, rows, vector
    )
    return jax.shard_map(
        shards,
        mesh=mesh,
        in_specs=(tokens, tokens, P("dp"), P("dp", None), *weights),
        out_specs=(tokens, tokens, *weights),
        check_vma=False,
    )
```

```python
import types

import jax
import jax.numpy as jnp
from jax import lax
from jax.experimental import pallas as pl
from jax.experimental.pallas import tpu as pltpu
from jax.sharding import PartitionSpec as P

HEAD = 64
HEADS = 12
LAYERS = 2
D = 768
FF = 3072
MESH = pl.DeviceIdType.MESH
BF16, F32 = jnp.bfloat16, jnp.float32

AXES = {"q": "yczx", "u": "yczx", "d": "czxy"}
STREAMS = ((slice(0, 16), "xyz"), (slice(16, 32), "yzx"), (slice(32, 48), "zxy"))
KINDS = "qud"
ALL = slice(None)
STEPS = (1, 3, 2)


def place():
    dp, core = lax.axis_index("dp"), lax.axis_index("fsdp")
    return {"z": dp // 16, "x": (dp // 4) % 4, "y": dp % 4, "c": core}


def device(at):
    return ((at["z"] * 4 + at["x"]) * 4 + at["y"], at["c"])


def moved(at, axis, step):
    size = 2 if axis == "c" else 4
    return {**at, axis: (at[axis] + step) % size}


class Batch:
    def __init__(self, links, whole):
        self.links, self.whole = links, whole
        self.number = links.batches
        links.batches += 1
        links.open.append(self)

    def copy(self, src, dst, target):
        return pltpu.make_async_remote_copy(
            src_ref=src,
            dst_ref=dst,
            send_sem=self.links.send_sems.at[self.number],
            recv_sem=self.links.recv_sems.at[self.number],
            device_id=device(target),
            device_id_type=MESH,
        )

    def send(self, src, dst, target):
        self.copy(src, dst, target).start()

    def all(self):
        return self.copy(self.whole, self.whole, self.links.sibling)

    def wait(self):
        self.all().wait_recv()


class Links:
    def __init__(self, me, send_sems, recv_sems):
        self.sibling = moved(me, "c", 1)
        self.send_sems, self.recv_sems, self.open, self.batches = send_sems, recv_sems, [], 0

    def send(self, src, dst, target):
        batch = Batch(self, src)
        batch.send(src, dst, target)
        return batch

    def drain(self):
        for batch in self.open:
            batch.all().wait_send()
        self.open = []


def greet(me):
    partners = [moved(moved(me, "y", dy), "c", dc) for dy in range(4) for dc in range(2)][1:]
    partners += [moved(me, axis, step) for axis in "xz" for step in (1, 2, 3)]
    barrier = pltpu.get_barrier_semaphore()
    for partner in partners:
        pl.semaphore_signal(barrier, inc=1, device_id=device(partner), device_id_type=MESH)
    pl.semaphore_wait(barrier, len(partners))


T = 256
ROWS = 128
GAIN1, OFF1, BIAS_Q, BIAS_OUT, GAIN2, OFF2, BIAS_UP, BIAS_DOWN = 0, 1, 2, 5, 6, 7, 8, 12


def dot(a, b):
    return jnp.dot(a, b, preferred_element_type=F32)


def dot_nt(a, b):
    return lax.dot_general(a, b, (((1,), (1,)), ((), ())), preferred_element_type=F32)


def dot_tn(a, b):
    return lax.dot_general(a, b, (((0,), (0,)), ((), ())), preferred_element_type=F32)


def slab(ref, layer, index):
    return jnp.concatenate([ref[layer, index, core].reshape(D, 384) for core in range(2)], axis=1)


def chunk(ref, layer, index):
    return jnp.concatenate([ref[layer, core, index].reshape(D, 384) for core in range(2)], axis=1)


def put_slab(ref, layer, index, value):
    for core in range(2):
        ref[layer, index, core] = value[:, core * 384 : (core + 1) * 384].reshape(4, 4, 48, 384)


def put_chunk(ref, layer, index, value):
    for core in range(2):
        ref[layer, core, index] = value[:, core * 384 : (core + 1) * 384].reshape(4, 4, 48, 384)


def rows_of(index):
    return pl.ds(pl.multiple_of(index * ROWS, ROWS), ROWS)


def normal(x):
    center = x - jnp.mean(x, axis=-1, keepdims=True)
    scale = lax.rsqrt(jnp.mean(center * center, axis=-1, keepdims=True) + 1e-05)
    return center * scale, scale


def norm_into(x_ref, vec, gain, offset, out_ref):
    @pl.loop(0, T // ROWS)
    def _(index):
        rows = rows_of(index)
        hat, _ = normal(x_ref[rows, :].astype(F32))
        out_ref[rows, :] = (hat * vec[gain : gain + 1, :] + vec[offset : offset + 1, :]).astype(BF16)


def fold(value):
    return jnp.sum(value.reshape(ROWS // 8, 8, value.shape[1]), axis=0)


def total(value):
    return jnp.sum(value, axis=0, keepdims=True)


def norm_back(x_ref, grad_ref, vec, sums, gain, offset, top_ref, out_ref, bias=None, low_ref=None):
    zero = jnp.zeros((8, D), F32)

    def body(index, carry):
        sum_gain, sum_offset, sum_bias = carry
        rows = rows_of(index)
        hat, scale = normal(x_ref[rows, :].astype(F32))
        grad = grad_ref[rows, :]
        scaled = grad * vec[gain : gain + 1, :]
        inner = scaled - jnp.mean(scaled, axis=-1, keepdims=True)
        inner -= hat * jnp.mean(scaled * hat, axis=-1, keepdims=True)
        result = top_ref[rows, :] + scale * inner
        out_ref[rows, :] = result
        low = result.astype(BF16)
        if low_ref is not None:
            low_ref[rows, :] = low
        return sum_gain + fold(grad * hat), sum_offset + fold(grad), sum_bias + fold(low.astype(F32))

    sum_gain, sum_offset, sum_bias = lax.fori_loop(0, T // ROWS, body, (zero, zero, zero))
    sums[gain : gain + 1, :] = total(sum_gain)
    sums[offset : offset + 1, :] = total(sum_offset)
    if bias is not None:
        sums[bias : bias + 1, :] = total(sum_bias)


def gelu_parts(u):
    inner = 0.7978845608028654 * (u + 0.044715 * u * u * u)
    t = jnp.tanh(inner)
    slope = 0.7978845608028654 * (1.0 + 0.134145 * u * u)
    half = 0.5 * (1.0 + t)
    return u * half, half + 0.5 * u * (1.0 - t * t) * slope


def gelu(u):
    return 0.5 * u * (1.0 + jnp.tanh(0.7978845608028654 * (u + 0.044715 * u * u * u)))


def head_mask(which, scale=1.0):
    lane = lax.broadcasted_iota(jnp.int32, (1, 128), 1)
    return jnp.where(lane // HEAD == which, scale, 0.0).astype(BF16)


def lanes_of(pair):
    return pl.ds(pl.multiple_of(pair * 128, 128), 128)


def forward_qkv(layer, m):
    norm_into(m.x[layer], m.vec.at[layer], GAIN1, OFF1, m.h.at[layer])

    @pl.loop(0, 3)
    def _(part):
        bias = m.vec[layer, pl.ds(BIAS_Q + part, 1), :]
        m.qkv[layer, part] = (dot(m.h[layer], slab(m.wq, layer, part)) + bias).astype(BF16)


def forward_attention(layer, m):
    @pl.loop(0, HEADS // 2)
    def _(pair):
        lanes = lanes_of(pair)
        query, keys, values = (m.qkv[layer, part, :, lanes] for part in range(3))
        attended = jnp.zeros((T, 128), F32)
        for which in range(2):
            scores = dot_nt(query * head_mask(which, 0.125), keys)
            grown = jnp.exp(scores - jnp.max(scores, axis=-1, keepdims=True))
            probs = grown * (1.0 / jnp.sum(grown, axis=-1, keepdims=True))
            probs = probs.astype(BF16)
            m.probs[layer, 2 * pair + which] = probs
            attended += dot(probs, values * head_mask(which))
        m.o[layer, :, lanes] = attended.astype(BF16)


def forward_out(layer, m):
    m.mid[layer] = (
        m.x[layer][...].astype(F32)
        + dot(m.o[layer], slab(m.wq, layer, 3))
        + m.vec[layer, BIAS_OUT : BIAS_OUT + 1, :]
    )
    norm_into(m.mid.at[layer], m.vec.at[layer], GAIN2, OFF2, m.h2.at[layer])


def forward_up(layer, m):
    @pl.loop(0, 4)
    def _(index):
        bias = m.vec[layer, pl.ds(BIAS_UP + index, 1), :]
        u = dot(m.h2[layer], slab(m.wu, layer, index)) + bias
        m.u[layer, index] = u.astype(BF16)
        m.a[index] = gelu(u).astype(BF16)


def forward_down(layer, m):
    out = m.x[layer + 1]
    out[...] = m.mid[layer] + m.vec[layer, BIAS_DOWN : BIAS_DOWN + 1, :]

    @pl.loop(0, 4)
    def _(index):
        out[...] += dot(m.a[index], chunk(m.wd, layer, index))


def backward_ffn(layer, m, index):
    grad_active = dot_nt(m.gz[...], chunk(m.wd, layer, index))
    active, slope = gelu_parts(m.u[layer, index].astype(F32))
    pre = (grad_active * slope).astype(BF16)
    m.gu[...] = pre
    m.a[0] = active.astype(BF16)
    m.sums[layer, pl.ds(BIAS_UP + index, 1), :] = total(pre.astype(F32))
    m.gh[...] += dot_nt(m.gu[...], slab(m.wu, layer, index))
    put_chunk(m.wd, layer, index, dot_tn(m.a[0], m.gz[...]).astype(BF16))
    put_slab(m.wu, layer, index, dot_tn(m.h2[layer], m.gu[...]).astype(BF16))


def backward_mid(layer, m):
    norm_back(
        m.mid.at[layer], m.gh, m.vec.at[layer], m.sums.at[layer], GAIN2, OFF2, m.g, m.g, BIAS_OUT, m.gz
    )
    m.go[...] = dot_nt(m.gz[...], slab(m.wq, layer, 3)).astype(BF16)
    put_slab(m.wq, layer, 3, dot_tn(m.o[layer], m.gz[...]).astype(BF16))


def backward_attention(layer, m):
    @pl.loop(0, HEADS // 2)
    def _(pair):
        lanes = lanes_of(pair)
        query, keys, values = (m.qkv[layer, part, :, lanes] for part in range(3))
        grad = m.go[:, lanes]
        zero = jnp.zeros((T, 128), F32)
        grad_query, grad_keys, grad_values = zero, zero, zero
        for which in range(2):
            low = m.probs[layer, 2 * pair + which]
            probs = low.astype(F32)
            part = grad * head_mask(which)
            grad_probs = dot_nt(part, values)
            grad_values += dot_tn(low, part)
            row_dot = jnp.sum(grad_probs * probs, axis=-1, keepdims=True)
            grad_scores = (probs * (grad_probs - row_dot)).astype(BF16)
            grad_query += dot(grad_scores, keys * head_mask(which, 0.125))
            grad_keys += dot_tn(grad_scores, query * head_mask(which, 0.125))
        for part, value in enumerate((grad_query, grad_keys, grad_values)):
            m.gqkv[part, :, lanes] = value.astype(BF16)


def backward_qkv(layer, m, part):
    m.sums[layer, pl.ds(BIAS_Q + part, 1), :] = total(m.gqkv[part].astype(F32))
    m.gh[...] += dot_nt(m.gqkv[part], slab(m.wq, layer, part))
    put_slab(m.wq, layer, part, dot_tn(m.h[layer], m.gqkv[part]).astype(BF16))


def backward_in(layer, m, out_ref):
    norm_back(m.x[layer], m.gh, m.vec.at[layer], m.sums.at[layer], GAIN1, OFF1, m.g, out_ref)


def upstream(order_ref, remaining_ref, cot_ref, m):
    live = lax.broadcasted_iota(jnp.int32, (1, T), 1) >= T - remaining_ref

    def body(index, carry):
        rows = rows_of(index)
        spot = index * ROWS + lax.broadcasted_iota(jnp.int32, (ROWS, 1), 0)
        hit = jnp.where((order_ref == spot) & live, 1.0, 0.0)
        mask = jnp.max(hit, axis=-1, keepdims=True)
        grad = cot_ref[rows, :].astype(F32) * mask
        m.g[rows, :] = grad
        return carry

    lax.fori_loop(0, T // ROWS, body, 0)


def top(layer, m):
    def body(index, carry):
        rows = rows_of(index)
        low = m.g[rows, :].astype(BF16)
        m.gz[rows, :] = low
        return carry + fold(low.astype(F32))

    sums = lax.fori_loop(0, T // ROWS, body, jnp.zeros((8, D), F32))
    m.sums[layer, BIAS_DOWN : BIAS_DOWN + 1, :] = total(sums)
    m.gh[...] = jnp.zeros((T, D), F32)


class Gather:
    def __init__(self, kind, layer, m):
        self.kind, self.layer, self.m = kind, layer, m
        sizes = m.wq.at[0]
        self.handed = Batch(m.links, sizes.at[:, 0])
        self.one = Batch(m.links, sizes.at[0, 0, 0, pl.ds(0, 3)])
        self.two = Batch(m.links, sizes.at[0, 0, pl.ds(0, 3)])
        self.three = Batch(m.links, sizes.at[pl.ds(0, 2), 0])
        self.halves = Batch(m.links, sizes.at[0, 0])

    def part(self, rows, at):
        index = tuple(at[axis] for axis in AXES[self.kind])
        return self.m.weights[self.kind].at[(self.layer, *index, rows, ALL)]

    def hand_over(self, rows, at):
        part = self.part(rows, at)
        self.handed.send(part, part, self.m.links.sibling)

    def out(self, batch, rows, at, axis, steps):
        part = self.part(rows, at)
        for step in steps:
            batch.send(part, part, moved(self.m.me, axis, step))

    def first(self):
        for rows, axes in STREAMS:
            self.out(self.one, rows, self.m.me, axes[0], STEPS)

    def second(self):
        self.one.wait()
        for rows, axes in STREAMS:
            self.out(self.two, rows, {**self.m.me, axes[0]: ALL}, axes[1], STEPS)

    def third(self):
        self.two.wait()
        planes = [
            (rows, axes, {**self.m.me, axes[0]: ALL, axes[1]: ALL}) for rows, axes in STREAMS
        ]
        for rows, axes, plane in planes:
            self.out(self.three, rows, plane, axes[2], (1, 3))
        for rows, axes, plane in planes:
            self.hand_over(rows, plane)

    def relay(self):
        self.three.wait()
        came = [
            (rows, axes, step, {**moved(self.m.me, axes[2], -step), axes[0]: ALL, axes[1]: ALL})
            for rows, axes in STREAMS
            for step in (1, 3)
        ]
        for rows, axes, step, at in came:
            self.out(self.halves, rows, {**at, axes[0]: pl.ds(step - 1, 2)}, axes[2], (step,))
        for rows, axes, step, at in came:
            self.hand_over(rows, at)

    def finish(self):
        self.halves.wait()
        for rows, axes in STREAMS:
            self.hand_over(rows, {**moved(self.m.me, axes[2], 2), axes[0]: ALL, axes[1]: ALL})

    def arrive(self):
        self.handed.wait()


class Scatter:
    def __init__(self, kind, layer, m):
        self.kind, self.layer, self.m = kind, layer, m
        self.slow = "z" if kind == "d" else "y"
        number = KINDS.index(kind)
        self.streams = []
        for stream, (rows, axes) in enumerate(STREAMS):
            others = [axis for axis in AXES[kind] if axis not in ("c", axes[2])]
            slots = m.first.at[number, stream]
            later = (m.second.at[layer, number, stream], m.third.at[layer, number, stream])
            free = m.free.at[3 * number + stream]
            self.streams.append((rows, axes[::-1], others, slots, *later, free))
        sizes = m.wq.at[0]
        self.shared = [Batch(m.links, sizes.at[pl.ds(0, 2), 0]) for _ in range(2)]
        self.passing, self.direct, self.passed = (Batch(m.links, sizes.at[0, 0]) for _ in range(3))
        self.two = Batch(m.links, sizes.at[0, 0, pl.ds(0, 3)])
        self.one = Batch(m.links, sizes.at[0, 0, 0, pl.ds(0, 3)])
        self.room, self.got = (m.free.at[9], m.got_d) if kind == "d" else (m.free.at[10], m.got_qu)

    def part(self, rows, at):
        index = tuple(at.get(axis, ALL) for axis in AXES[self.kind])
        return self.m.weights[self.kind].at[(self.layer, *index, rows, ALL)]

    def share(self, index, half):
        sibling = self.m.links.sibling
        src = self.part(ALL, {self.slow: index, "c": sibling["c"]})
        self.shared[half].send(src, self.got.at[index], sibling)

    def wait_room(self):
        pl.semaphore_wait(self.room, 1)

    def give_room(self):
        sibling = device(self.m.links.sibling)
        pl.semaphore_signal(self.room, inc=1, device_id=sibling, device_id_type=MESH)

    def join(self, half):
        m, me = self.m, self.m.me
        other = "x" if self.kind == "d" else "z"
        self.shared[half].wait()

        @pl.loop(8 * half, 8 * half + 8)
        def _(spot):
            own = self.part(ALL, {self.slow: spot // 4, other: spot % 4, "c": me["c"]})
            own[...] += self.got[spot // 4, spot % 4]

        ready = []
        for rows, axes, others, slots, _, _, free in self.streams:
            split = others[0] == self.slow
            if self.layer == 0 and half == (0 if split else 1):
                pl.semaphore_wait(free, 2)
            for now in (half,) if split else (0, 1) if half else ():
                ready.append((rows, axes[0], others[0], slots, now))
        for now in ready:
            self.pass_on(*now)
        for now in ready:
            self.leave(*now)

    def pass_on(self, rows, axis, split, slots, half):
        me, halves = self.m.me, pl.ds(2 * half, 2)
        src = self.part(rows, {"c": me["c"], split: halves, axis: moved(me, axis, 2)[axis]})
        self.passing.send(src, slots.at[2, halves], moved(me, axis, 1 + 2 * half))

    def leave(self, rows, axis, split, slots, half):
        me, halves = self.m.me, pl.ds(2 * half, 2)
        target = moved(me, axis, 3 - 2 * half)
        src = self.part(rows, {"c": me["c"], split: halves, axis: target[axis]})
        self.direct.send(src, slots.at[1 - half, halves], target)

    def relay(self):
        me = self.m.me
        self.passing.wait()
        for rows, axes, others, slots, _, _, _ in self.streams:
            for half in range(2):
                target = moved(me, axes[0], 1 + 2 * half)
                spot = {"c": me["c"], axes[0]: target[axes[0]]}
                for index in (2 * half, 2 * half + 1):
                    own = self.part(rows, {**spot, others[0]: index})
                    own[...] += slots[2, index]
                halves = pl.ds(2 * half, 2)
                src = self.part(rows, {**spot, others[0]: halves})
                self.passed.send(src, slots.at[half, halves], target)

    def add(self, target, slots):
        value = target[...].astype(F32)
        for slot in slots:
            value += slot[...].astype(F32)
        return value

    def second(self):
        m, me = self.m, self.m.me
        self.direct.wait()
        self.passed.wait()
        for rows, axes, others, slots, later, _, free in self.streams:
            here = {"c": me["c"], axes[0]: me[axes[0]]}

            @pl.loop(0, 4)
            def _(index):
                target = self.part(rows, {**here, others[0]: index})
                total = self.add(target, [slots.at[side, index] for side in range(2)])
                target[...] = total.astype(BF16)

            if self.layer == 1:
                for step in (1, 3):
                    peer = device(moved(me, axes[0], step))
                    pl.semaphore_signal(free, inc=1, device_id=peer, device_id_type=MESH)
            for step in STEPS:
                target = moved(me, axes[1], step)
                src = self.part(rows, {**here, axes[1]: target[axes[1]]})
                self.two.send(src, later.at[step - 1], target)

    def third(self):
        m, me = self.m, self.m.me
        self.two.wait()
        for rows, axes, _, _, later, last, _ in self.streams:
            here = {"c": me["c"], axes[0]: me[axes[0]], axes[1]: me[axes[1]]}
            target = self.part(rows, here)
            target[...] = self.add(target, [later.at[step] for step in range(3)]).astype(BF16)
            for step in STEPS:
                target = moved(me, axes[2], step)
                src = self.part(rows, {**here, axes[2]: target[axes[2]]})
                self.one.send(src, last.at[step - 1], target)

    def finish(self):
        self.one.wait()
        for rows, _, _, _, _, last, _ in self.streams:
            total = self.add(self.part(rows, self.m.me), [last.at[step] for step in range(3)])
            self.m.totals[self.kind][self.layer, rows, :] = total


TILE_PAIRS = ((GAIN1, OFF1), (BIAS_OUT, GAIN2), (OFF2, BIAS_DOWN))
NARROW_ROWS = tuple(row for pair in TILE_PAIRS for row in pair)


def spot_matrix(base, width):
    row = lax.broadcasted_iota(jnp.int32, (128, 128), 0)
    lane = lax.broadcasted_iota(jnp.int32, (128, 128), 1)
    return jnp.where((lane == base + row) & (row < width), 1.0, 0.0).astype(BF16)


def spot_matrices(member):
    return (
        spot_matrix(6 * member, 6), spot_matrix(48 + 6 * member, 6),
        spot_matrix(12 * member, 12), spot_matrix(24 * (member % 4), 24),
    )


def flag(condition):
    return jnp.where(condition, 1.0, 0.0).astype(F32)


def vector_tile(member, narrow, wide_qv, wide_up, stage):
    stage[...] = jnp.zeros(stage.shape, F32)
    for layer in range(LAYERS):
        rows = slice(layer, layer + 1)
        for number, vector in enumerate(narrow):
            row = 8 * layer + number // 2
            stage[number % 2, row : row + 1, 0:6] = vector[rows, :].astype(F32)
        row = 8 * layer + 3
        stage[2, row : row + 1, 0:12] = wide_qv[rows, :].astype(F32)
        for half in range(2):
            up = wide_up[rows, :].astype(F32) * flag(member // 4 == half)
            stage[3, row + 1 + half : row + 2 + half, 0:24] = up
    total = jnp.zeros((16, 128), F32)
    for number, matrix in enumerate(spot_matrices(member)):
        total += dot(stage[number].astype(BF16), matrix)
    return total.astype(BF16)


def whole_vectors(tiles, vec):
    tiles = [tiles[index // 4, index % 4].astype(F32) for index in range(16)]

    def joined(row, first, last, groups):
        return jnp.concatenate([tiles[group][row : row + 1, first:last] for group in groups], axis=1)

    for layer in range(LAYERS):
        vec[layer] = jnp.zeros((16, D), F32)
        for number, pair in enumerate(TILE_PAIRS):
            for side, row in enumerate(pair):
                value = joined(8 * layer + number, 48 * side, 48 * side + 48, range(16))
                vec[layer, row : row + 1, :] = value
        for side in range(2):
            value = joined(8 * layer + 3, 0, 96, range(8 * side, 8 * side + 8))
            vec[layer, BIAS_Q + 2 * side : BIAS_Q + 2 * side + 1, :] = value
        for part in range(4):
            pieces = []
            for group in range(4 * part, 4 * part + 4):
                for half in range(2):
                    row = 8 * layer + 4 + half
                    pieces.append(tiles[group][row : row + 1, 0:96])
            value = jnp.concatenate(pieces, axis=1)
            vec[layer, BIAS_UP + part : BIAS_UP + part + 1, :] = value


def vector_tiles(sums, tiles):
    tiles[...] = jnp.zeros(tiles.shape, F32)
    for layer in range(LAYERS):
        for group in range(16):
            spot = tiles.at[group // 4, group % 4]
            for number, pair in enumerate(TILE_PAIRS):
                for side, row in enumerate(pair):
                    value = sums[layer, row : row + 1, 48 * group : 48 * group + 48]
                    at = 8 * layer + number
                    spot[at : at + 1, 48 * side : 48 * side + 48] = value
            row, start = BIAS_Q + 2 * (group // 8), 96 * (group % 8)
            at = 8 * layer + 3
            spot[at : at + 1, 0:96] = sums[layer, row : row + 1, start : start + 96]
            row, start = BIAS_UP + group // 4, 192 * (group % 4)
            for half in range(2):
                first = start + 96 * half
                value = sums[layer, row : row + 1, first : first + 96]
                spot[at + 1 + half : at + 2 + half, 0:96] = value


def own_entries(member, value, out):
    high = value.astype(BF16)
    middle = (value - high.astype(F32)).astype(BF16)
    low = (value - high.astype(F32) - middle.astype(F32)).astype(BF16)
    found = [
        dot_nt(high, matrix) + (dot_nt(middle, matrix) + dot_nt(low, matrix))
        for matrix in spot_matrices(member)
    ]
    for layer in range(LAYERS):
        rows = slice(layer, layer + 1)
        for number in range(6):
            row = 8 * layer + number // 2
            out[number][rows, :] = found[number % 2][row : row + 1, 0:6]
        row = 8 * layer + 3
        out[6][rows, :] = found[2][row : row + 1, 0:12]
        up = found[3][row + 1 : row + 2] * flag(member // 4 == 0)
        up += found[3][row + 2 : row + 3] * flag(member // 4 == 1)
        out[7][rows, :] = up[:, 0:24]


def kernel(*refs):
    inputs, refs = refs[:16], refs[16:]
    outputs, refs = refs[:14], refs[14:]
    staged, refs = refs[:14], refs[14:]
    ready, refs = refs[:12], refs[12:]
    (
        wq, wu, wd, got_qu, got_d, first, second, third, sum_q, sum_u, sum_d,
        x0, x1, x2, h, qkv, probs, o, mid, h2, u, tmp, g, gh, gz, cots, outs, vec, sums,
        vec_out, vec_in, vec_all, stage, sum_all, sum_in, sum_next, sum_out, sum_got,
        send_a, recv_a, send_d, recv_d, asm, send_f, recv_f, send_df, recv_df,
        send_sems, recv_sems, local_sems, free,
    ) = refs
    hidden, cot = inputs[:2]
    out, grad = outputs[:2]
    order, remaining, w_qkv, w_out, w_up, w_down, *vectors_in = staged
    gain1, off1, bias_qv, bias_out, gain2, off2, bias_up, bias_down = vectors_in
    g_qkv, g_out, g_up, g_down, *vectors_out = ready
    loads = []
    for number, (src, dst) in enumerate(zip(inputs[2:], staged)):
        loads.append(pltpu.make_async_copy(src, dst, local_sems.at[4 + number]))
        loads[-1].start()
    me = place()
    sibling = moved(me, "c", 1)
    mine = 2 * me["y"] + me["c"]
    links = Links(me, send_sems, recv_sems)
    m = types.SimpleNamespace(
        me=me, links=links, weights={"q": wq, "u": wu, "d": wd}, wq=wq, wu=wu, wd=wd,
        got_qu=got_qu, got_d=got_d, free=free, totals={"q": sum_q, "u": sum_u, "d": sum_d},
        first=first, second=second, third=third,
        x=[x0, x1, x2], h=h, qkv=qkv, probs=probs, o=o, mid=mid, h2=h2, u=u, a=tmp, g=g, gh=gh, gz=gz,
        gu=tmp.at[1], go=tmp.at[3], gqkv=tmp, vec=vec, sums=sums,
    )
    send_f[...] = jnp.zeros(send_f.shape, F32)
    for copy in loads:
        copy.wait()

    for owner in range(8):
        columns = slice(384 * (owner % 2), 384 * (owner % 2) + 384)
        for layer in range(LAYERS):
            for row in range(6):
                if owner < 6:
                    part = w_qkv[row, layer : layer + 1, 384 * owner : 384 * owner + 384]
                else:
                    part = w_out[row, layer : layer + 1, columns]
                send_f[owner, 8 * layer + row : 8 * layer + row + 1, :] = part.astype(F32)
                part = w_up[row, layer : layer + 1, 384 * owner : 384 * owner + 384]
                send_f[owner, 16 + 8 * layer + row : 17 + 8 * layer + row, :] = part.astype(F32)
    for owner in range(8):
        send_a[owner] = send_f[owner].astype(BF16)
    for half in range(2):
        for layer in range(LAYERS):
            part = w_down[layer, :, 384 * half : 384 * half + 384]
            send_df[half, 24 * layer : 24 * layer + 24, :] = part.astype(F32)
        send_d[half] = send_df[half].astype(BF16)
    narrow = (gain1, off1, bias_out, gain2, off2, bias_down)
    vec_out[...] = vector_tile(mine, narrow, bias_qv, bias_up, stage)

    greet(me)

    def group_sends(src, dst, rows=ALL):
        batch = Batch(links, dst.at[pl.ds(0, 7), rows])
        for dy in range(4):
            for dc in range(2):
                if dy or dc:
                    target = moved(moved(me, "y", dy), "c", dc)
                    spot = src.at[2 * target["y"] + target["c"], rows]
                    batch.send(spot, dst.at[mine, rows], target)
        return batch

    def group_tiles(src, dst):
        batch = Batch(links, dst.at[pl.ds(0, 7)])
        for dy in range(4):
            for dc in range(2):
                if dy or dc:
                    batch.send(src, dst.at[mine], moved(moved(me, "y", dy), "c", dc))
        return batch

    arrivals = [group_tiles(vec_out, vec_in), group_sends(send_a, recv_a)]
    arrivals.append(links.send(send_d.at[1 - me["c"]], recv_d.at[me["c"]], sibling))
    recv_a[mine] = send_a[mine]
    recv_d[me["c"]] = send_d[me["c"]]
    vec_in[mine] = vec_out[...]
    here = pl.ds(pl.multiple_of(128 * me["c"], 128), 128)
    there = pl.ds(pl.multiple_of(128 * (1 - me["c"]), 128), 128)
    halves = []
    for number, (src, dst) in enumerate(((hidden, x0), (cot, cots))):
        halves.append(links.send(src.at[1 - me["c"]], dst.at[here, :], sibling))
        copy = pltpu.make_async_copy(src.at[me["c"]], dst.at[here, :], local_sems.at[number])
        copy.start()
        halves.append(copy)
    for batch in arrivals:
        batch.wait()
    gathers = [Gather(kind, layer, m) for layer in range(LAYERS) for kind in KINDS]
    own = (me["y"], me["c"], me["z"], me["x"])
    tile = jnp.zeros((16, 128), F32)
    for source in range(8):
        tile += vec_in[source].astype(F32)
    vec_all[me["z"], me["x"]] = tile.astype(BF16)
    spot = vec_all.at[me["z"], me["x"]]
    along_z = Batch(links, vec_all.at[0, pl.ds(0, 3)])
    for step in STEPS:
        along_z.send(spot, spot, moved(me, "z", step))
    for layer in range(LAYERS):
        for group, target in enumerate((wq, wu)):
            for source in range(8):
                rows = slice(16 * group + 8 * layer, 16 * group + 8 * layer + 6)
                asm[group, 6 * source : 6 * source + 6, :] = recv_a[source].astype(F32)[rows]
            target[(layer, *own)] = asm[group].astype(BF16)
            gathers[3 * layer + group].first()
        for half in range(2):
            asm[2, 24 * half : 24 * half + 24, :] = recv_d[half].astype(F32)[
                24 * layer : 24 * layer + 24
            ]
        wd[layer, me["c"], me["z"], me["x"], me["y"]] = asm[2].astype(BF16)
        gathers[3 * layer + 2].first()
    q0, u0, d0, q1, u1, d1 = gathers
    q0.second()
    along_z.wait()
    column = vec_all.at[:, me["x"]]
    along_x = Batch(links, vec_all.at[pl.ds(0, 3)])
    for step in STEPS:
        along_x.send(column, column, moved(me, "x", step))
    u0.second()
    q0.third()
    d0.second()
    u0.third()
    along_x.wait()
    whole_vectors(vec_all, vec)
    q1.second()
    q0.relay()
    d0.third()
    u1.second()
    d1.second()
    q0.finish()
    u0.relay()
    q1.third()
    halves[0].wait()
    halves[1].wait()
    q0.arrive()

    forward_qkv(0, m)
    u0.finish()
    d0.relay()
    u1.third()
    forward_attention(0, m)
    u0.arrive()
    d0.finish()
    q1.relay()
    d1.third()
    forward_out(0, m)
    forward_up(0, m)
    d0.arrive()
    forward_down(0, m)
    q1.finish()
    u1.relay()
    halves[2].wait()
    halves[3].wait()
    upstream(order[pl.ds(me["c"], 1), :], remaining[me["c"]], cots, m)
    sums[...] = jnp.zeros(sums.shape, F32)
    top(1, m)
    q1.arrive()
    forward_qkv(1, m)
    u1.finish()
    forward_attention(1, m)
    d1.relay()
    forward_out(1, m)
    u1.arrive()
    forward_up(1, m)
    d1.finish()
    d1.arrive()
    forward_down(1, m)
    outs[...] = x2[...].astype(BF16)
    links.drain()

    def swap(src, dst, number):
        remote = links.send(src.at[there, :], dst.at[me["c"]], sibling)
        copy = pltpu.make_async_copy(src.at[here, :], dst.at[me["c"]], local_sems.at[number])
        copy.start()
        return remote, copy

    results = [swap(outs, out, 2)]
    scatters = {(kind, layer): Scatter(kind, layer, m) for layer in (1, 0) for kind in KINDS}

    def ffn(layer):
        groups = [scatters[kind, layer] for kind in "ud"]
        if layer == 0:
            for group in groups:
                group.wait_room()

        @pl.loop(0, 2)
        def _(half):
            @pl.loop(0, 2)
            def _(part):
                backward_ffn(layer, m, 2 * half + part)

                @pl.when(half == 0)
                def _():
                    for group in groups:
                        group.share(part, 0)

                    if layer == 0:

                        @pl.when(part == 1)
                        def _():
                            scatters["q", 1].relay()

                @pl.when(half == 1)
                def _():
                    for group in groups:
                        group.share(2 + part, 1)

                    @pl.when(part == 0)
                    def _():
                        for group in groups:
                            group.join(0)

    def attention_grads(layer):
        scatter = scatters["q", layer]
        scatter.wait_room()
        scatter.share(3, 1)
        m.gh[...] = jnp.zeros((T, D), F32)

        @pl.loop(0, 3)
        def _(part):
            backward_qkv(layer, m, part)

            @pl.when(part < 2)
            def _():
                scatter.share(part, 0)

            @pl.when(part == 2)
            def _():
                scatter.share(2, 1)

    def steps(step, kinds, layer, *given):
        for kind in kinds:
            getattr(scatters[kind, layer], step)(*given)

    ffn(1)
    backward_mid(1, m)
    steps("join", "ud", 1, 1)
    steps("give_room", "ud", 1)
    backward_attention(1, m)
    steps("relay", "ud", 1)
    attention_grads(1)
    backward_in(1, m, g)
    top(0, m)
    steps("join", "q", 1, 0)
    steps("join", "q", 1, 1)
    steps("give_room", "q", 1)
    steps("second", "ud", 1)
    ffn(0)
    backward_mid(0, m)
    for kind in "ud":
        steps("join", kind, 0, 1)
    steps("give_room", "u", 0)
    steps("second", "q", 1)
    steps("third", "ud", 1)
    backward_attention(0, m)
    steps("relay", "ud", 0)
    steps("third", "q", 1)
    attention_grads(0)
    backward_in(0, m, g)
    vector_tiles(sums, sum_all)
    along_z = Batch(links, sum_in)
    for step in STEPS:
        target = moved(me, "z", step)
        along_z.send(sum_all.at[target["z"]], sum_in.at[step - 1], target)
    results.append(swap(g, grad, 3))
    steps("join", "q", 0, 0)
    steps("join", "q", 0, 1)
    steps("second", "ud", 0)
    steps("finish", "udq", 1)
    along_z.wait()
    for index in range(4):
        row = sum_all[me["z"], index]
        for step in range(3):
            row += sum_in[step, index]
        sum_all[me["z"], index] = row
    along_x = Batch(links, sum_next)
    for step in STEPS:
        target = moved(me, "x", step)
        along_x.send(sum_all.at[me["z"], target["x"]], sum_next.at[step - 1], target)
    steps("relay", "q", 0)
    steps("third", "ud", 0)
    along_x.wait()
    tile = sum_all[me["z"], me["x"]]
    for step in range(3):
        tile += sum_next[step]
    sum_out[...] = tile
    last = [group_tiles(sum_out, sum_got)]
    sum_got[mine] = tile
    steps("second", "q", 0)
    steps("finish", "ud", 0)

    def owned(total, layer, start):
        for owner in range(8):
            send_f[owner, start : start + 6, :] = total[layer, 6 * owner : 6 * owner + 6, :]

    owned(sum_q, 1, 8)
    owned(sum_u, 0, 16)
    owned(sum_u, 1, 24)
    for layer in range(LAYERS):
        for owner in range(2):
            send_df[owner, 24 * layer : 24 * layer + 24, :] = sum_d[
                layer, 24 * owner : 24 * owner + 24, :
            ]
    last.append(group_sends(send_f, recv_f, slice(8, 32)))
    last.append(links.send(send_df.at[1 - me["c"]], recv_df.at[me["c"]], sibling))
    recv_df[me["c"]] = send_df[me["c"]]
    steps("third", "q", 0)
    steps("finish", "q", 0)
    owned(sum_q, 0, 0)
    last.append(group_sends(send_f, recv_f, slice(0, 8)))
    recv_f[mine] = send_f[mine]
    last[0].wait()
    tile = sum_got[0]
    for source in range(1, 8):
        tile += sum_got[source]
    own_entries(mine, tile, vectors_out)
    for batch in last[1:]:
        batch.wait()
    for owner in range(8):
        columns = slice(384 * (owner % 2), 384 * (owner % 2) + 384)
        for layer in range(LAYERS):
            for row in range(6):
                spot = 8 * layer + row
                value = recv_f[owner, spot : spot + 1, :]
                if owner < 6:
                    g_qkv[row, layer : layer + 1, 384 * owner : 384 * owner + 384] = value
                else:
                    g_out[row, layer : layer + 1, columns] = value
                value = recv_f[owner, 16 + spot : 17 + spot, :]
                g_up[row, layer : layer + 1, 384 * owner : 384 * owner + 384] = value
    for layer in range(LAYERS):
        for half in range(2):
            g_down[layer, :, 384 * half : 384 * half + 384] = recv_df[
                half, 24 * layer : 24 * layer + 24, :
            ]
    stores = []
    for number, (src, dst) in enumerate(zip(ready, outputs[2:])):
        stores.append(pltpu.make_async_copy(src, dst, local_sems.at[4 + number]))
        stores[-1].start()
    for remote, copy in results:
        remote.wait()
        copy.wait()
    links.drain()
    for copy in stores:
        copy.wait()


def deliver_kernel(*refs):
    count = len(refs) // 3
    sources, results, held, sems = refs[:count], refs[count : 2 * count], refs[2 * count : -1], refs[-1]
    loads = [
        pltpu.make_async_copy(src, dst, sems.at[0, number])
        for number, (src, dst) in enumerate(zip(sources, held))
    ]
    stores = [
        pltpu.make_async_copy(src, dst, sems.at[1, number])
        for number, (src, dst) in enumerate(zip(held, results))
    ]
    for copy in loads:
        copy.start()
    for load, store in zip(loads, stores):
        load.wait()
        store.start()
    for copy in stores:
        copy.wait()


def deliver(values):
    hbm = pl.BlockSpec(memory_space=pl.ANY)
    return pl.pallas_call(
        deliver_kernel,
        out_shape=[jax.ShapeDtypeStruct(value.shape, value.dtype) for value in values],
        in_specs=[hbm] * len(values),
        out_specs=[hbm] * len(values),
        scratch_shapes=[
            *[pltpu.VMEM(value.shape, value.dtype) for value in values],
            pltpu.SemaphoreType.DMA((2, len(values))),
        ],
        name="deliver",
    )(*values)


def shards(
    hidden, cotangent, remaining, order,
    norm1_gain, norm1_bias, w_qkv, bias_qv, w_out, bias_out,
    norm2_gain, norm2_bias, w_up, bias_up, w_down, bias_down,
):
    half = hidden.shape[1]
    hbm = pl.BlockSpec(memory_space=pl.ANY)
    swapped = [jnp.transpose(weight, (1, 0, 2)) for weight in (w_qkv, w_out, w_up)]
    wide, deep = (LAYERS, 4, 2, 4, 4, 48, 384), (LAYERS, 2, 4, 4, 4, 48, 384)
    inputs = (
        hidden, cotangent, order, remaining, *swapped, w_down,
        norm1_gain, norm1_bias, bias_qv, bias_out, norm2_gain, norm2_bias, bias_up, bias_down,
    )
    results = [((2, half, D), BF16)] + [
        (shape, F32)
        for shape in (
            (2, half, D), (6, LAYERS, 3 * D), (6, LAYERS, D), (6, LAYERS, FF), (LAYERS, 24, D),
            *[(LAYERS, 6)] * 6, (LAYERS, 12), (LAYERS, 24),
        )
    ]
    staged = [pltpu.VMEM(value.shape, value.dtype) for value in inputs[2:]]
    staged[1] = pltpu.SMEM(remaining.shape, remaining.dtype)
    values = pl.pallas_call(
        kernel,
        out_shape=[jax.ShapeDtypeStruct(*result) for result in results],
        in_specs=[hbm] * len(inputs),
        out_specs=[hbm] * len(results),
        scratch_shapes=[
            *staged,
            *[pltpu.VMEM(*result) for result in results[2:]],
            pltpu.VMEM(wide, BF16),
            pltpu.VMEM(wide, BF16),
            pltpu.VMEM(deep, BF16),
            pltpu.VMEM((4, 4, 4, 48, 384), BF16),
            pltpu.VMEM((4, 4, 4, 48, 384), BF16),
            pltpu.VMEM((3, 3, 3, 4, 4, 16, 384), BF16),
            pltpu.VMEM((LAYERS, 3, 3, 3, 4, 16, 384), BF16),
            pltpu.VMEM((LAYERS, 3, 3, 3, 16, 384), BF16),
            *[pltpu.VMEM((LAYERS, 48, 384), F32) for _ in range(3)],
            pltpu.VMEM((T, D), BF16),
            pltpu.VMEM((T, D), F32),
            pltpu.VMEM((T, D), F32),
            pltpu.VMEM((LAYERS, T, D), BF16),
            pltpu.VMEM((LAYERS, 3, T, D), BF16),
            pltpu.VMEM((LAYERS, HEADS, T, T), BF16),
            pltpu.VMEM((LAYERS, T, D), BF16),
            pltpu.VMEM((LAYERS, T, D), F32),
            pltpu.VMEM((LAYERS, T, D), BF16),
            pltpu.VMEM((LAYERS, 4, T, D), BF16),
            pltpu.VMEM((4, T, D), BF16),
            pltpu.VMEM((T, D), F32),
            pltpu.VMEM((T, D), F32),
            pltpu.VMEM((T, D), BF16),
            pltpu.VMEM((T, D), BF16),
            pltpu.VMEM((T, D), BF16),
            pltpu.VMEM((LAYERS, 16, D), F32),
            pltpu.VMEM((LAYERS, 16, D), F32),
            pltpu.VMEM((16, 128), BF16),
            pltpu.VMEM((8, 16, 128), BF16),
            pltpu.VMEM((4, 4, 16, 128), BF16),
            pltpu.VMEM((4, 16, 128), F32),
            pltpu.VMEM((4, 4, 16, 128), F32),
            pltpu.VMEM((3, 4, 16, 128), F32),
            pltpu.VMEM((3, 16, 128), F32),
            pltpu.VMEM((16, 128), F32),
            pltpu.VMEM((8, 16, 128), F32),
            pltpu.VMEM((8, 32, 384), BF16),
            pltpu.VMEM((8, 32, 384), BF16),
            pltpu.VMEM((2, 48, 384), BF16),
            pltpu.VMEM((2, 48, 384), BF16),
            pltpu.VMEM((3, 48, 384), F32),
            pltpu.VMEM((8, 32, 384), F32),
            pltpu.VMEM((8, 32, 384), F32),
            pltpu.VMEM((2, 48, 384), F32),
            pltpu.VMEM((2, 48, 384), F32),
            pltpu.SemaphoreType.DMA((87,)),
            pltpu.SemaphoreType.DMA((87,)),
            pltpu.SemaphoreType.DMA((18,)),
            pltpu.SemaphoreType.REGULAR((11,)),
        ],
        compiler_params=pltpu.CompilerParams(
            collective_id=0, has_side_effects=True, vmem_limit_bytes=(63 << 20) + (1 << 19)
        ),
        name="layers",
    )(*inputs)
    values = deliver(values)
    out, grad, g_qkv, g_out, g_up, g_down, gain1, off1, b_out, gain2, off2, b_down, b_qv, b_up = values
    g_qkv, g_out, g_up = (jnp.transpose(part, (1, 0, 2)) for part in (g_qkv, g_out, g_up))
    return out, grad, gain1, off1, g_qkv, b_qv, g_out, b_out, gain2, off2, g_up, b_up, g_down, b_down


def solution(mesh):
    tokens, rows = P("dp", "fsdp", None), P(None, ("dp", "fsdp"), None)
    vector = P(None, ("dp", "fsdp"))
    weights = (
        vector, vector, rows, vector, rows, vector, vector, vector, rows, vector, rows, vector
    )
    return jax.shard_map(
        shards,
        mesh=mesh,
        in_specs=(tokens, tokens, P("dp"), P("dp", None), *weights),
        out_specs=(tokens, tokens, *weights),
        check_vma=False,
    )
```

```python
import types

import jax
import jax.numpy as jnp
from jax import lax
from jax.experimental import pallas as pl
from jax.experimental.pallas import tpu as pltpu
from jax.sharding import PartitionSpec as P

HEAD = 64
HEADS = 12
LAYERS = 2
D = 768
FF = 3072
MESH = pl.DeviceIdType.MESH
BF16, F32 = jnp.bfloat16, jnp.float32

AXES = {"q": "yczx", "u": "yczx", "d": "czxy"}
STREAMS = ((slice(0, 16), "xyz"), (slice(16, 32), "yzx"), (slice(32, 48), "zxy"))
KINDS = "qud"
ALL = slice(None)
STEPS = (1, 3, 2)


def place():
    dp, core = lax.axis_index("dp"), lax.axis_index("fsdp")
    return {"z": dp // 16, "x": (dp // 4) % 4, "y": dp % 4, "c": core}


def device(at):
    return ((at["z"] * 4 + at["x"]) * 4 + at["y"], at["c"])


def moved(at, axis, step):
    size = 2 if axis == "c" else 4
    return {**at, axis: (at[axis] + step) % size}


class Batch:
    def __init__(self, links, whole):
        self.links, self.whole = links, whole
        self.number = links.batches
        links.batches += 1
        links.open.append(self)

    def copy(self, src, dst, target):
        return pltpu.make_async_remote_copy(
            src_ref=src,
            dst_ref=dst,
            send_sem=self.links.send_sems.at[self.number],
            recv_sem=self.links.recv_sems.at[self.number],
            device_id=device(target),
            device_id_type=MESH,
        )

    def send(self, src, dst, target):
        self.copy(src, dst, target).start()

    def all(self):
        return self.copy(self.whole, self.whole, self.links.sibling)

    def wait(self):
        self.all().wait_recv()


class Links:
    def __init__(self, me, send_sems, recv_sems):
        self.sibling = moved(me, "c", 1)
        self.send_sems, self.recv_sems, self.open, self.batches = send_sems, recv_sems, [], 0

    def send(self, src, dst, target):
        batch = Batch(self, src)
        batch.send(src, dst, target)
        return batch

    def so_far(self):
        batches, self.open = self.open, []
        return batches

    def drain(self, batches):
        for batch in batches:
            batch.all().wait_send()


def greet(me):
    partners = [moved(moved(me, "y", dy), "c", dc) for dy in range(4) for dc in range(2)][1:]
    partners += [moved(me, axis, step) for axis in "xz" for step in (1, 2, 3)]
    barrier = pltpu.get_barrier_semaphore()
    for partner in partners:
        pl.semaphore_signal(barrier, inc=1, device_id=device(partner), device_id_type=MESH)
    return len(partners)


T = 256
ROWS = 128
GAIN1, OFF1, BIAS_Q, BIAS_OUT, GAIN2, OFF2, BIAS_UP, BIAS_DOWN = 0, 1, 2, 5, 6, 7, 8, 12


def dot(a, b):
    return jnp.dot(a, b, preferred_element_type=F32)


def dot_nt(a, b):
    return lax.dot_general(a, b, (((1,), (1,)), ((), ())), preferred_element_type=F32)


def dot_tn(a, b):
    return lax.dot_general(a, b, (((0,), (0,)), ((), ())), preferred_element_type=F32)


def slab(ref, layer, index):
    return jnp.concatenate([ref[layer, index, core].reshape(D, 384) for core in range(2)], axis=1)


def chunk(ref, layer, index):
    return jnp.concatenate([ref[layer, core, index].reshape(D, 384) for core in range(2)], axis=1)


def put_slab(ref, layer, index, value):
    for core in range(2):
        ref[layer, index, core] = value[:, core * 384 : (core + 1) * 384].reshape(4, 4, 48, 384)


def put_chunk(ref, layer, index, value):
    for core in range(2):
        ref[layer, core, index] = value[:, core * 384 : (core + 1) * 384].reshape(4, 4, 48, 384)


def rows_of(index):
    return pl.ds(pl.multiple_of(index * ROWS, ROWS), ROWS)


def normal(x):
    center = x - jnp.mean(x, axis=-1, keepdims=True)
    scale = lax.rsqrt(jnp.mean(center * center, axis=-1, keepdims=True) + 1e-05)
    return center * scale, scale


def norm_into(x_ref, vec, gain, offset, out_ref):
    @pl.loop(0, T // ROWS)
    def _(index):
        rows = rows_of(index)
        hat, _ = normal(x_ref[rows, :].astype(F32))
        out_ref[rows, :] = (hat * vec[gain : gain + 1, :] + vec[offset : offset + 1, :]).astype(BF16)


def fold(value):
    return jnp.sum(value.reshape(ROWS // 8, 8, value.shape[1]), axis=0)


def total(value):
    return jnp.sum(value, axis=0, keepdims=True)


def norm_back(x_ref, grad_ref, vec, sums, gain, offset, top_ref, out_ref, bias=None, low_ref=None):
    zero = jnp.zeros((8, D), F32)

    def body(index, carry):
        sum_gain, sum_offset, sum_bias = carry
        rows = rows_of(index)
        hat, scale = normal(x_ref[rows, :].astype(F32))
        grad = grad_ref[rows, :]
        scaled = grad * vec[gain : gain + 1, :]
        inner = scaled - jnp.mean(scaled, axis=-1, keepdims=True)
        inner -= hat * jnp.mean(scaled * hat, axis=-1, keepdims=True)
        result = top_ref[rows, :] + scale * inner
        out_ref[rows, :] = result
        low = result.astype(BF16)
        if low_ref is not None:
            low_ref[rows, :] = low
        return sum_gain + fold(grad * hat), sum_offset + fold(grad), sum_bias + fold(low.astype(F32))

    sum_gain, sum_offset, sum_bias = lax.fori_loop(0, T // ROWS, body, (zero, zero, zero))
    sums[gain : gain + 1, :] = total(sum_gain)
    sums[offset : offset + 1, :] = total(sum_offset)
    if bias is not None:
        sums[bias : bias + 1, :] = total(sum_bias)


def gelu_parts(u):
    inner = 0.7978845608028654 * (u + 0.044715 * u * u * u)
    t = jnp.tanh(inner)
    slope = 0.7978845608028654 * (1.0 + 0.134145 * u * u)
    half = 0.5 * (1.0 + t)
    return u * half, half + 0.5 * u * (1.0 - t * t) * slope


def gelu(u):
    return 0.5 * u * (1.0 + jnp.tanh(0.7978845608028654 * (u + 0.044715 * u * u * u)))


def head_mask(which, scale=1.0):
    lane = lax.broadcasted_iota(jnp.int32, (1, 128), 1)
    return jnp.where(lane // HEAD == which, scale, 0.0).astype(BF16)


def lanes_of(pair):
    return pl.ds(pl.multiple_of(pair * 128, 128), 128)


def forward_qkv(layer, m):
    norm_into(m.x[layer], m.vec.at[layer], GAIN1, OFF1, m.h.at[layer])

    @pl.loop(0, 3)
    def _(part):
        bias = m.vec[layer, pl.ds(BIAS_Q + part, 1), :]
        m.qkv[layer, part] = (dot(m.h[layer], slab(m.wq, layer, part)) + bias).astype(BF16)


def forward_attention(layer, m):
    @pl.loop(0, HEADS // 2)
    def _(pair):
        lanes = lanes_of(pair)
        query, keys, values = (m.qkv[layer, part, :, lanes] for part in range(3))
        attended = jnp.zeros((T, 128), F32)
        for which in range(2):
            scores = dot_nt(query * head_mask(which, 0.125), keys)
            grown = jnp.exp(scores - jnp.max(scores, axis=-1, keepdims=True))
            probs = grown * (1.0 / jnp.sum(grown, axis=-1, keepdims=True))
            probs = probs.astype(BF16)
            m.probs[layer, 2 * pair + which] = probs
            attended += dot(probs, values * head_mask(which))
        m.o[layer, :, lanes] = attended.astype(BF16)


def forward_out(layer, m):
    m.mid[layer] = (
        m.x[layer][...].astype(F32)
        + dot(m.o[layer], slab(m.wq, layer, 3))
        + m.vec[layer, BIAS_OUT : BIAS_OUT + 1, :]
    )
    norm_into(m.mid.at[layer], m.vec.at[layer], GAIN2, OFF2, m.h2.at[layer])


def forward_up(layer, m):
    @pl.loop(0, 4)
    def _(index):
        bias = m.vec[layer, pl.ds(BIAS_UP + index, 1), :]
        u = dot(m.h2[layer], slab(m.wu, layer, index)) + bias
        m.u[layer, index] = u.astype(BF16)
        m.a[index] = gelu(u).astype(BF16)


def forward_down(layer, m):
    out = m.x[layer + 1]
    out[...] = m.mid[layer] + m.vec[layer, BIAS_DOWN : BIAS_DOWN + 1, :]

    @pl.loop(0, 4)
    def _(index):
        out[...] += dot(m.a[index], chunk(m.wd, layer, index))


def forward_last(layer, m, out):
    for core in range(2):
        columns = slice(384 * core, 384 * core + 384)
        value = m.mid[layer, :, columns] + m.vec[layer, BIAS_DOWN : BIAS_DOWN + 1, columns]
        for index in range(4):
            value += dot(m.a[index], m.wd[layer, core, index].reshape(D, 384))
        out[:, columns] = value.astype(BF16)


def backward_down(layer, m, index):
    for core, ref in ((m.me["c"], m.top_down), (1 - m.me["c"], m.got_qu)):
        columns = pl.ds(pl.multiple_of(384 * core, 128), 384)
        value = dot_tn(m.a[index], m.gz[:, columns])
        ref[index] = value.astype(BF16).reshape(4, 4, 48, 384)


def backward_ffn(layer, m, index):
    grad_active = dot_nt(m.gz[...], chunk(m.wd, layer, index))
    active, slope = gelu_parts(m.u[layer, index].astype(F32))
    pre = (grad_active * slope).astype(BF16)
    gu = m.gu[layer]
    gu[...] = pre
    m.sums[layer, pl.ds(BIAS_UP + index, 1), :] = total(pre.astype(F32))
    m.gh[...] += dot_nt(gu[...], slab(m.wu, layer, index))
    if layer == 0:
        m.a[0] = active.astype(BF16)
        put_chunk(m.wd, layer, index, dot_tn(m.a[0], m.gz[...]).astype(BF16))
    put_slab(m.wu, layer, index, dot_tn(m.h2[layer], gu[...]).astype(BF16))


def backward_mid(layer, m):
    norm_back(
        m.mid.at[layer], m.gh, m.vec.at[layer], m.sums.at[layer], GAIN2, OFF2, m.g, m.g, BIAS_OUT, m.gz
    )
    m.go[...] = dot_nt(m.gz[...], slab(m.wq, layer, 3)).astype(BF16)
    put_slab(m.wq, layer, 3, dot_tn(m.o[layer], m.gz[...]).astype(BF16))


def backward_attention(layer, m):
    @pl.loop(0, HEADS // 2)
    def _(pair):
        lanes = lanes_of(pair)
        query, keys, values = (m.qkv[layer, part, :, lanes] for part in range(3))
        grad = m.go[:, lanes]
        zero = jnp.zeros((T, 128), F32)
        grad_query, grad_keys, grad_values = zero, zero, zero
        for which in range(2):
            low = m.probs[layer, 2 * pair + which]
            probs = low.astype(F32)
            part = grad * head_mask(which)
            grad_probs = dot_nt(part, values)
            grad_values += dot_tn(low, part)
            row_dot = jnp.sum(grad_probs * probs, axis=-1, keepdims=True)
            grad_scores = (probs * (grad_probs - row_dot)).astype(BF16)
            grad_query += dot(grad_scores, keys * head_mask(which, 0.125))
            grad_keys += dot_tn(grad_scores, query * head_mask(which, 0.125))
        for part, value in enumerate((grad_query, grad_keys, grad_values)):
            m.gqkv[part, :, lanes] = value.astype(BF16)


def backward_qkv(layer, m, part):
    m.sums[layer, pl.ds(BIAS_Q + part, 1), :] = total(m.gqkv[part].astype(F32))
    m.gh[...] += dot_nt(m.gqkv[part], slab(m.wq, layer, part))
    put_slab(m.wq, layer, part, dot_tn(m.h[layer], m.gqkv[part]).astype(BF16))


def backward_in(layer, m, out_ref):
    norm_back(m.x[layer], m.gh, m.vec.at[layer], m.sums.at[layer], GAIN1, OFF1, m.g, out_ref)


def upstream(order_ref, remaining_ref, cot_ref, m):
    live = lax.broadcasted_iota(jnp.int32, (1, T), 1) >= T - remaining_ref

    def body(index, carry):
        rows = rows_of(index)
        spot = index * ROWS + lax.broadcasted_iota(jnp.int32, (ROWS, 1), 0)
        hit = jnp.where((order_ref == spot) & live, 1.0, 0.0)
        mask = jnp.max(hit, axis=-1, keepdims=True)
        grad = cot_ref[rows, :].astype(F32) * mask
        m.g[rows, :] = grad
        return carry

    lax.fori_loop(0, T // ROWS, body, 0)


def top(layer, m):
    def body(index, carry):
        rows = rows_of(index)
        low = m.g[rows, :].astype(BF16)
        m.gz[rows, :] = low
        return carry + fold(low.astype(F32))

    sums = lax.fori_loop(0, T // ROWS, body, jnp.zeros((8, D), F32))
    m.sums[layer, BIAS_DOWN : BIAS_DOWN + 1, :] = total(sums)
    m.gh[...] = jnp.zeros((T, D), F32)


class Gather:
    def __init__(self, kind, layer, m):
        self.kind, self.layer, self.m = kind, layer, m
        sizes = m.wq.at[0]
        self.handed = Batch(m.links, sizes.at[:, 0])
        self.one = Batch(m.links, sizes.at[0, 0, 0, pl.ds(0, 3)])
        self.ring = (kind, layer) != ("q", 0)
        self.two = Batch(m.links, sizes.at[0, 0, pl.ds(0, 2 if self.ring else 3)])
        self.two_halves = Batch(m.links, sizes.at[0, 0, 0]) if self.ring else None
        self.three = Batch(m.links, sizes.at[pl.ds(0, 2), 0])
        self.halves = Batch(m.links, sizes.at[0, 0])

    def part(self, rows, at):
        index = tuple(at[axis] for axis in AXES[self.kind])
        return self.m.weights[self.kind].at[(self.layer, *index, rows, ALL)]

    def hand_over(self, rows, at):
        part = self.part(rows, at)
        self.handed.send(part, part, self.m.links.sibling)

    def out(self, batch, rows, at, axis, steps):
        part = self.part(rows, at)
        for step in steps:
            batch.send(part, part, moved(self.m.me, axis, step))

    def first(self):
        for rows, axes in STREAMS:
            self.out(self.one, rows, self.m.me, axes[0], STEPS)

    def second(self):
        self.one.wait()
        for rows, axes in STREAMS:
            steps = (1, 3) if self.ring else STEPS
            self.out(self.two, rows, {**self.m.me, axes[0]: ALL}, axes[1], steps)

    def relay_two(self):
        self.two.wait()
        for rows, axes in STREAMS:
            for step in (1, 3):
                came = {**moved(self.m.me, axes[1], -step), axes[0]: pl.ds(step - 1, 2)}
                self.out(self.two_halves, rows, came, axes[1], (step,))

    def third(self):
        (self.two_halves if self.ring else self.two).wait()
        planes = [
            (rows, axes, {**self.m.me, axes[0]: ALL, axes[1]: ALL}) for rows, axes in STREAMS
        ]
        for rows, axes, plane in planes:
            self.out(self.three, rows, plane, axes[2], (1, 3))
        for rows, axes, plane in planes:
            self.hand_over(rows, plane)

    def relay(self):
        self.three.wait()
        came = [
            (rows, axes, step, {**moved(self.m.me, axes[2], -step), axes[0]: ALL, axes[1]: ALL})
            for rows, axes in STREAMS
            for step in (1, 3)
        ]
        for rows, axes, step, at in came:
            self.out(self.halves, rows, {**at, axes[0]: pl.ds(step - 1, 2)}, axes[2], (step,))
        for rows, axes, step, at in came:
            self.hand_over(rows, at)

    def finish(self):
        self.halves.wait()
        for rows, axes in STREAMS:
            self.hand_over(rows, {**moved(self.m.me, axes[2], 2), axes[0]: ALL, axes[1]: ALL})

    def arrive(self):
        self.handed.wait()


class Scatter:
    def __init__(self, kind, layer, m):
        self.kind, self.layer, self.m = kind, layer, m
        self.slow = "z" if kind == "d" else "y"
        number = KINDS.index(kind)
        self.streams = []
        for stream, (rows, axes) in enumerate(STREAMS):
            others = [axis for axis in AXES[kind] if axis not in ("c", axes[2])]
            slots = m.first.at[number, stream]
            later = (m.second.at[layer, number, stream], m.third.at[layer, number, stream])
            free = m.free.at[3 * number + stream]
            self.streams.append((rows, axes[::-1], others, slots, *later, free))
        sizes = m.wq.at[0]
        self.shared = [Batch(m.links, sizes.at[pl.ds(0, 2), 0]) for _ in range(2)]
        self.passing, self.direct, self.passed = (Batch(m.links, sizes.at[0, 0]) for _ in range(3))
        self.two = Batch(m.links, sizes.at[0, 0, pl.ds(0, 3)])
        self.one = Batch(m.links, sizes.at[0, 0, 0, pl.ds(0, 3)])
        self.room, self.got = (m.free.at[9], m.got_d) if kind == "d" else (m.free.at[10], m.got_qu)

    def part(self, rows, at):
        if self.kind == "d" and self.layer == 1:
            return self.m.top_down.at[(*(at.get(axis, ALL) for axis in "zxy"), rows, ALL)]
        index = tuple(at.get(axis, ALL) for axis in AXES[self.kind])
        return self.m.weights[self.kind].at[(self.layer, *index, rows, ALL)]

    def share(self, index, half):
        sibling = self.m.links.sibling
        if self.kind == "d" and self.layer == 1:
            src = self.m.got_qu.at[index]
        else:
            src = self.part(ALL, {self.slow: index, "c": sibling["c"]})
        self.shared[half].send(src, self.got.at[index], sibling)

    def wait_room(self):
        pl.semaphore_wait(self.room, 1)

    def give_room(self):
        sibling = device(self.m.links.sibling)
        pl.semaphore_signal(self.room, inc=1, device_id=sibling, device_id_type=MESH)

    def join(self, half):
        other = "x" if self.kind == "d" else "z"
        self.shared[half].wait()

        @pl.loop(8 * half, 8 * half + 8)
        def _(spot):
            own = self.part(ALL, {self.slow: spot // 4, other: spot % 4, "c": self.m.me["c"]})
            own[...] += self.got[spot // 4, spot % 4]

    def leave(self, half):
        ready = []
        for rows, axes, others, slots, _, _, free in self.streams:
            split = others[0] == self.slow
            if self.layer == 0 and half == (0 if split else 1):
                pl.semaphore_wait(free, 2)
            for now in (half,) if split else (0, 1) if half else ():
                ready.append((rows, axes[0], others[0], slots, now))
        for now in ready:
            self.pass_on(*now)
        for now in ready:
            self.go(*now)

    def pass_on(self, rows, axis, split, slots, half):
        me, halves = self.m.me, pl.ds(2 * half, 2)
        src = self.part(rows, {"c": me["c"], split: halves, axis: moved(me, axis, 2)[axis]})
        self.passing.send(src, slots.at[2, halves], moved(me, axis, 1 + 2 * half))

    def go(self, rows, axis, split, slots, half):
        me, halves = self.m.me, pl.ds(2 * half, 2)
        target = moved(me, axis, 3 - 2 * half)
        src = self.part(rows, {"c": me["c"], split: halves, axis: target[axis]})
        self.direct.send(src, slots.at[1 - half, halves], target)

    def relay(self):
        me = self.m.me
        self.passing.wait()
        for rows, axes, others, slots, _, _, _ in self.streams:
            for half in range(2):
                target = moved(me, axes[0], 1 + 2 * half)
                spot = {"c": me["c"], axes[0]: target[axes[0]]}
                for index in (2 * half, 2 * half + 1):
                    own = self.part(rows, {**spot, others[0]: index})
                    own[...] += slots[2, index]
                halves = pl.ds(2 * half, 2)
                src = self.part(rows, {**spot, others[0]: halves})
                self.passed.send(src, slots.at[half, halves], target)

    def add(self, target, slots):
        value = target[...].astype(F32)
        for slot in slots:
            value += slot[...].astype(F32)
        return value

    def second(self):
        m, me = self.m, self.m.me
        self.direct.wait()
        self.passed.wait()
        for rows, axes, others, slots, later, _, free in self.streams:
            here = {"c": me["c"], axes[0]: me[axes[0]]}

            @pl.loop(0, 4)
            def _(index):
                target = self.part(rows, {**here, others[0]: index})
                total = self.add(target, [slots.at[side, index] for side in range(2)])
                target[...] = total.astype(BF16)

            if self.layer == 1:
                for step in (1, 3):
                    peer = device(moved(me, axes[0], step))
                    pl.semaphore_signal(free, inc=1, device_id=peer, device_id_type=MESH)
            for step in STEPS:
                target = moved(me, axes[1], step)
                src = self.part(rows, {**here, axes[1]: target[axes[1]]})
                self.two.send(src, later.at[step - 1], target)

    def third(self):
        m, me = self.m, self.m.me
        self.two.wait()
        for rows, axes, _, _, later, last, _ in self.streams:
            here = {"c": me["c"], axes[0]: me[axes[0]], axes[1]: me[axes[1]]}
            target = self.part(rows, here)
            target[...] = self.add(target, [later.at[step] for step in range(3)]).astype(BF16)
            for step in STEPS:
                target = moved(me, axes[2], step)
                src = self.part(rows, {**here, axes[2]: target[axes[2]]})
                self.one.send(src, last.at[step - 1], target)

    def finish(self):
        self.one.wait()
        for rows, _, _, _, _, last, _ in self.streams:
            total = self.add(self.part(rows, self.m.me), [last.at[step] for step in range(3)])
            self.m.totals[self.kind][self.layer, rows, :] = total


TILE_PAIRS = ((GAIN1, OFF1), (BIAS_OUT, GAIN2), (OFF2, BIAS_DOWN))
NARROW_ROWS = tuple(row for pair in TILE_PAIRS for row in pair)


def spot_matrix(base, width):
    row = lax.broadcasted_iota(jnp.int32, (128, 128), 0)
    lane = lax.broadcasted_iota(jnp.int32, (128, 128), 1)
    return jnp.where((lane == base + row) & (row < width), 1.0, 0.0).astype(BF16)


def spot_matrices(member):
    return (
        spot_matrix(6 * member, 6), spot_matrix(48 + 6 * member, 6),
        spot_matrix(12 * member, 12), spot_matrix(24 * (member % 4), 24),
    )


def flag(condition):
    return jnp.where(condition, 1.0, 0.0).astype(F32)


def vector_tile(member, narrow, wide_qv, wide_up, stage):
    stage[...] = jnp.zeros(stage.shape, F32)
    for layer in range(LAYERS):
        rows = slice(layer, layer + 1)
        for number, vector in enumerate(narrow):
            row = 8 * layer + number // 2
            stage[number % 2, row : row + 1, 0:6] = vector[rows, :].astype(F32)
        row = 8 * layer + 3
        stage[2, row : row + 1, 0:12] = wide_qv[rows, :].astype(F32)
        for half in range(2):
            up = wide_up[rows, :].astype(F32) * flag(member // 4 == half)
            stage[3, row + 1 + half : row + 2 + half, 0:24] = up
    total = jnp.zeros((16, 128), F32)
    for number, matrix in enumerate(spot_matrices(member)):
        total += dot(stage[number].astype(BF16), matrix)
    return total.astype(BF16)


def whole_vectors(tiles, vec):
    tiles = [tiles[index // 4, index % 4].astype(F32) for index in range(16)]

    def joined(row, first, last, groups):
        return jnp.concatenate([tiles[group][row : row + 1, first:last] for group in groups], axis=1)

    for layer in range(LAYERS):
        vec[layer] = jnp.zeros((16, D), F32)
        for number, pair in enumerate(TILE_PAIRS):
            for side, row in enumerate(pair):
                value = joined(8 * layer + number, 48 * side, 48 * side + 48, range(16))
                vec[layer, row : row + 1, :] = value
        for side in range(2):
            value = joined(8 * layer + 3, 0, 96, range(8 * side, 8 * side + 8))
            vec[layer, BIAS_Q + 2 * side : BIAS_Q + 2 * side + 1, :] = value
        for part in range(4):
            pieces = []
            for group in range(4 * part, 4 * part + 4):
                for half in range(2):
                    row = 8 * layer + 4 + half
                    pieces.append(tiles[group][row : row + 1, 0:96])
            value = jnp.concatenate(pieces, axis=1)
            vec[layer, BIAS_UP + part : BIAS_UP + part + 1, :] = value


def vector_tiles(sums, tiles):
    tiles[...] = jnp.zeros(tiles.shape, F32)
    for layer in range(LAYERS):
        for group in range(16):
            spot = tiles.at[group // 4, group % 4]
            for number, pair in enumerate(TILE_PAIRS):
                for side, row in enumerate(pair):
                    value = sums[layer, row : row + 1, 48 * group : 48 * group + 48]
                    at = 8 * layer + number
                    spot[at : at + 1, 48 * side : 48 * side + 48] = value
            row, start = BIAS_Q + 2 * (group // 8), 96 * (group % 8)
            at = 8 * layer + 3
            spot[at : at + 1, 0:96] = sums[layer, row : row + 1, start : start + 96]
            row, start = BIAS_UP + group // 4, 192 * (group % 4)
            for half in range(2):
                first = start + 96 * half
                value = sums[layer, row : row + 1, first : first + 96]
                spot[at + 1 + half : at + 2 + half, 0:96] = value


def own_entries(member, value, out):
    high = value.astype(BF16)
    middle = (value - high.astype(F32)).astype(BF16)
    low = (value - high.astype(F32) - middle.astype(F32)).astype(BF16)
    found = [
        dot_nt(high, matrix) + (dot_nt(middle, matrix) + dot_nt(low, matrix))
        for matrix in spot_matrices(member)
    ]
    for layer in range(LAYERS):
        rows = slice(layer, layer + 1)
        for number in range(6):
            row = 8 * layer + number // 2
            out[number][rows, :] = found[number % 2][row : row + 1, 0:6]
        row = 8 * layer + 3
        out[6][rows, :] = found[2][row : row + 1, 0:12]
        up = found[3][row + 1 : row + 2] * flag(member // 4 == 0)
        up += found[3][row + 2 : row + 3] * flag(member // 4 == 1)
        out[7][rows, :] = up[:, 0:24]


def kernel(*refs):
    inputs, refs = refs[:16], refs[16:]
    outputs, refs = refs[:14], refs[14:]
    staged, refs = refs[:14], refs[14:]
    ready, refs = refs[:12], refs[12:]
    (
        wq, wu, wd, got_qu, got_d, top_down, first, second, third, sum_q, sum_u, sum_d,
        x0, x1, h, qkv, probs, o, mid, h2, u, tmp, g, gh, gz, cots, vec, sums,
        vec_out, vec_in, vec_all, stage, sum_all, sum_in, sum_next, sum_out, sum_got,
        send_a, recv_a, send_d, recv_d, send_f, recv_f, send_df, recv_df,
        send_sems, recv_sems, local_sems, free,
    ) = refs
    hidden, cot = inputs[:2]
    out, grad = outputs[:2]
    order, remaining, w_qkv, w_out, w_up, w_down, *vectors_in = staged
    gain1, off1, bias_qv, bias_out, gain2, off2, bias_up, bias_down = vectors_in
    g_qkv, g_out, g_up, g_down, *vectors_out = ready
    me = place()
    partners = greet(me)
    loads = []
    for number, (src, dst) in enumerate(zip(inputs[2:], staged)):
        loads.append(pltpu.make_async_copy(src, dst, local_sems.at[4 + number]))
        loads[-1].start()
    sibling = moved(me, "c", 1)
    mine = 2 * me["y"] + me["c"]
    links = Links(me, send_sems, recv_sems)
    m = types.SimpleNamespace(
        me=me, links=links, weights={"q": wq, "u": wu, "d": wd}, wq=wq, wu=wu, wd=wd,
        got_qu=got_qu, got_d=got_d, free=free, totals={"q": sum_q, "u": sum_u, "d": sum_d},
        first=first, second=second, third=third,
        x=[x0, x1], h=h, qkv=qkv, probs=probs, o=o, mid=mid, h2=h2, u=u, a=tmp, g=g, gh=gh, gz=gz,
        gu=[tmp.at[1], cots], top_down=top_down, go=tmp.at[3], gqkv=tmp, vec=vec, sums=sums,
    )
    send_f[...] = jnp.zeros(send_f.shape, F32)
    for copy in loads:
        copy.wait()

    for owner in range(8):
        columns = slice(384 * (owner % 2), 384 * (owner % 2) + 384)
        for layer in range(LAYERS):
            for row in range(6):
                if owner < 6:
                    part = w_qkv[row, layer : layer + 1, 384 * owner : 384 * owner + 384]
                else:
                    part = w_out[row, layer : layer + 1, columns]
                send_f[owner, 8 * layer + row : 8 * layer + row + 1, :] = part.astype(F32)
                part = w_up[row, layer : layer + 1, 384 * owner : 384 * owner + 384]
                send_f[owner, 16 + 8 * layer + row : 17 + 8 * layer + row, :] = part.astype(F32)
    for owner in range(8):
        send_a[owner] = send_f[owner].astype(BF16)
    for half in range(2):
        for layer in range(LAYERS):
            part = w_down[layer, :, 384 * half : 384 * half + 384]
            send_df[half, 24 * layer : 24 * layer + 24, :] = part.astype(F32)
        send_d[half] = send_df[half].astype(BF16)
    narrow = (gain1, off1, bias_out, gain2, off2, bias_down)
    vec_out[...] = vector_tile(mine, narrow, bias_qv, bias_up, stage)

    pl.semaphore_wait(pltpu.get_barrier_semaphore(), partners)

    def group_sends(src, dst, rows=ALL):
        batch = Batch(links, dst.at[pl.ds(0, 7), rows])
        for dy in range(4):
            for dc in range(2):
                if dy or dc:
                    target = moved(moved(me, "y", dy), "c", dc)
                    spot = src.at[2 * target["y"] + target["c"], rows]
                    batch.send(spot, dst.at[mine, rows], target)
        return batch

    def group_tiles(src, dst):
        batch = Batch(links, dst.at[pl.ds(0, 7)])
        for dy in range(4):
            for dc in range(2):
                if dy or dc:
                    batch.send(src, dst.at[mine], moved(moved(me, "y", dy), "c", dc))
        return batch

    arrivals = [group_tiles(vec_out, vec_in), group_sends(send_a, recv_a)]
    arrivals.append(links.send(send_d.at[1 - me["c"]], recv_d.at[me["c"]], sibling))
    recv_a[mine] = send_a[mine]
    recv_d[me["c"]] = send_d[me["c"]]
    vec_in[mine] = vec_out[...]
    here = pl.ds(pl.multiple_of(128 * me["c"], 128), 128)
    there = pl.ds(pl.multiple_of(128 * (1 - me["c"]), 128), 128)
    halves = []
    for number, (src, dst) in enumerate(((hidden, x0), (cot, cots))):
        halves.append(links.send(src.at[1 - me["c"]], dst.at[here, :], sibling))
        copy = pltpu.make_async_copy(src.at[me["c"]], dst.at[here, :], local_sems.at[number])
        copy.start()
        halves.append(copy)
    for batch in arrivals:
        batch.wait()
    gathers = [Gather(kind, layer, m) for layer in range(LAYERS) for kind in KINDS]
    own = (me["y"], me["c"], me["z"], me["x"])
    tile = jnp.zeros((16, 128), F32)
    for source in range(8):
        tile += vec_in[source].astype(F32)
    vec_all[me["z"], me["x"]] = tile.astype(BF16)
    spot = vec_all.at[me["z"], me["x"]]
    along_z = Batch(links, vec_all.at[0, pl.ds(0, 3)])
    for step in STEPS:
        along_z.send(spot, spot, moved(me, "z", step))

    def prepare(layer):
        for group, target in enumerate((wq, wu)):
            for source in range(8):
                rows = slice(16 * group + 8 * layer, 16 * group + 8 * layer + 6)
                sum_q[group, 6 * source : 6 * source + 6, :] = recv_a[source].astype(F32)[rows]
            target[(layer, *own)] = sum_q[group].astype(BF16)
            gathers[3 * layer + group].first()
        for half in range(2):
            sum_d[0, 24 * half : 24 * half + 24, :] = recv_d[half].astype(F32)[
                24 * layer : 24 * layer + 24
            ]
        wd[layer, me["c"], me["z"], me["x"], me["y"]] = sum_d[0].astype(BF16)
        gathers[3 * layer + 2].first()

    prepare(0)
    q0, u0, d0, q1, u1, d1 = gathers
    q0.second()
    along_z.wait()
    column = vec_all.at[:, me["x"]]
    along_x = Batch(links, vec_all.at[pl.ds(0, 3)])
    for step in STEPS:
        along_x.send(column, column, moved(me, "x", step))
    u0.second()
    q0.third()
    u0.relay_two()
    d0.second()
    prepare(1)
    u0.third()
    along_x.wait()
    whole_vectors(vec_all, vec)
    d0.relay_two()
    q1.second()
    q0.relay()
    d0.third()
    q1.relay_two()
    u1.second()
    d1.second()
    q0.finish()
    u0.relay()
    q1.third()
    halves[0].wait()
    halves[1].wait()
    q0.arrive()

    forward_qkv(0, m)
    u1.relay_two()
    d1.relay_two()
    u0.finish()
    d0.relay()
    u1.third()
    forward_attention(0, m)
    u0.arrive()
    d0.finish()
    q1.relay()
    d1.third()
    forward_out(0, m)
    forward_up(0, m)
    d0.arrive()
    forward_down(0, m)
    q1.finish()
    u1.relay()
    halves[2].wait()
    halves[3].wait()
    upstream(order[pl.ds(me["c"], 1), :], remaining[me["c"]], cots, m)
    sums[...] = jnp.zeros(sums.shape, F32)
    top(1, m)
    q1.arrive()
    forward_qkv(1, m)
    u1.finish()
    forward_attention(1, m)
    d1.relay()
    forward_out(1, m)
    u1.arrive()
    forward_up(1, m)
    gathered = links.so_far()
    scatters = {(kind, layer): Scatter(kind, layer, m) for layer in (1, 0) for kind in KINDS}

    def steps(*plan):
        for word in plan:
            name, step, *given = word.split(".")
            getattr(scatters[name[0], int(name[1])], step)(*map(int, given))

    @pl.loop(0, 4)
    def _(part):
        backward_down(1, m, part)
        for now in range(4):

            @pl.when(part == now)
            def _():
                scatters["d", 1].share(now, now // 2)

    d1.finish()
    steps("d1.join.0", "d1.leave.0", "d1.join.1", "d1.leave.1")
    links.drain(scatters["d", 1].shared)
    steps("u1.give_room")
    d1.arrive()
    links.drain(gathered)

    def swap(src, dst, number):
        remote = links.send(src.at[there, :], dst.at[me["c"]], sibling)
        copy = pltpu.make_async_copy(src.at[here, :], dst.at[me["c"]], local_sems.at[number])
        copy.start()
        return remote, copy

    def ffn(layer, *plans):
        groups = [scatters[kind, layer] for kind in ("u" if layer else "ud")]
        for group in groups:
            group.wait_room()

        @pl.loop(0, 4)
        def _(part):
            backward_ffn(layer, m, part)
            for now in range(4):

                @pl.when(part == now)
                def _():
                    for group in groups:
                        group.share(now, now // 2)
                    steps(*plans[now])

    def attention_grads(layer):
        scatter = scatters["q", layer]
        scatter.wait_room()
        scatter.share(3, 1)
        m.gh[...] = jnp.zeros((T, D), F32)

        @pl.loop(0, 3)
        def _(part):
            backward_qkv(layer, m, part)

            @pl.when(part < 2)
            def _():
                scatter.share(part, 0)

            @pl.when(part == 2)
            def _():
                scatter.share(2, 1)
                scatter.join(0)
                scatter.leave(0)

    ffn(1, (), (), ("u1.join.0", "u1.leave.0"), ())
    forward_last(1, m, cots)
    results = [swap(cots, out, 2)]
    steps("u1.join.1", "u1.leave.1", "u1.give_room", "d1.give_room", "d1.relay")
    backward_mid(1, m)
    backward_attention(1, m)
    steps("u1.relay")
    attention_grads(1)
    steps("d1.second")
    backward_in(1, m, g)
    top(0, m)
    steps("q1.join.1", "q1.give_room", "q1.leave.1", "u1.second")
    ffn(
        0, (), ("d1.third",), ("q1.relay", "u0.join.0", "u0.leave.0"), ("d0.join.0", "d0.leave.0")
    )
    backward_mid(0, m)
    steps("u0.join.1", "u0.leave.1", "u0.give_room", "d0.join.1", "d0.leave.1", "u1.third")
    backward_attention(0, m)
    steps("q1.second", "u0.relay")
    attention_grads(0)
    steps("d0.relay", "q0.join.1", "q0.leave.1")
    backward_in(0, m, g)
    vector_tiles(sums, sum_all)
    along_z = Batch(links, sum_in)
    for step in STEPS:
        target = moved(me, "z", step)
        along_z.send(sum_all.at[target["z"]], sum_in.at[step - 1], target)
    results.append(swap(g, grad, 3))
    steps("q1.third", "u0.second", "q0.relay", "d0.second")
    along_z.wait()
    for index in range(4):
        row = sum_all[me["z"], index]
        for step in range(3):
            row += sum_in[step, index]
        sum_all[me["z"], index] = row
    along_x = Batch(links, sum_next)
    for step in STEPS:
        target = moved(me, "x", step)
        along_x.send(sum_all.at[me["z"], target["x"]], sum_next.at[step - 1], target)
    steps("u1.finish", "d1.finish", "q1.finish")

    spots = {("q", 1): 0, ("u", 1): 8, ("u", 0): 16, ("q", 0): 24}

    def give_back(rows, *groups):
        for kind, layer in groups:
            start, total = spots[kind, layer], {"q": sum_q, "u": sum_u}[kind]
            for owner in range(8):
                send_f[owner, start : start + 6, :] = total[layer, 6 * owner : 6 * owner + 6, :]
        return group_sends(send_f, recv_f, rows)

    def give_back_down(layer):
        rows = slice(24 * layer, 24 * layer + 24)
        for owner in range(2):
            send_df[owner, rows, :] = sum_d[layer, 24 * owner : 24 * owner + 24, :]
        recv_df[me["c"], rows, :] = send_df[me["c"], rows, :]
        return links.send(send_df.at[1 - me["c"], rows], recv_df.at[me["c"], rows], sibling)

    def take_back(kind, layer):
        start, wide_out = spots[kind, layer], g_up if kind == "u" else g_qkv
        for owner in range(8):
            columns = slice(384 * owner, 384 * owner + 384)
            target = wide_out
            if kind == "q" and owner >= 6:
                columns, target = slice(384 * (owner - 6), 384 * (owner - 5)), g_out
            for row in range(6):
                value = recv_f[owner, start + row : start + row + 1, :]
                target[row, layer : layer + 1, columns] = value

    early = [give_back(slice(0, 16), ("q", 1), ("u", 1)), give_back_down(1)]
    steps("q0.second", "u0.third", "d0.third")
    along_x.wait()
    tile = sum_all[me["z"], me["x"]]
    for step in range(3):
        tile += sum_next[step]
    sum_out[...] = tile
    tiles = group_tiles(sum_out, sum_got)
    sum_got[mine] = tile
    steps("q0.third", "u0.finish", "d0.finish")
    early += [give_back(slice(16, 24), ("u", 0)), give_back_down(0)]
    steps("q0.finish")
    last = give_back(slice(24, 32), ("q", 0))
    recv_f[mine] = send_f[mine]
    tiles.wait()
    tile = sum_got[0]
    for source in range(1, 8):
        tile += sum_got[source]
    own_entries(mine, tile, vectors_out)
    for batch in early:
        batch.wait()
    for kind, layer in (("q", 1), ("u", 1), ("u", 0)):
        take_back(kind, layer)
    for half in range(2):
        for layer in range(LAYERS):
            g_down[layer, :, 384 * half : 384 * half + 384] = recv_df[
                half, 24 * layer : 24 * layer + 24, :
            ]
    last.wait()
    take_back("q", 0)
    stores = []
    for number, (src, dst) in enumerate(zip(ready, outputs[2:])):
        stores.append(pltpu.make_async_copy(src, dst, local_sems.at[4 + number]))
        stores[-1].start()
    for remote, copy in results:
        remote.wait()
        copy.wait()
    links.drain([batch for batch in links.so_far() if batch not in scatters["d", 1].shared])
    assert links.batches <= 96
    for copy in stores:
        copy.wait()


def deliver_kernel(*refs):
    count = len(refs) // 3
    sources, results, held, sems = refs[:count], refs[count : 2 * count], refs[2 * count : -1], refs[-1]
    loads = [
        pltpu.make_async_copy(src, dst, sems.at[0, number])
        for number, (src, dst) in enumerate(zip(sources, held))
    ]
    stores = [
        pltpu.make_async_copy(src, dst, sems.at[1, number])
        for number, (src, dst) in enumerate(zip(held, results))
    ]
    for copy in loads:
        copy.start()
    for load, store in zip(loads, stores):
        load.wait()
        store.start()
    for copy in stores:
        copy.wait()


def deliver(values):
    hbm = pl.BlockSpec(memory_space=pl.ANY)
    return pl.pallas_call(
        deliver_kernel,
        out_shape=[jax.ShapeDtypeStruct(value.shape, value.dtype) for value in values],
        in_specs=[hbm] * len(values),
        out_specs=[hbm] * len(values),
        scratch_shapes=[
            *[pltpu.VMEM(value.shape, value.dtype) for value in values],
            pltpu.SemaphoreType.DMA((2, len(values))),
        ],
        name="deliver",
    )(*values)


def shards(
    hidden, cotangent, remaining, order,
    norm1_gain, norm1_bias, w_qkv, bias_qv, w_out, bias_out,
    norm2_gain, norm2_bias, w_up, bias_up, w_down, bias_down,
):
    half = hidden.shape[1]
    hbm = pl.BlockSpec(memory_space=pl.ANY)
    swapped = [jnp.transpose(weight, (1, 0, 2)) for weight in (w_qkv, w_out, w_up)]
    wide, deep = (LAYERS, 4, 2, 4, 4, 48, 384), (LAYERS, 2, 4, 4, 4, 48, 384)
    inputs = (
        hidden, cotangent, order, remaining, *swapped, w_down,
        norm1_gain, norm1_bias, bias_qv, bias_out, norm2_gain, norm2_bias, bias_up, bias_down,
    )
    results = [((2, half, D), BF16)] + [
        (shape, F32)
        for shape in (
            (2, half, D), (6, LAYERS, 3 * D), (6, LAYERS, D), (6, LAYERS, FF), (LAYERS, 24, D),
            *[(LAYERS, 6)] * 6, (LAYERS, 12), (LAYERS, 24),
        )
    ]
    staged = [pltpu.VMEM(value.shape, value.dtype) for value in inputs[2:]]
    staged[1] = pltpu.SMEM(remaining.shape, remaining.dtype)
    values = pl.pallas_call(
        kernel,
        out_shape=[jax.ShapeDtypeStruct(*result) for result in results],
        in_specs=[hbm] * len(inputs),
        out_specs=[hbm] * len(results),
        scratch_shapes=[
            *staged,
            *[pltpu.VMEM(*result) for result in results[2:]],
            pltpu.VMEM(wide, BF16),
            pltpu.VMEM(wide, BF16),
            pltpu.VMEM(deep, BF16),
            pltpu.VMEM((4, 4, 4, 48, 384), BF16),
            pltpu.VMEM((4, 4, 4, 48, 384), BF16),
            pltpu.VMEM((4, 4, 4, 48, 384), BF16),
            pltpu.VMEM((3, 3, 3, 4, 4, 16, 384), BF16),
            pltpu.VMEM((LAYERS, 3, 3, 3, 4, 16, 384), BF16),
            pltpu.VMEM((LAYERS, 3, 3, 3, 16, 384), BF16),
            *[pltpu.VMEM((LAYERS, 48, 384), F32) for _ in range(3)],
            pltpu.VMEM((T, D), BF16),
            pltpu.VMEM((T, D), F32),
            pltpu.VMEM((LAYERS, T, D), BF16),
            pltpu.VMEM((LAYERS, 3, T, D), BF16),
            pltpu.VMEM((LAYERS, HEADS, T, T), BF16),
            pltpu.VMEM((LAYERS, T, D), BF16),
            pltpu.VMEM((LAYERS, T, D), F32),
            pltpu.VMEM((LAYERS, T, D), BF16),
            pltpu.VMEM((LAYERS, 4, T, D), BF16),
            pltpu.VMEM((4, T, D), BF16),
            pltpu.VMEM((T, D), F32),
            pltpu.VMEM((T, D), F32),
            pltpu.VMEM((T, D), BF16),
            pltpu.VMEM((T, D), BF16),
            pltpu.VMEM((LAYERS, 16, D), F32),
            pltpu.VMEM((LAYERS, 16, D), F32),
            pltpu.VMEM((16, 128), BF16),
            pltpu.VMEM((8, 16, 128), BF16),
            pltpu.VMEM((4, 4, 16, 128), BF16),
            pltpu.VMEM((4, 16, 128), F32),
            pltpu.VMEM((4, 4, 16, 128), F32),
            pltpu.VMEM((3, 4, 16, 128), F32),
            pltpu.VMEM((3, 16, 128), F32),
            pltpu.VMEM((16, 128), F32),
            pltpu.VMEM((8, 16, 128), F32),
            pltpu.VMEM((8, 32, 384), BF16),
            pltpu.VMEM((8, 32, 384), BF16),
            pltpu.VMEM((2, 48, 384), BF16),
            pltpu.VMEM((2, 48, 384), BF16),
            pltpu.VMEM((8, 32, 384), F32),
            pltpu.VMEM((8, 32, 384), F32),
            pltpu.VMEM((2, 48, 384), F32),
            pltpu.VMEM((2, 48, 384), F32),
            pltpu.SemaphoreType.DMA((96,)),
            pltpu.SemaphoreType.DMA((96,)),
            pltpu.SemaphoreType.DMA((18,)),
            pltpu.SemaphoreType.REGULAR((11,)),
        ],
        compiler_params=pltpu.CompilerParams(
            collective_id=0, has_side_effects=True, vmem_limit_bytes=(63 << 20) + (1 << 19)
        ),
        name="layers",
    )(*inputs)
    values = deliver(values)
    out, grad, g_qkv, g_out, g_up, g_down, gain1, off1, b_out, gain2, off2, b_down, b_qv, b_up = values
    g_qkv, g_out, g_up = (jnp.transpose(part, (1, 0, 2)) for part in (g_qkv, g_out, g_up))
    return out, grad, gain1, off1, g_qkv, b_qv, g_out, b_out, gain2, off2, g_up, b_up, g_down, b_down


def solution(mesh):
    tokens, rows = P("dp", "fsdp", None), P(None, ("dp", "fsdp"), None)
    vector = P(None, ("dp", "fsdp"))
    weights = (
        vector, vector, rows, vector, rows, vector, vector, vector, rows, vector, rows, vector
    )
    return jax.shard_map(
        shards,
        mesh=mesh,
        in_specs=(tokens, tokens, P("dp"), P("dp", None), *weights),
        out_specs=(tokens, tokens, *weights),
        check_vma=False,
    )
```

```python
import types

import jax
import jax.numpy as jnp
from jax import lax
from jax.experimental import pallas as pl
from jax.experimental.pallas import tpu as pltpu
from jax.sharding import PartitionSpec as P

HEAD = 64
HEADS = 12
LAYERS = 2
D = 768
FF = 3072
MESH = pl.DeviceIdType.MESH
BF16, F32 = jnp.bfloat16, jnp.float32

AXES = {"q": "yczx", "u": "yczx", "d": "czxy"}
STREAMS = ((slice(0, 16), "xyz"), (slice(16, 32), "yzx"), (slice(32, 48), "zxy"))
KINDS = "qud"
ALL = slice(None)
STEPS = (1, 3, 2)


def place():
    dp, core = lax.axis_index("dp"), lax.axis_index("fsdp")
    return {"z": dp // 16, "x": (dp // 4) % 4, "y": dp % 4, "c": core}


def device(at):
    return ((at["z"] * 4 + at["x"]) * 4 + at["y"], at["c"])


def moved(at, axis, step):
    size = 2 if axis == "c" else 4
    return {**at, axis: (at[axis] + step) % size}


class Batch:
    def __init__(self, links, whole):
        self.links, self.whole = links, whole
        self.number = links.batches
        links.batches += 1
        links.open.append(self)

    def copy(self, src, dst, target):
        return pltpu.make_async_remote_copy(
            src_ref=src,
            dst_ref=dst,
            send_sem=self.links.send_sems.at[self.number],
            recv_sem=self.links.recv_sems.at[self.number],
            device_id=device(target),
            device_id_type=MESH,
        )

    def send(self, src, dst, target):
        self.copy(src, dst, target).start()

    def all(self):
        return self.copy(self.whole, self.whole, self.links.sibling)

    def wait(self):
        self.all().wait_recv()


class Links:
    def __init__(self, me, send_sems, recv_sems):
        self.sibling = moved(me, "c", 1)
        self.send_sems, self.recv_sems, self.open, self.batches = send_sems, recv_sems, [], 0

    def send(self, src, dst, target):
        batch = Batch(self, src)
        batch.send(src, dst, target)
        return batch

    def so_far(self):
        batches, self.open = self.open, []
        return batches

    def drain(self, batches):
        for batch in batches:
            batch.all().wait_send()


def greet(me):
    partners = [moved(moved(me, "y", dy), "c", dc) for dy in range(4) for dc in range(2)][1:]
    partners += [moved(me, axis, step) for axis in "xz" for step in (1, 2, 3)]
    barrier = pltpu.get_barrier_semaphore()
    for partner in partners:
        pl.semaphore_signal(barrier, inc=1, device_id=device(partner), device_id_type=MESH)
    return len(partners)


T = 256
ROWS = 128
GAIN1, OFF1, BIAS_Q, BIAS_OUT, GAIN2, OFF2, BIAS_UP, BIAS_DOWN = 0, 1, 2, 5, 6, 7, 8, 12


def dot(a, b):
    return jnp.dot(a, b, preferred_element_type=F32)


def dot_nt(a, b):
    return lax.dot_general(a, b, (((1,), (1,)), ((), ())), preferred_element_type=F32)


def dot_tn(a, b):
    return lax.dot_general(a, b, (((0,), (0,)), ((), ())), preferred_element_type=F32)


def slab(ref, layer, index):
    return jnp.concatenate([ref[layer, index, core].reshape(D, 384) for core in range(2)], axis=1)


def chunk(ref, layer, index):
    return jnp.concatenate([ref[layer, core, index].reshape(D, 384) for core in range(2)], axis=1)


def put_slab(ref, layer, index, value):
    for core in range(2):
        ref[layer, index, core] = value[:, core * 384 : (core + 1) * 384].reshape(4, 4, 48, 384)


def put_chunk(ref, layer, index, value):
    for core in range(2):
        ref[layer, core, index] = value[:, core * 384 : (core + 1) * 384].reshape(4, 4, 48, 384)


def rows_of(index):
    return pl.ds(pl.multiple_of(index * ROWS, ROWS), ROWS)


def normal(x):
    center = x - jnp.mean(x, axis=-1, keepdims=True)
    scale = lax.rsqrt(jnp.mean(center * center, axis=-1, keepdims=True) + 1e-05)
    return center * scale, scale


def norm_into(x_ref, vec, gain, offset, out_ref):
    @pl.loop(0, T // ROWS)
    def _(index):
        rows = rows_of(index)
        hat, _ = normal(x_ref[rows, :].astype(F32))
        out_ref[rows, :] = (hat * vec[gain : gain + 1, :] + vec[offset : offset + 1, :]).astype(BF16)


def fold(value):
    return jnp.sum(value.reshape(ROWS // 8, 8, value.shape[1]), axis=0)


def total(value):
    return jnp.sum(value, axis=0, keepdims=True)


def norm_back(x_ref, grad_ref, vec, sums, gain, offset, top_ref, out_ref, bias=None, low_ref=None):
    zero = jnp.zeros((8, D), F32)

    def body(index, carry):
        sum_gain, sum_offset, sum_bias = carry
        rows = rows_of(index)
        hat, scale = normal(x_ref[rows, :].astype(F32))
        grad = grad_ref[rows, :]
        scaled = grad * vec[gain : gain + 1, :]
        inner = scaled - jnp.mean(scaled, axis=-1, keepdims=True)
        inner -= hat * jnp.mean(scaled * hat, axis=-1, keepdims=True)
        result = top_ref[rows, :] + scale * inner
        out_ref[rows, :] = result
        low = result.astype(BF16)
        if low_ref is not None:
            low_ref[rows, :] = low
        return sum_gain + fold(grad * hat), sum_offset + fold(grad), sum_bias + fold(low.astype(F32))

    sum_gain, sum_offset, sum_bias = lax.fori_loop(0, T // ROWS, body, (zero, zero, zero))
    sums[gain : gain + 1, :] = total(sum_gain)
    sums[offset : offset + 1, :] = total(sum_offset)
    if bias is not None:
        sums[bias : bias + 1, :] = total(sum_bias)


def gelu_parts(u):
    inner = 0.7978845608028654 * (u + 0.044715 * u * u * u)
    t = jnp.tanh(inner)
    slope = 0.7978845608028654 * (1.0 + 0.134145 * u * u)
    half = 0.5 * (1.0 + t)
    return u * half, half + 0.5 * u * (1.0 - t * t) * slope


def gelu(u):
    return 0.5 * u * (1.0 + jnp.tanh(0.7978845608028654 * (u + 0.044715 * u * u * u)))


def head_mask(which, scale=1.0):
    lane = lax.broadcasted_iota(jnp.int32, (1, 128), 1)
    return jnp.where(lane // HEAD == which, scale, 0.0).astype(BF16)


def lanes_of(pair):
    return pl.ds(pl.multiple_of(pair * 128, 128), 128)


def forward_qkv(layer, m):
    norm_into(m.x[layer], m.vec.at[layer], GAIN1, OFF1, m.h.at[layer])

    @pl.loop(0, 3)
    def _(part):
        bias = m.vec[layer, pl.ds(BIAS_Q + part, 1), :]
        m.qkv[layer, part] = (dot(m.h[layer], slab(m.wq, layer, part)) + bias).astype(BF16)


def forward_attention(layer, m):
    @pl.loop(0, HEADS // 2, unroll=2)
    def _(pair):
        lanes = lanes_of(pair)
        query, keys, values = (m.qkv[layer, part, :, lanes] for part in range(3))
        attended = jnp.zeros((T, 128), F32)
        for which in range(2):
            scores = dot_nt(query * head_mask(which, 0.125), keys)
            grown = jnp.exp(scores - jnp.max(scores, axis=-1, keepdims=True))
            probs = grown * (1.0 / jnp.sum(grown, axis=-1, keepdims=True))
            probs = probs.astype(BF16)
            m.probs[layer, 2 * pair + which] = probs
            attended += dot(probs, values * head_mask(which))
        m.o[layer, :, lanes] = attended.astype(BF16)


def forward_out(layer, m):
    m.mid[layer] = (
        m.x[layer][...].astype(F32)
        + dot(m.o[layer], slab(m.wq, layer, 3))
        + m.vec[layer, BIAS_OUT : BIAS_OUT + 1, :]
    )
    norm_into(m.mid.at[layer], m.vec.at[layer], GAIN2, OFF2, m.h2.at[layer])


def forward_up(layer, m):
    @pl.loop(0, 4)
    def _(index):
        bias = m.vec[layer, pl.ds(BIAS_UP + index, 1), :]
        u = dot(m.h2[layer], slab(m.wu, layer, index)) + bias
        m.u[layer, index] = u.astype(BF16)
        m.a[index] = gelu(u).astype(BF16)


def forward_down(layer, m):
    out = m.x[layer + 1]
    out[...] = m.mid[layer] + m.vec[layer, BIAS_DOWN : BIAS_DOWN + 1, :]

    @pl.loop(0, 4)
    def _(index):
        out[...] += dot(m.a[index], chunk(m.wd, layer, index))


def forward_last(layer, m, out):
    for core in range(2):
        columns = slice(384 * core, 384 * core + 384)
        value = m.mid[layer, :, columns] + m.vec[layer, BIAS_DOWN : BIAS_DOWN + 1, columns]
        for index in range(4):
            value += dot(m.a[index], m.wd[layer, core, index].reshape(D, 384))
        out[:, columns] = value.astype(BF16)


def backward_down(layer, m, index):
    for core, ref in ((m.me["c"], m.top_down), (1 - m.me["c"], m.got_qu)):
        columns = pl.ds(pl.multiple_of(384 * core, 128), 384)
        value = dot_tn(m.a[index], m.gz[:, columns])
        ref[index] = value.astype(BF16).reshape(4, 4, 48, 384)


def backward_ffn(layer, m, index):
    grad_active = dot_nt(m.gz[...], chunk(m.wd, layer, index))
    active, slope = gelu_parts(m.u[layer, index].astype(F32))
    pre = (grad_active * slope).astype(BF16)
    gu = m.gu[layer]
    gu[...] = pre
    m.sums[layer, pl.ds(BIAS_UP + index, 1), :] = total(pre.astype(F32))
    m.gh[...] += dot_nt(gu[...], slab(m.wu, layer, index))
    if layer == 0:
        m.a[0] = active.astype(BF16)
        put_chunk(m.wd, layer, index, dot_tn(m.a[0], m.gz[...]).astype(BF16))
    put_slab(m.wu, layer, index, dot_tn(m.h2[layer], gu[...]).astype(BF16))


def backward_mid(layer, m):
    norm_back(
        m.mid.at[layer], m.gh, m.vec.at[layer], m.sums.at[layer], GAIN2, OFF2, m.g, m.g, BIAS_OUT, m.gz
    )
    m.go[...] = dot_nt(m.gz[...], slab(m.wq, layer, 3)).astype(BF16)
    put_slab(m.wq, layer, 3, dot_tn(m.o[layer], m.gz[...]).astype(BF16))


def backward_attention(layer, m):
    @pl.loop(0, HEADS // 2, unroll=2)
    def _(pair):
        lanes = lanes_of(pair)
        query, keys, values = (m.qkv[layer, part, :, lanes] for part in range(3))
        grad = m.go[:, lanes]
        zero = jnp.zeros((T, 128), F32)
        grad_query, grad_keys, grad_values = zero, zero, zero
        for which in range(2):
            low = m.probs[layer, 2 * pair + which]
            probs = low.astype(F32)
            part = grad * head_mask(which)
            grad_probs = dot_nt(part, values)
            grad_values += dot_tn(low, part)
            row_dot = jnp.sum(grad_probs * probs, axis=-1, keepdims=True)
            grad_scores = (probs * (grad_probs - row_dot)).astype(BF16)
            grad_query += dot(grad_scores, keys * head_mask(which, 0.125))
            grad_keys += dot_tn(grad_scores, query * head_mask(which, 0.125))
        for part, value in enumerate((grad_query, grad_keys, grad_values)):
            m.gqkv[part, :, lanes] = value.astype(BF16)


def backward_qkv(layer, m, part):
    m.sums[layer, pl.ds(BIAS_Q + part, 1), :] = total(m.gqkv[part].astype(F32))
    m.gh[...] += dot_nt(m.gqkv[part], slab(m.wq, layer, part))
    put_slab(m.wq, layer, part, dot_tn(m.h[layer], m.gqkv[part]).astype(BF16))


def backward_in(layer, m, out_ref):
    norm_back(m.x[layer], m.gh, m.vec.at[layer], m.sums.at[layer], GAIN1, OFF1, m.g, out_ref)


def upstream(order_ref, remaining_ref, cot_ref, m):
    live = lax.broadcasted_iota(jnp.int32, (1, T), 1) >= T - remaining_ref

    def body(index, carry):
        rows = rows_of(index)
        spot = index * ROWS + lax.broadcasted_iota(jnp.int32, (ROWS, 1), 0)
        hit = jnp.where((order_ref == spot) & live, 1.0, 0.0)
        mask = jnp.max(hit, axis=-1, keepdims=True)
        grad = cot_ref[rows, :].astype(F32) * mask
        m.g[rows, :] = grad
        return carry

    lax.fori_loop(0, T // ROWS, body, 0)


def top(layer, m):
    def body(index, carry):
        rows = rows_of(index)
        low = m.g[rows, :].astype(BF16)
        m.gz[rows, :] = low
        return carry + fold(low.astype(F32))

    sums = lax.fori_loop(0, T // ROWS, body, jnp.zeros((8, D), F32))
    m.sums[layer, BIAS_DOWN : BIAS_DOWN + 1, :] = total(sums)
    m.gh[...] = jnp.zeros((T, D), F32)


class Gather:
    def __init__(self, kind, layer, m):
        self.kind, self.layer, self.m = kind, layer, m
        sizes = m.wq.at[0]
        self.handed = Batch(m.links, sizes.at[:, 0])
        self.one = Batch(m.links, sizes.at[0, 0, 0, pl.ds(0, 3)])
        self.ring = (kind, layer) != ("q", 0)
        self.two = Batch(m.links, sizes.at[0, 0, pl.ds(0, 2 if self.ring else 3)])
        self.two_halves = Batch(m.links, sizes.at[0, 0, 0]) if self.ring else None
        self.three = Batch(m.links, sizes.at[pl.ds(0, 2), 0])
        self.halves = Batch(m.links, sizes.at[0, 0])

    def part(self, rows, at):
        index = tuple(at[axis] for axis in AXES[self.kind])
        return self.m.weights[self.kind].at[(self.layer, *index, rows, ALL)]

    def hand_over(self, rows, at):
        part = self.part(rows, at)
        self.handed.send(part, part, self.m.links.sibling)

    def out(self, batch, rows, at, axis, steps):
        part = self.part(rows, at)
        for step in steps:
            batch.send(part, part, moved(self.m.me, axis, step))

    def first(self):
        for rows, axes in STREAMS:
            self.out(self.one, rows, self.m.me, axes[0], STEPS)

    def second(self):
        self.one.wait()
        for rows, axes in STREAMS:
            steps = (1, 3) if self.ring else STEPS
            self.out(self.two, rows, {**self.m.me, axes[0]: ALL}, axes[1], steps)

    def relay_two(self):
        self.two.wait()
        for rows, axes in STREAMS:
            for step in (1, 3):
                came = {**moved(self.m.me, axes[1], -step), axes[0]: pl.ds(step - 1, 2)}
                self.out(self.two_halves, rows, came, axes[1], (step,))

    def third(self):
        (self.two_halves if self.ring else self.two).wait()
        planes = [
            (rows, axes, {**self.m.me, axes[0]: ALL, axes[1]: ALL}) for rows, axes in STREAMS
        ]
        for rows, axes, plane in planes:
            self.out(self.three, rows, plane, axes[2], (1, 3))
        for rows, axes, plane in planes:
            self.hand_over(rows, plane)

    def relay(self):
        self.three.wait()
        came = [
            (rows, axes, step, {**moved(self.m.me, axes[2], -step), axes[0]: ALL, axes[1]: ALL})
            for rows, axes in STREAMS
            for step in (1, 3)
        ]
        for rows, axes, step, at in came:
            self.out(self.halves, rows, {**at, axes[0]: pl.ds(step - 1, 2)}, axes[2], (step,))
        for rows, axes, step, at in came:
            self.hand_over(rows, at)

    def finish(self):
        self.halves.wait()
        for rows, axes in STREAMS:
            self.hand_over(rows, {**moved(self.m.me, axes[2], 2), axes[0]: ALL, axes[1]: ALL})

    def arrive(self):
        self.handed.wait()


class Scatter:
    def __init__(self, kind, layer, m):
        self.kind, self.layer, self.m = kind, layer, m
        self.slow = "z" if kind == "d" else "y"
        number = KINDS.index(kind)
        self.streams = []
        for stream, (rows, axes) in enumerate(STREAMS):
            others = [axis for axis in AXES[kind] if axis not in ("c", axes[2])]
            slots = m.first.at[number, stream]
            later = (m.second.at[layer, number, stream], m.third.at[layer, number, stream])
            free = m.free.at[3 * number + stream]
            self.streams.append((rows, axes[::-1], others, slots, *later, free))
        sizes = m.wq.at[0]
        self.shared = [Batch(m.links, sizes.at[pl.ds(0, 2), 0]) for _ in range(2)]
        self.passing, self.direct, self.passed = (Batch(m.links, sizes.at[0, 0]) for _ in range(3))
        self.two = Batch(m.links, sizes.at[0, 0, pl.ds(0, 3)])
        self.one = Batch(m.links, sizes.at[0, 0, 0, pl.ds(0, 3)])
        self.room, self.got = (m.free.at[9], m.got_d) if kind == "d" else (m.free.at[10], m.got_qu)

    def part(self, rows, at):
        if self.kind == "d" and self.layer == 1:
            return self.m.top_down.at[(*(at.get(axis, ALL) for axis in "zxy"), rows, ALL)]
        index = tuple(at.get(axis, ALL) for axis in AXES[self.kind])
        return self.m.weights[self.kind].at[(self.layer, *index, rows, ALL)]

    def share(self, index, half):
        sibling = self.m.links.sibling
        if self.kind == "d" and self.layer == 1:
            src = self.m.got_qu.at[index]
        else:
            src = self.part(ALL, {self.slow: index, "c": sibling["c"]})
        self.shared[half].send(src, self.got.at[index], sibling)

    def wait_room(self):
        pl.semaphore_wait(self.room, 1)

    def give_room(self):
        sibling = device(self.m.links.sibling)
        pl.semaphore_signal(self.room, inc=1, device_id=sibling, device_id_type=MESH)

    def join(self, half):
        other = "x" if self.kind == "d" else "z"
        self.shared[half].wait()

        @pl.loop(8 * half, 8 * half + 8)
        def _(spot):
            own = self.part(ALL, {self.slow: spot // 4, other: spot % 4, "c": self.m.me["c"]})
            own[...] += self.got[spot // 4, spot % 4]

    def leave(self, half):
        ready = []
        for rows, axes, others, slots, _, _, free in self.streams:
            split = others[0] == self.slow
            if self.layer == 0 and half == (0 if split else 1):
                pl.semaphore_wait(free, 2)
            for now in (half,) if split else (0, 1) if half else ():
                ready.append((rows, axes[0], others[0], slots, now))
        for now in ready:
            self.pass_on(*now)
        for now in ready:
            self.go(*now)

    def pass_on(self, rows, axis, split, slots, half):
        me, halves = self.m.me, pl.ds(2 * half, 2)
        src = self.part(rows, {"c": me["c"], split: halves, axis: moved(me, axis, 2)[axis]})
        self.passing.send(src, slots.at[2, halves], moved(me, axis, 1 + 2 * half))

    def go(self, rows, axis, split, slots, half):
        me, halves = self.m.me, pl.ds(2 * half, 2)
        target = moved(me, axis, 3 - 2 * half)
        src = self.part(rows, {"c": me["c"], split: halves, axis: target[axis]})
        self.direct.send(src, slots.at[1 - half, halves], target)

    def relay(self):
        me = self.m.me
        self.passing.wait()
        for rows, axes, others, slots, _, _, _ in self.streams:
            for half in range(2):
                target = moved(me, axes[0], 1 + 2 * half)
                spot = {"c": me["c"], axes[0]: target[axes[0]]}
                for index in (2 * half, 2 * half + 1):
                    own = self.part(rows, {**spot, others[0]: index})
                    own[...] += slots[2, index]
                halves = pl.ds(2 * half, 2)
                src = self.part(rows, {**spot, others[0]: halves})
                self.passed.send(src, slots.at[half, halves], target)

    def add(self, target, slots):
        value = target[...].astype(F32)
        for slot in slots:
            value += slot[...].astype(F32)
        return value

    def second(self):
        m, me = self.m, self.m.me
        self.direct.wait()
        self.passed.wait()
        for rows, axes, others, slots, later, _, free in self.streams:
            here = {"c": me["c"], axes[0]: me[axes[0]]}

            @pl.loop(0, 4)
            def _(index):
                target = self.part(rows, {**here, others[0]: index})
                total = self.add(target, [slots.at[side, index] for side in range(2)])
                target[...] = total.astype(BF16)

            if self.layer == 1:
                for step in (1, 3):
                    peer = device(moved(me, axes[0], step))
                    pl.semaphore_signal(free, inc=1, device_id=peer, device_id_type=MESH)
            for step in STEPS:
                target = moved(me, axes[1], step)
                src = self.part(rows, {**here, axes[1]: target[axes[1]]})
                self.two.send(src, later.at[step - 1], target)

    def third(self):
        m, me = self.m, self.m.me
        self.two.wait()
        for rows, axes, _, _, later, last, _ in self.streams:
            here = {"c": me["c"], axes[0]: me[axes[0]], axes[1]: me[axes[1]]}
            target = self.part(rows, here)
            target[...] = self.add(target, [later.at[step] for step in range(3)]).astype(BF16)
            for step in STEPS:
                target = moved(me, axes[2], step)
                src = self.part(rows, {**here, axes[2]: target[axes[2]]})
                self.one.send(src, last.at[step - 1], target)

    def finish(self):
        self.one.wait()
        for rows, _, _, _, _, last, _ in self.streams:
            total = self.add(self.part(rows, self.m.me), [last.at[step] for step in range(3)])
            self.m.totals[self.kind][self.layer, rows, :] = total


TILE_PAIRS = ((GAIN1, OFF1), (BIAS_OUT, GAIN2), (OFF2, BIAS_DOWN))
NARROW_ROWS = tuple(row for pair in TILE_PAIRS for row in pair)


def spot_matrix(base, width):
    row = lax.broadcasted_iota(jnp.int32, (128, 128), 0)
    lane = lax.broadcasted_iota(jnp.int32, (128, 128), 1)
    return jnp.where((lane == base + row) & (row < width), 1.0, 0.0).astype(BF16)


def spot_matrices(member):
    return (
        spot_matrix(6 * member, 6), spot_matrix(48 + 6 * member, 6),
        spot_matrix(12 * member, 12), spot_matrix(24 * (member % 4), 24),
    )


def flag(condition):
    return jnp.where(condition, 1.0, 0.0).astype(F32)


def vector_tile(member, narrow, wide_qv, wide_up, stage):
    stage[...] = jnp.zeros(stage.shape, F32)
    for layer in range(LAYERS):
        rows = slice(layer, layer + 1)
        for number, vector in enumerate(narrow):
            row = 8 * layer + number // 2
            stage[number % 2, row : row + 1, 0:6] = vector[rows, :].astype(F32)
        row = 8 * layer + 3
        stage[2, row : row + 1, 0:12] = wide_qv[rows, :].astype(F32)
        for half in range(2):
            up = wide_up[rows, :].astype(F32) * flag(member // 4 == half)
            stage[3, row + 1 + half : row + 2 + half, 0:24] = up
    total = jnp.zeros((16, 128), F32)
    for number, matrix in enumerate(spot_matrices(member)):
        total += dot(stage[number].astype(BF16), matrix)
    return total.astype(BF16)


def whole_vectors(tiles, vec):
    tiles = [tiles[index // 4, index % 4].astype(F32) for index in range(16)]

    def joined(row, first, last, groups):
        return jnp.concatenate([tiles[group][row : row + 1, first:last] for group in groups], axis=1)

    for layer in range(LAYERS):
        vec[layer] = jnp.zeros((16, D), F32)
        for number, pair in enumerate(TILE_PAIRS):
            for side, row in enumerate(pair):
                value = joined(8 * layer + number, 48 * side, 48 * side + 48, range(16))
                vec[layer, row : row + 1, :] = value
        for side in range(2):
            value = joined(8 * layer + 3, 0, 96, range(8 * side, 8 * side + 8))
            vec[layer, BIAS_Q + 2 * side : BIAS_Q + 2 * side + 1, :] = value
        for part in range(4):
            pieces = []
            for group in range(4 * part, 4 * part + 4):
                for half in range(2):
                    row = 8 * layer + 4 + half
                    pieces.append(tiles[group][row : row + 1, 0:96])
            value = jnp.concatenate(pieces, axis=1)
            vec[layer, BIAS_UP + part : BIAS_UP + part + 1, :] = value


def vector_tiles(sums, tiles):
    tiles[...] = jnp.zeros(tiles.shape, F32)
    for layer in range(LAYERS):
        for group in range(16):
            spot = tiles.at[group // 4, group % 4]
            for number, pair in enumerate(TILE_PAIRS):
                for side, row in enumerate(pair):
                    value = sums[layer, row : row + 1, 48 * group : 48 * group + 48]
                    at = 8 * layer + number
                    spot[at : at + 1, 48 * side : 48 * side + 48] = value
            row, start = BIAS_Q + 2 * (group // 8), 96 * (group % 8)
            at = 8 * layer + 3
            spot[at : at + 1, 0:96] = sums[layer, row : row + 1, start : start + 96]
            row, start = BIAS_UP + group // 4, 192 * (group % 4)
            for half in range(2):
                first = start + 96 * half
                value = sums[layer, row : row + 1, first : first + 96]
                spot[at + 1 + half : at + 2 + half, 0:96] = value


def own_entries(member, value, out):
    high = value.astype(BF16)
    middle = (value - high.astype(F32)).astype(BF16)
    low = (value - high.astype(F32) - middle.astype(F32)).astype(BF16)
    found = [
        dot_nt(high, matrix) + (dot_nt(middle, matrix) + dot_nt(low, matrix))
        for matrix in spot_matrices(member)
    ]
    for layer in range(LAYERS):
        rows = slice(layer, layer + 1)
        for number in range(6):
            row = 8 * layer + number // 2
            out[number][rows, :] = found[number % 2][row : row + 1, 0:6]
        row = 8 * layer + 3
        out[6][rows, :] = found[2][row : row + 1, 0:12]
        up = found[3][row + 1 : row + 2] * flag(member // 4 == 0)
        up += found[3][row + 2 : row + 3] * flag(member // 4 == 1)
        out[7][rows, :] = up[:, 0:24]


def kernel(*refs):
    inputs, refs = refs[:16], refs[16:]
    outputs, refs = refs[:14], refs[14:]
    staged, refs = refs[:14], refs[14:]
    ready, refs = refs[:12], refs[12:]
    (
        wq, wu, wd, got_qu, got_d, top_down, first, second, third, sum_q, sum_u, sum_d,
        x0, x1, h, qkv, probs, o, mid, h2, u, tmp, g, gh, gz, cots, vec, sums,
        vec_out, vec_in, vec_all, stage, sum_all, sum_in, sum_next, sum_out, sum_got,
        send_a, recv_a, send_d, recv_d, send_f, recv_f, send_df, recv_df,
        send_sems, recv_sems, local_sems, free,
    ) = refs
    hidden, cot = inputs[:2]
    out, grad = outputs[:2]
    order, remaining, w_qkv, w_out, w_up, w_down, *vectors_in = staged
    gain1, off1, bias_qv, bias_out, gain2, off2, bias_up, bias_down = vectors_in
    g_qkv, g_out, g_up, g_down, *vectors_out = ready
    me = place()
    partners = greet(me)
    loads = []
    for number, (src, dst) in enumerate(zip(inputs[2:], staged)):
        loads.append(pltpu.make_async_copy(src, dst, local_sems.at[4 + number]))
        loads[-1].start()
    sibling = moved(me, "c", 1)
    mine = 2 * me["y"] + me["c"]
    links = Links(me, send_sems, recv_sems)
    m = types.SimpleNamespace(
        me=me, links=links, weights={"q": wq, "u": wu, "d": wd}, wq=wq, wu=wu, wd=wd,
        got_qu=got_qu, got_d=got_d, free=free, totals={"q": sum_q, "u": sum_u, "d": sum_d},
        first=first, second=second, third=third,
        x=[x0, x1], h=h, qkv=qkv, probs=probs, o=o, mid=mid, h2=h2, u=u, a=tmp, g=g, gh=gh, gz=gz,
        gu=[tmp.at[1], cots], top_down=top_down, go=tmp.at[3], gqkv=tmp, vec=vec, sums=sums,
    )
    send_f[...] = jnp.zeros(send_f.shape, F32)
    for copy in loads:
        copy.wait()

    def build(layer):
        start, rows = 16 * layer, slice(16 * layer, 16 * layer + 16)
        for owner in range(8):
            columns = slice(384 * (owner % 2), 384 * (owner % 2) + 384)
            for row in range(6):
                if owner < 6:
                    part = w_qkv[row, layer : layer + 1, 384 * owner : 384 * owner + 384]
                else:
                    part = w_out[row, layer : layer + 1, columns]
                send_f[owner, start + row : start + row + 1, :] = part.astype(F32)
                part = w_up[row, layer : layer + 1, 384 * owner : 384 * owner + 384]
                send_f[owner, start + 8 + row : start + 9 + row, :] = part.astype(F32)
        for owner in range(8):
            send_a[owner, rows, :] = send_f[owner, rows, :].astype(BF16)
        recv_a[mine, rows, :] = send_a[mine, rows, :]

    build(0)
    for half in range(2):
        for layer in range(LAYERS):
            part = w_down[layer, :, 384 * half : 384 * half + 384]
            send_df[half, 24 * layer : 24 * layer + 24, :] = part.astype(F32)
        send_d[half] = send_df[half].astype(BF16)
    pl.semaphore_wait(pltpu.get_barrier_semaphore(), partners)

    def group_sends(src, dst, rows=ALL):
        batch = Batch(links, dst.at[pl.ds(0, 7), rows])
        for dy in range(4):
            for dc in range(2):
                if dy or dc:
                    target = moved(moved(me, "y", dy), "c", dc)
                    spot = src.at[2 * target["y"] + target["c"], rows]
                    batch.send(spot, dst.at[mine, rows], target)
        return batch

    def group_tiles(src, dst):
        batch = Batch(links, dst.at[pl.ds(0, 7)])
        for dy in range(4):
            for dc in range(2):
                if dy or dc:
                    batch.send(src, dst.at[mine], moved(moved(me, "y", dy), "c", dc))
        return batch

    arrivals = [group_sends(send_a, recv_a, slice(0, 16))]
    arrivals.append(links.send(send_d.at[1 - me["c"]], recv_d.at[me["c"]], sibling))
    recv_d[me["c"]] = send_d[me["c"]]
    narrow = (gain1, off1, bias_out, gain2, off2, bias_down)
    vec_out[...] = vector_tile(mine, narrow, bias_qv, bias_up, stage)
    vec_in[mine] = vec_out[...]
    tiles = group_tiles(vec_out, vec_in)
    build(1)
    second_layer = group_sends(send_a, recv_a, slice(16, 32))
    here = pl.ds(pl.multiple_of(128 * me["c"], 128), 128)
    there = pl.ds(pl.multiple_of(128 * (1 - me["c"]), 128), 128)
    halves = []
    for number, (src, dst) in enumerate(((hidden, x0), (cot, cots))):
        halves.append(links.send(src.at[1 - me["c"]], dst.at[here, :], sibling))
        copy = pltpu.make_async_copy(src.at[me["c"]], dst.at[here, :], local_sems.at[number])
        copy.start()
        halves.append(copy)
    for batch in arrivals:
        batch.wait()
    gathers = [Gather(kind, layer, m) for layer in range(LAYERS) for kind in KINDS]
    own = (me["y"], me["c"], me["z"], me["x"])

    def prepare(layer):
        for group, target in enumerate((wq, wu)):
            for source in range(8):
                rows = recv_a[source, 16 * layer : 16 * layer + 16, :].astype(F32)
                sum_q[group, 6 * source : 6 * source + 6, :] = rows[8 * group : 8 * group + 6]
            target[(layer, *own)] = sum_q[group].astype(BF16)
            gathers[3 * layer + group].first()
        for half in range(2):
            sum_d[0, 24 * half : 24 * half + 24, :] = recv_d[half].astype(F32)[
                24 * layer : 24 * layer + 24
            ]
        wd[layer, me["c"], me["z"], me["x"], me["y"]] = sum_d[0].astype(BF16)
        gathers[3 * layer + 2].first()

    prepare(0)
    tiles.wait()
    tile = jnp.zeros((16, 128), F32)
    for source in range(8):
        tile += vec_in[source].astype(F32)
    vec_all[me["z"], me["x"]] = tile.astype(BF16)
    spot = vec_all.at[me["z"], me["x"]]
    along_z = Batch(links, vec_all.at[0, pl.ds(0, 3)])
    for step in STEPS:
        along_z.send(spot, spot, moved(me, "z", step))
    q0, u0, d0, q1, u1, d1 = gathers
    q0.second()
    along_z.wait()
    column = vec_all.at[:, me["x"]]
    along_x = Batch(links, vec_all.at[pl.ds(0, 3)])
    for step in STEPS:
        along_x.send(column, column, moved(me, "x", step))
    u0.second()
    q0.third()
    u0.relay_two()
    d0.second()
    second_layer.wait()
    prepare(1)
    u0.third()
    along_x.wait()
    whole_vectors(vec_all, vec)
    d0.relay_two()
    q1.second()
    q0.relay()
    d0.third()
    q1.relay_two()
    u1.second()
    d1.second()
    q0.finish()
    u0.relay()
    q1.third()
    halves[0].wait()
    halves[1].wait()
    q0.arrive()

    forward_qkv(0, m)
    u1.relay_two()
    d1.relay_two()
    u0.finish()
    d0.relay()
    u1.third()
    forward_attention(0, m)
    u0.arrive()
    d0.finish()
    q1.relay()
    d1.third()
    forward_out(0, m)
    forward_up(0, m)
    d0.arrive()
    forward_down(0, m)
    q1.finish()
    u1.relay()
    halves[2].wait()
    halves[3].wait()
    upstream(order[pl.ds(me["c"], 1), :], remaining[me["c"]], cots, m)
    sums[...] = jnp.zeros(sums.shape, F32)
    top(1, m)
    q1.arrive()
    forward_qkv(1, m)
    u1.finish()
    forward_attention(1, m)
    d1.relay()
    forward_out(1, m)
    u1.arrive()
    forward_up(1, m)
    gathered = links.so_far()
    scatters = {(kind, layer): Scatter(kind, layer, m) for layer in (1, 0) for kind in KINDS}

    def steps(*plan):
        for word in plan:
            name, step, *given = word.split(".")
            getattr(scatters[name[0], int(name[1])], step)(*map(int, given))

    @pl.loop(0, 4)
    def _(part):
        backward_down(1, m, part)
        for now in range(4):

            @pl.when(part == now)
            def _():
                scatters["d", 1].share(now, now // 2)

    d1.finish()
    steps("d1.join.0", "d1.leave.0", "d1.join.1", "d1.leave.1")
    links.drain(scatters["d", 1].shared)
    steps("u1.give_room")
    d1.arrive()
    links.drain(gathered)

    def swap(src, dst, number):
        remote = links.send(src.at[there, :], dst.at[me["c"]], sibling)
        copy = pltpu.make_async_copy(src.at[here, :], dst.at[me["c"]], local_sems.at[number])
        copy.start()
        return remote, copy

    def ffn(layer, *plans):
        groups = [scatters[kind, layer] for kind in ("u" if layer else "ud")]
        for group in groups:
            group.wait_room()

        @pl.loop(0, 4)
        def _(part):
            backward_ffn(layer, m, part)
            for now in range(4):

                @pl.when(part == now)
                def _():
                    for group in groups:
                        group.share(now, now // 2)
                    steps(*plans[now])

    def attention_grads(layer):
        scatter = scatters["q", layer]
        scatter.wait_room()
        scatter.share(3, 1)
        m.gh[...] = jnp.zeros((T, D), F32)

        @pl.loop(0, 3)
        def _(part):
            backward_qkv(layer, m, part)

            @pl.when(part < 2)
            def _():
                scatter.share(part, 0)

            @pl.when(part == 2)
            def _():
                scatter.share(2, 1)
                scatter.join(0)
                scatter.leave(0)

    ffn(1, (), (), ("u1.join.0", "u1.leave.0"), ())
    forward_last(1, m, cots)
    results = [swap(cots, out, 2)]
    steps("u1.join.1", "u1.leave.1", "u1.give_room", "d1.give_room", "d1.relay")
    backward_mid(1, m)
    backward_attention(1, m)
    steps("u1.relay")
    attention_grads(1)
    steps("d1.second")
    backward_in(1, m, g)
    top(0, m)
    steps("q1.join.1", "q1.give_room", "q1.leave.1", "u1.second")
    ffn(
        0, (), ("d1.third",), ("q1.relay", "u0.join.0", "u0.leave.0"), ("d0.join.0", "d0.leave.0")
    )
    backward_mid(0, m)
    steps("u0.join.1", "u0.leave.1", "u0.give_room", "d0.join.1", "d0.leave.1", "u1.third")
    backward_attention(0, m)
    steps("q1.second", "u0.relay")
    attention_grads(0)
    steps("d0.relay", "q0.join.1", "q0.leave.1")
    backward_in(0, m, g)
    vector_tiles(sums, sum_all)
    along_z = Batch(links, sum_in)
    for step in STEPS:
        target = moved(me, "z", step)
        along_z.send(sum_all.at[target["z"]], sum_in.at[step - 1], target)
    results.append(swap(g, grad, 3))
    steps("q1.third", "u0.second", "q0.relay", "d0.second")
    along_z.wait()
    for index in range(4):
        row = sum_all[me["z"], index]
        for step in range(3):
            row += sum_in[step, index]
        sum_all[me["z"], index] = row
    along_x = Batch(links, sum_next)
    for step in STEPS:
        target = moved(me, "x", step)
        along_x.send(sum_all.at[me["z"], target["x"]], sum_next.at[step - 1], target)
    steps("u1.finish", "d1.finish", "q1.finish")

    spots = {("q", 1): 0, ("u", 1): 8, ("u", 0): 16, ("q", 0): 24}

    def give_back(rows, *groups):
        for kind, layer in groups:
            start, total = spots[kind, layer], {"q": sum_q, "u": sum_u}[kind]
            for owner in range(8):
                send_f[owner, start : start + 6, :] = total[layer, 6 * owner : 6 * owner + 6, :]
        return group_sends(send_f, recv_f, rows)

    def give_back_down(layer):
        rows = slice(24 * layer, 24 * layer + 24)
        for owner in range(2):
            send_df[owner, rows, :] = sum_d[layer, 24 * owner : 24 * owner + 24, :]
        recv_df[me["c"], rows, :] = send_df[me["c"], rows, :]
        return links.send(send_df.at[1 - me["c"], rows], recv_df.at[me["c"], rows], sibling)

    def take_back(kind, layer):
        start, wide_out = spots[kind, layer], g_up if kind == "u" else g_qkv
        for owner in range(8):
            columns = slice(384 * owner, 384 * owner + 384)
            target = wide_out
            if kind == "q" and owner >= 6:
                columns, target = slice(384 * (owner - 6), 384 * (owner - 5)), g_out
            for row in range(6):
                value = recv_f[owner, start + row : start + row + 1, :]
                target[row, layer : layer + 1, columns] = value

    early = [give_back(slice(0, 16), ("q", 1), ("u", 1)), give_back_down(1)]
    steps("q0.second", "u0.third", "d0.third")
    along_x.wait()
    tile = sum_all[me["z"], me["x"]]
    for step in range(3):
        tile += sum_next[step]
    sum_out[...] = tile
    tiles = group_tiles(sum_out, sum_got)
    sum_got[mine] = tile
    steps("q0.third", "u0.finish", "d0.finish")
    early += [give_back(slice(16, 24), ("u", 0)), give_back_down(0)]
    steps("q0.finish")
    last = give_back(slice(24, 32), ("q", 0))
    recv_f[mine] = send_f[mine]
    tiles.wait()
    tile = sum_got[0]
    for source in range(1, 8):
        tile += sum_got[source]
    own_entries(mine, tile, vectors_out)
    for batch in early:
        batch.wait()
    for kind, layer in (("q", 1), ("u", 1), ("u", 0)):
        take_back(kind, layer)
    for half in range(2):
        for layer in range(LAYERS):
            g_down[layer, :, 384 * half : 384 * half + 384] = recv_df[
                half, 24 * layer : 24 * layer + 24, :
            ]
    last.wait()
    take_back("q", 0)
    stores = []
    for number, (src, dst) in enumerate(zip(ready, outputs[2:])):
        stores.append(pltpu.make_async_copy(src, dst, local_sems.at[4 + number]))
        stores[-1].start()
    for remote, copy in results:
        remote.wait()
        copy.wait()
    links.drain([batch for batch in links.so_far() if batch not in scatters["d", 1].shared])
    assert links.batches <= 96
    for copy in stores:
        copy.wait()


def deliver_kernel(*refs):
    count = len(refs) // 3
    sources, results, held, sems = refs[:count], refs[count : 2 * count], refs[2 * count : -1], refs[-1]
    loads = [
        pltpu.make_async_copy(src, dst, sems.at[0, number])
        for number, (src, dst) in enumerate(zip(sources, held))
    ]
    stores = [
        pltpu.make_async_copy(src, dst, sems.at[1, number])
        for number, (src, dst) in enumerate(zip(held, results))
    ]
    for copy in loads:
        copy.start()
    for load, store in zip(loads, stores):
        load.wait()
        store.start()
    for copy in stores:
        copy.wait()


def deliver(values):
    hbm = pl.BlockSpec(memory_space=pl.ANY)
    return pl.pallas_call(
        deliver_kernel,
        out_shape=[jax.ShapeDtypeStruct(value.shape, value.dtype) for value in values],
        in_specs=[hbm] * len(values),
        out_specs=[hbm] * len(values),
        scratch_shapes=[
            *[pltpu.VMEM(value.shape, value.dtype) for value in values],
            pltpu.SemaphoreType.DMA((2, len(values))),
        ],
        name="deliver",
    )(*values)


def shards(
    hidden, cotangent, remaining, order,
    norm1_gain, norm1_bias, w_qkv, bias_qv, w_out, bias_out,
    norm2_gain, norm2_bias, w_up, bias_up, w_down, bias_down,
):
    half = hidden.shape[1]
    hbm = pl.BlockSpec(memory_space=pl.ANY)
    swapped = [jnp.transpose(weight, (1, 0, 2)) for weight in (w_qkv, w_out, w_up)]
    wide, deep = (LAYERS, 4, 2, 4, 4, 48, 384), (LAYERS, 2, 4, 4, 4, 48, 384)
    inputs = (
        hidden, cotangent, order, remaining, *swapped, w_down,
        norm1_gain, norm1_bias, bias_qv, bias_out, norm2_gain, norm2_bias, bias_up, bias_down,
    )
    results = [((2, half, D), BF16)] + [
        (shape, F32)
        for shape in (
            (2, half, D), (6, LAYERS, 3 * D), (6, LAYERS, D), (6, LAYERS, FF), (LAYERS, 24, D),
            *[(LAYERS, 6)] * 6, (LAYERS, 12), (LAYERS, 24),
        )
    ]
    staged = [pltpu.VMEM(value.shape, value.dtype) for value in inputs[2:]]
    staged[1] = pltpu.SMEM(remaining.shape, remaining.dtype)
    values = pl.pallas_call(
        kernel,
        out_shape=[jax.ShapeDtypeStruct(*result) for result in results],
        in_specs=[hbm] * len(inputs),
        out_specs=[hbm] * len(results),
        scratch_shapes=[
            *staged,
            *[pltpu.VMEM(*result) for result in results[2:]],
            pltpu.VMEM(wide, BF16),
            pltpu.VMEM(wide, BF16),
            pltpu.VMEM(deep, BF16),
            pltpu.VMEM((4, 4, 4, 48, 384), BF16),
            pltpu.VMEM((4, 4, 4, 48, 384), BF16),
            pltpu.VMEM((4, 4, 4, 48, 384), BF16),
            pltpu.VMEM((3, 3, 3, 4, 4, 16, 384), BF16),
            pltpu.VMEM((LAYERS, 3, 3, 3, 4, 16, 384), BF16),
            pltpu.VMEM((LAYERS, 3, 3, 3, 16, 384), BF16),
            *[pltpu.VMEM((LAYERS, 48, 384), F32) for _ in range(3)],
            pltpu.VMEM((T, D), BF16),
            pltpu.VMEM((T, D), F32),
            pltpu.VMEM((LAYERS, T, D), BF16),
            pltpu.VMEM((LAYERS, 3, T, D), BF16),
            pltpu.VMEM((LAYERS, HEADS, T, T), BF16),
            pltpu.VMEM((LAYERS, T, D), BF16),
            pltpu.VMEM((LAYERS, T, D), F32),
            pltpu.VMEM((LAYERS, T, D), BF16),
            pltpu.VMEM((LAYERS, 4, T, D), BF16),
            pltpu.VMEM((4, T, D), BF16),
            pltpu.VMEM((T, D), F32),
            pltpu.VMEM((T, D), F32),
            pltpu.VMEM((T, D), BF16),
            pltpu.VMEM((T, D), BF16),
            pltpu.VMEM((LAYERS, 16, D), F32),
            pltpu.VMEM((LAYERS, 16, D), F32),
            pltpu.VMEM((16, 128), BF16),
            pltpu.VMEM((8, 16, 128), BF16),
            pltpu.VMEM((4, 4, 16, 128), BF16),
            pltpu.VMEM((4, 16, 128), F32),
            pltpu.VMEM((4, 4, 16, 128), F32),
            pltpu.VMEM((3, 4, 16, 128), F32),
            pltpu.VMEM((3, 16, 128), F32),
            pltpu.VMEM((16, 128), F32),
            pltpu.VMEM((8, 16, 128), F32),
            pltpu.VMEM((8, 32, 384), BF16),
            pltpu.VMEM((8, 32, 384), BF16),
            pltpu.VMEM((2, 48, 384), BF16),
            pltpu.VMEM((2, 48, 384), BF16),
            pltpu.VMEM((8, 32, 384), F32),
            pltpu.VMEM((8, 32, 384), F32),
            pltpu.VMEM((2, 48, 384), F32),
            pltpu.VMEM((2, 48, 384), F32),
            pltpu.SemaphoreType.DMA((96,)),
            pltpu.SemaphoreType.DMA((96,)),
            pltpu.SemaphoreType.DMA((18,)),
            pltpu.SemaphoreType.REGULAR((11,)),
        ],
        compiler_params=pltpu.CompilerParams(
            collective_id=0, has_side_effects=True, vmem_limit_bytes=(63 << 20) + (1 << 19)
        ),
        name="layers",
    )(*inputs)
    values = deliver(values)
    out, grad, g_qkv, g_out, g_up, g_down, gain1, off1, b_out, gain2, off2, b_down, b_qv, b_up = values
    g_qkv, g_out, g_up = (jnp.transpose(part, (1, 0, 2)) for part in (g_qkv, g_out, g_up))
    return out, grad, gain1, off1, g_qkv, b_qv, g_out, b_out, gain2, off2, g_up, b_up, g_down, b_down


def solution(mesh):
    tokens, rows = P("dp", "fsdp", None), P(None, ("dp", "fsdp"), None)
    vector = P(None, ("dp", "fsdp"))
    weights = (
        vector, vector, rows, vector, rows, vector, vector, vector, rows, vector, rows, vector
    )
    return jax.shard_map(
        shards,
        mesh=mesh,
        in_specs=(tokens, tokens, P("dp"), P("dp", None), *weights),
        out_specs=(tokens, tokens, *weights),
        check_vma=False,
    )
```
